32 devices in a mesh: gx: 8 (over z, y), gy: 4 (over x, core).
Axes of the slice: x: 2, y: 2, z: 4, core: 2. Of those that a mesh axis runs over, the one named last changes fastest.
Arguments:
- right_side: float32 [2, 32, 32, 384], P(None, 'gx', 'gy'), may hold values from -6 to 6
- velocity_table: float32 [16], replicated, may hold values from 2500 to 5000
- layer_index: int32 [32, 32, 384], P('gx', 'gy'), may hold values from 0 to 15
- absorb_level: int32 [32, 32, 384], P('gx', 'gy'), may hold values from 0 to 3
Outputs:
- solution_field: float32 [2, 32, 32, 384], P(None, 'gx', 'gy')
The draws below stay inside these ranges and needn't reach their ends.
All inputs are finite; a program needn't handle non-finite values.
Results may differ from the reference program's by a relative error of at most 0.0001.
Values sent between devices are 32-bit elements; how exact they have to be, the bound alone decides.
A program may use at most 64 MiB of HBM per device.

```python
import math
import jax
import jax.numpy as jnp

LAYERS = 16
NU = 2
NC = 8
CYCLES = 2
NX = 32
NY = 32
NZ = 384


def place_ends(drawn, key, low, largest):
    shape = drawn.shape
    spot = [jax.random.randint(jax.random.fold_in(key, axis), (), 0, shape[axis]) for axis in range(len(shape))]
    drawn = drawn.at[tuple(spot)].set(low)
    longest = shape.index(max(shape))
    spot[longest] = (spot[longest] + 1) % shape[longest]
    return drawn.at[tuple(spot)].set(largest)


def block_levels(rng, extent, pieces, smallest, high):
    gain, own = 1.0, jax.random.fold_in(rng, 6)
    for axis_at, shards_of in pieces:
        heights = jnp.exp(jax.random.uniform(jax.random.fold_in(own, axis_at), (shards_of,), jnp.float32, smallest / len(pieces), high / len(pieces)))
        gain = gain * jnp.repeat(heights, extent[axis_at] // shards_of).reshape([-1 if axis == axis_at else 1 for axis in range(len(extent))])
    return gain


def scatter_about(own_key, shape, width, reach, shards=(), held_as=jnp.bfloat16):
    loudness = block_levels(own_key, shape, shards, -0.22, 0.18) if shards else 1.0
    entries = jax.random.normal(own_key, shape, jnp.float32) * width * loudness
    return jnp.minimum(jnp.maximum(entries, -reach), reach).astype(held_as)


def setup_inputs(seed: int = 0) -> dict:
    arg_keys = jax.random.split(jax.random.key(seed), 5)
    right_side = scatter_about(arg_keys[0], (2, NX, NY, NZ), 1.0, 6.0, ((1, 8), (2, 4)), jnp.float32)
    velocity_table = jnp.clip(jnp.exp(jax.random.uniform(arg_keys[1], (LAYERS,), jnp.float32, math.log(2500.0), math.log(5000.0))), 2500.0, 5000.0)
    layer_index = place_ends(jax.random.randint(arg_keys[2], (NX, NY, NZ), 0, LAYERS), jax.random.fold_in(arg_keys[2], 1), 0, LAYERS - 1).astype(jnp.int32)
    absorb_level = place_ends(jax.random.randint(arg_keys[3], (NX, NY, NZ), 0, 4), jax.random.fold_in(arg_keys[3], 1), 0, 3).astype(jnp.int32)
    return dict(right_side=right_side, velocity_table=velocity_table, layer_index=layer_index, absorb_level=absorb_level)


OMEGA = 0.6
BETA = 0.5
ABSORB = 0.25
KH_FACTOR = 2.0 * math.pi * 6.0 * 20.0


def complex_product(first, second):
    return jnp.stack([first[0] * second[0] - first[1] * second[1], first[0] * second[1] + first[1] * second[0]])


def neighbour_sum(padded):
    total = padded[:, 2:, 1:-1, 1:-1] + padded[:, :-2, 1:-1, 1:-1]
    total = total + padded[:, 1:-1, 2:, 1:-1] + padded[:, 1:-1, :-2, 1:-1]
    total = total + padded[:, 1:-1, 1:-1, 2:] + padded[:, 1:-1, 1:-1, :-2]
    return total


def apply_operator(field, shift_term, grid_level):
    padded = jnp.pad(field, ((0, 0), (1, 1), (1, 1), (1, 1)))
    return (6.0 * field - neighbour_sum(padded)) * (0.25 ** grid_level) - complex_product(shift_term, field)


def restrict(field):
    size_x, size_y, size_z = field.shape[1], field.shape[2], field.shape[3]
    return field.reshape(2, size_x // 2, 2, size_y // 2, 2, size_z // 2, 2).mean(axis=(2, 4, 6))


def prolong(field):
    return jnp.repeat(jnp.repeat(jnp.repeat(field, 2, 1), 2, 2), 2, 3)


def inverse_of(shift_term, grid_level):
    diag_real = 6.0 * (0.25 ** grid_level) - shift_term[0]
    diag_imag = -shift_term[1]
    denom = diag_real * diag_real + diag_imag * diag_imag
    return jnp.stack([diag_real / denom, -diag_imag / denom])


def smooth(update, source, shift_term, inverse_diag, grid_level, sweeps):
    for sweep in range(sweeps):
        update = update + OMEGA * complex_product(inverse_diag, source - apply_operator(update, shift_term, grid_level))
    return update


def vcycle(source, shifts, inverses, grid_level):
    if grid_level == 2:
        return smooth(jnp.zeros_like(source), source, shifts[2], inverses[2], 2, NC)
    update = smooth(jnp.zeros_like(source), source, shifts[grid_level], inverses[grid_level], grid_level, NU)
    residual = source - apply_operator(update, shifts[grid_level], grid_level)
    correction = vcycle(restrict(residual), shifts, inverses, grid_level + 1)
    update = update + prolong(correction)
    return smooth(update, source, shifts[grid_level], inverses[grid_level], grid_level, NU)


def reference(right_side, velocity_table, layer_index, absorb_level):
    velocity = velocity_table[layer_index]
    kh_square = (KH_FACTOR / velocity) ** 2
    damping = BETA + ABSORB * absorb_level.astype(jnp.float32)
    shift_zero = jnp.stack([kh_square, -kh_square * damping])
    shift_one = restrict(shift_zero)
    shift_two = restrict(shift_one)
    shifts = (shift_zero, shift_one, shift_two)
    inverses = (inverse_of(shift_zero, 0), inverse_of(shift_one, 1), inverse_of(shift_two, 2))
    first = vcycle(right_side, shifts, inverses, 0)
    residual = right_side - apply_operator(first, shift_zero, 0)
    for cycle_number in range(CYCLES - 1):
        first = first + vcycle(residual, shifts, inverses, 0)
        if cycle_number + 2 < CYCLES:
            residual = right_side - apply_operator(first, shift_zero, 0)
    return first
```

```python
import functools
import math

import jax
import jax.numpy as jnp
from jax import lax
from jax.experimental import pallas as pl
from jax.experimental.pallas import tpu as pltpu
from jax.sharding import PartitionSpec as P

NC = 8
OMEGA = 0.6
BETA = 0.5
ABSORB = 0.25
KH_FACTOR = 2.0 * math.pi * 6.0 * 20.0
MESH = pl.DeviceIdType.MESH
HIGHEST = lax.Precision.HIGHEST

STEPS = [(1, 0), (-1, 0), (0, 1), (0, -1), (1, 1), (1, -1), (-1, 1), (-1, -1)]
EXCHANGES = [
    (4, 2, 2),
    (2, 2, 1),
    (2, 2, 1), (4, 2, 1), (2, 2, 1), (2, 1, 1),
    (4, 3, 1),
    (2, 2, 1), (4, 2, 1), (2, 2, 1), (2, 1, 1),
]


def product(a, b):
    return a[0] * b[0] - a[1] * b[1], a[0] * b[1] + a[1] * b[0]


def dot(a, b):
    return jnp.dot(a, b, precision=HIGHEST, preferred_element_type=jnp.float32)


def iota(shape, dim):
    return lax.broadcasted_iota(jnp.int32, shape, dim)


def kernel(ngx, ngy, depth, *refs):
    rhs, table, layer, absorb, out = refs[:5]
    buffers = refs[5 : 5 + 5 * len(EXCHANGES)]
    (shift0, diag0, w0, wf0, upd0, upd0b, first, w1, diag1, wf1, g1, upd1, upd1b, padded, tiles0, tiles1,
     send_sem, recv_sem, tile_send, tile_recv) = refs[5 + 5 * len(EXCHANGES) :]
    gathered = (tiles0, tiles1)
    count = ngx * ngy
    gx, gy = lax.axis_index("gx"), lax.axis_index("gy")
    me = gx * ngy + gy
    f32 = jnp.float32

    barrier = pltpu.get_barrier_semaphore()

    def greet(k, carry):
        other = lax.rem(me + k, count)
        pl.semaphore_signal(barrier, inc=1, device_id=(other // ngy, lax.rem(other, ngy)), device_id_type=MESH)
        return carry

    lax.fori_loop(1, count, greet, 0)

    def exists(dx, dy):
        checks = []
        if dx > 0:
            checks.append(gx < ngx - 1)
        if dx < 0:
            checks.append(gx > 0)
        if dy > 0:
            checks.append(gy < ngy - 1)
        if dy < 0:
            checks.append(gy > 0)
        return functools.reduce(jnp.logical_and, checks)

    def views(k):
        return buffers[5 * k : 5 * k + 5]

    for k, (size, wide, fields) in enumerate(EXCHANGES):
        ext, _, _, low, high = views(k)

        def clear(ref, start, n):
            ref[pl.ds(start, n)] = jnp.zeros((n,) + ref.shape[1:], f32)

        @pl.when(gx == 0)
        def _():
            for ref in (ext, low, high):
                clear(ref, 0, wide)

        @pl.when(gx == ngx - 1)
        def _():
            for ref in (ext, low, high):
                clear(ref, wide + size, wide)

        @pl.when(gy == 0)
        def _():
            clear(low, 0, size + 2 * wide)

        @pl.when(gy == ngy - 1)
        def _():
            clear(high, 0, size + 2 * wide)

    def copy_of(k, d):
        size, wide, fields = EXCHANGES[k]
        ext, up, down, low, high = views(k)
        dx, dy = STEPS[d]
        if dy == 0:
            src = ext.at[pl.ds(size if dx > 0 else wide, wide)]
            dst = ext.at[pl.ds(0 if dx > 0 else wide + size, wide)]
        else:
            source, target = (up, low) if dy > 0 else (down, high)
            if dx == 0:
                src, dst = source, target.at[pl.ds(wide, size)]
            elif dx > 0:
                src, dst = source.at[pl.ds(size - wide, wide)], target.at[pl.ds(0, wide)]
            else:
                src, dst = source.at[pl.ds(0, wide)], target.at[pl.ds(wide + size, wide)]
        return pltpu.make_async_remote_copy(
            src_ref=src, dst_ref=dst, send_sem=send_sem.at[k, d], recv_sem=recv_sem.at[k, d],
            device_id=(gx + dx, gy + dy), device_id_type=MESH,
        )

    row8 = iota((8, depth), 0)

    def put(k, plane, field, pair):
        size, wide, fields = EXCHANGES[k]
        ext, up, down, low, high = views(k)
        re, im = pair
        ext[wide + plane, 2 * field] = re
        ext[wide + plane, 2 * field + 1] = im
        up[plane, field] = jnp.where(row8 < 4, pltpu.roll(re, 4, 0), im)
        down[plane, field] = jnp.where(row8 < 4, re, pltpu.roll(im, 4, 0))

    def start(k):
        for d in range(8):
            @pl.when(exists(*STEPS[d]))
            def _(d=d):
                copy_of(k, d).start()

    def receive(k):
        for d in range(8):
            dx, dy = STEPS[d]

            @pl.when(exists(-dx, -dy))
            def _(d=d):
                copy_of(k, d).wait_recv()

    def get(k, plane, field):
        size, wide, fields = EXCHANGES[k]
        ext, up, down, low, high = views(k)
        above, below = high[plane, field], low[plane, field]
        re = jnp.where(row8 < 4, above, pltpu.roll(below, 4, 0))
        im = jnp.where(row8 < 4, pltpu.roll(above, 4, 0), below)
        return (
            jnp.concatenate([ext[plane, 2 * field], re], axis=0),
            jnp.concatenate([ext[plane, 2 * field + 1], im], axis=0),
        )

    lane16 = iota((16, depth), 1)

    def around(before, mid, after, s):
        total = before + after + pltpu.roll(mid, s, 0) + pltpu.roll(mid, 16 - s, 0)
        total = total + jnp.where(lane16 >= s, pltpu.roll(mid, s, 1), 0.0)
        return total + jnp.where(lane16 < depth - s, pltpu.roll(mid, depth - s, 1), 0.0)

    def load(ref, plane, rows=16):
        return ref[plane, 0, :rows], ref[plane, 1, :rows]

    def store(ref, plane, pair):
        ref[plane, 0], ref[plane, 1] = pair

    def neighbours(ref, plane, s):
        return tuple(around(ref[plane - 1, c], ref[plane, c], ref[plane + 1, c], s) for c in range(2))

    def weight(diag, inside):
        denom = diag[0] * diag[0] + diag[1] * diag[1]
        scale = jnp.where(inside, OMEGA / denom, 0.0)
        return diag[0] * scale, -diag[1] * scale

    def first_two(wf_ref, w_ref, target, planes, s, c):
        for p in planes:
            wf, ns, w = load(wf_ref, p), neighbours(wf_ref, p, s), load(w_ref, p)
            part = product(w, ns)
            store(target, p, tuple(1.4 * a + c * b for a, b in zip(wf, part)))

    def sweep(ref, wf_ref, w_ref, planes, shift, s, c):
        for p in planes:
            e, ns = load(ref, p), neighbours(ref, p, s)
            part = product(load(w_ref, p + shift), ns)
            wf = load(wf_ref, p + shift)
            yield p, tuple(0.4 * a + b + c * d for a, b, d in zip(e, wf, part))

    def residual(source, ref, diag, p, s, c):
        ns, part = neighbours(ref, p, s), product(diag, load(ref, p))
        return tuple(f + c * n - q for f, n, q in zip(source, ns, part))

    lane8 = iota((8, depth), 1)

    def pair_mean(value):
        value = value + jnp.where(row8 % 2 == 0, pltpu.roll(value, 7, 0), pltpu.roll(value, 1, 0))
        other = jnp.where(lane8 % 2 == 0, pltpu.roll(value, depth - 1, 1), pltpu.roll(value, 1, 1))
        return (value + other) * 0.125

    shifts1 = []
    shifts = []
    for p in range(4):
        index = layer[p]
        velocity = jnp.zeros((8, depth), f32)
        for number in range(table.shape[0]):
            velocity = jnp.where(index == number, table[number], velocity)
        ratio = KH_FACTOR / velocity
        kh2 = ratio * ratio
        shift = (kh2, -kh2 * (BETA + ABSORB * absorb[p].astype(f32)))
        shifts.append(shift)
        put(0, p, 0, (rhs[0, p], rhs[1, p]))
        put(0, p, 1, shift)
        if p % 2 == 1:
            mean = tuple(pair_mean(shifts[p - 1][c] + shift[c]) for c in range(2))
            shifts1.append(mean)
            put(1, p // 2, 0, mean)
    pl.semaphore_wait(barrier, count - 1)
    start(0)
    start(1)

    spread = 0.25 * (iota((depth, 128), 0) // 4 == iota((depth, 128), 1)).astype(f32)
    widen = (iota((128, depth), 1) // 4 == iota((128, depth), 0)).astype(f32)
    rows2 = 2 * ngy
    slot = iota((96, 3 * 2 * rows2), 0)
    entry = iota((96, 3 * 2 * rows2), 1)
    inner = slot % 16
    offset = jnp.where(inner < 12, inner // 4, -1)
    expand = ((entry // rows2 == slot // 16) & (entry % rows2 == 2 * gy + offset)).astype(f32)

    shift2_sum = tuple(shifts1[0][c] + shifts1[1][c] for c in range(2))
    zero_plane = jnp.zeros((rows2, 128), f32)
    for c in range(2):
        padded[0, c] = zero_plane
        padded[ngx + 1, c] = zero_plane
    row2 = iota((ngx, rows2, 128), 1)
    block8 = iota((8, 128), 0) // 2

    def unpack(buffer, comp):
        planes = []
        for x in range(ngx):
            groups = []
            for q in range(0, ngy, 4):
                value = buffer[x * ngy + q]
                for j in range(1, min(4, ngy - q)):
                    value = jnp.where(block8 == (comp + j) % 4, buffer[x * ngy + q + j], value)
                groups.append(pltpu.roll(value, 8 - 2 * comp, 0) if comp else value)
            planes.append(jnp.concatenate(groups, axis=0)[:rows2] if len(groups) > 1 else groups[0][:rows2])
        return jnp.stack(planes)

    coarse = {}

    def coarsest(cycle, sums):
        buffer = gathered[cycle]
        stacked = jnp.concatenate(list(sums) + (list(shift2_sum) if cycle == 0 else []), axis=0)
        rows = stacked.shape[0]
        at, to = iota((8, rows), 1), iota((8, rows), 0)
        left = 0.125 * ((at // 4) == (to + 8 - 2 * lax.rem(gy, 4)) % 8).astype(f32)
        buffer[me] = dot(dot(left, stacked), spread)

        def send(k, carry):
            other = lax.rem(me + k, count)
            pltpu.make_async_remote_copy(
                src_ref=buffer.at[me], dst_ref=buffer.at[me],
                send_sem=tile_send.at[cycle], recv_sem=tile_recv.at[cycle],
                device_id=(other // ngy, lax.rem(other, ngy)), device_id_type=MESH,
            ).start()
            return carry

        lax.fori_loop(1, count, send, 0)

    def coarsest_finish(cycle):
        buffer = gathered[cycle]
        every = buffer.at[pl.ds(0, count - 1)]
        pltpu.make_async_copy(every, every, tile_recv.at[cycle]).wait()
        source = unpack(buffer, 0), unpack(buffer, 1)
        if cycle == 0:
            shift = unpack(buffer, 2), unpack(buffer, 3)
            coarse["w"] = weight((0.375 - shift[0], -shift[1]), shift[0] > 0.0)
        w = coarse["w"]
        wf = product(w, source)
        none = jnp.zeros((1, rows2, 128), f32)

        def total(e):
            result = jnp.concatenate([none, e[:-1]], axis=0) + jnp.concatenate([e[1:], none], axis=0)
            result = result + jnp.where(row2 > 0, pltpu.roll(e, 1, 1), 0.0)
            result = result + jnp.where(row2 < rows2 - 1, pltpu.roll(e, rows2 - 1, 1), 0.0)
            return result + pltpu.roll(e, 1, 2) + pltpu.roll(e, 127, 2)

        def step(_, e):
            part = product(w, (total(e[0]), total(e[1])))
            return tuple(0.4 * a + b + 0.0625 * d for a, b, d in zip(e, wf, part))

        e = lax.fori_loop(0, NC - 1, step, wf)
        for c in range(2):
            for x in range(ngx):
                padded[x + 1, c] = e[c][x]
        own = jnp.concatenate([padded[gx + i, c] for i in range(3) for c in range(2)], axis=0)
        wide = dot(dot(expand, own), widen)
        return [tuple(wide[32 * i + 16 * c : 32 * i + 16 * c + 16] for c in range(2)) for i in range(3)]

    def cycle_part(cycle, base):
        source1, update0, update1, solution1 = base, base + 1, base + 2, base + 3
        first_two(wf0, w0, upd0, range(1, 7), 1, 1.0)
        held = []
        for p in range(4):
            r = residual(load(first, p + 2), upd0, load(diag0, p + 2), p + 2, 1, 1.0)
            held.append(tuple(v[:8] for v in r))
            if p % 2 == 1:
                put(source1, p // 2, 0, tuple(pair_mean(held[p - 1][c] + held[p][c]) for c in range(2)))
        start(source1)
        for p in range(4):
            put(update0, p, 0, load(upd0, p + 2, 8))
        start(update0)
        if cycle == 0:
            receive(1)
            for p in range(6):
                shift = get(1, p, 0)
                diag = (1.5 - shift[0], -shift[1])
                store(diag1, p, diag)
                store(w1, p, weight(diag, shift[0] > 0.0))
        receive(source1)
        for p in range(6):
            source = get(source1, p, 0)
            store(g1, p, source)
            store(wf1, p, product(load(w1, p), source))
        first_two(wf1, w1, upd1, range(1, 5), 2, 0.25)
        left, right = [
            residual(load(g1, p), upd1, load(diag1, p), p, 2, 0.25) for p in (2, 3)
        ]
        coarsest(cycle, tuple(left[c][:8] + right[c][:8] for c in range(2)))
        for p in range(2):
            put(update1, p, 0, load(upd1, p + 2, 8))
        start(update1)
        receive(update1)
        receive(update0)
        correction = coarsest_finish(cycle)
        for p in range(6):
            e = get(update1, p, 0)
            store(upd1, p, tuple(a + b for a, b in zip(e, correction[p // 2])))
        for p, e in sweep(upd1, wf1, w1, range(1, 5), 0, 2, 0.25):
            store(upd1b, p, e)
        for p, e in sweep(upd1b, wf1, w1, range(2, 4), 0, 2, 0.25):
            put(solution1, p - 2, 0, tuple(v[:8] for v in e))
        start(solution1)
        receive(solution1)
        for p in range(4):
            extra = get(solution1, p, 0)
            for fine in (2 * p, 2 * p + 1):
                e = get(update0, fine, 0)
                store(upd0, fine, tuple(a + b for a, b in zip(e, extra)))
        for p, e in sweep(upd0, wf0, w0, range(1, 7), 0, 1, 1.0):
            store(upd0b, p, e)
        return sweep(upd0b, wf0, w0, range(2, 6), 0, 1, 1.0)

    receive(0)
    for p in range(8):
        source, shift = get(0, p, 0), get(0, p, 1)
        diag = (6.0 - shift[0], -shift[1])
        store(first, p, source)
        store(diag0, p, diag)
        w = weight(diag, shift[0] > 0.0)
        store(w0, p, w)
        store(wf0, p, product(w, source))
    kept = []
    for p, e in cycle_part(0, 2):
        put(6, p - 2, 0, tuple(v[:8] for v in e))
    start(6)
    receive(6)
    for p in range(10):
        store(shift0, p, get(6, p, 0))
    for p in range(8):
        r = residual(load(first, p), shift0, load(diag0, p), p + 1, 1, 1.0) if False else None
        ns = neighbours(shift0, p + 1, 1)
        part = product(load(diag0, p), load(shift0, p + 1))
        r = tuple(f + n - q for f, n, q in zip(load(first, p), ns, part))
        store(first, p, r)
        store(wf0, p, product(load(w0, p), r))
    ext6 = views(6)[0]
    for p, e in cycle_part(1, 7):
        for c in range(2):
            out[c, p - 2] = ext6[3 + p - 2, c] + e[c][:8]

    for k in range(len(EXCHANGES)):
        for d in range(8):
            @pl.when(exists(*STEPS[d]))
            def _(k=k, d=d):
                copy_of(k, d).wait_send()
    for cycle in range(2):
        every = gathered[cycle].at[pl.ds(0, count - 1)]
        pltpu.make_async_copy(every, every, tile_send.at[cycle]).wait()


def local(ngx, ngy, right_side, velocity_table, layer_index, absorb_level):
    depth = right_side.shape[-1]
    scratch = []
    for size, wide, fields in EXCHANGES:
        scratch += [
            pltpu.VMEM((size + 2 * wide, 2 * fields, 8, depth), jnp.float32),
            pltpu.VMEM((size, fields, 8, depth), jnp.float32),
            pltpu.VMEM((size, fields, 8, depth), jnp.float32),
            pltpu.VMEM((size + 2 * wide, fields, 8, depth), jnp.float32),
            pltpu.VMEM((size + 2 * wide, fields, 8, depth), jnp.float32),
        ]
    scratch += [pltpu.VMEM((n, 2, 16, depth), jnp.float32) for n in (10, 8, 8, 8, 8, 8, 8, 6, 6, 6, 6, 6, 6)]
    scratch += [pltpu.VMEM((ngx + 2, 2, 2 * ngy, 128), jnp.float32)]
    scratch += [pltpu.VMEM((ngx * ngy, 8, 128), jnp.float32)] * 2
    scratch += [pltpu.SemaphoreType.DMA((len(EXCHANGES), 8))] * 2
    scratch += [pltpu.SemaphoreType.DMA((2,))] * 2
    vmem = pl.BlockSpec(memory_space=pltpu.VMEM)
    return pl.pallas_call(
        functools.partial(kernel, ngx, ngy, depth),
        out_shape=jax.ShapeDtypeStruct(right_side.shape, jnp.float32),
        in_specs=[vmem, pl.BlockSpec(memory_space=pltpu.SMEM), vmem, vmem],
        out_specs=vmem,
        scratch_shapes=scratch,
        compiler_params=pltpu.CompilerParams(
            collective_id=0, has_side_effects=True, vmem_limit_bytes=32 * 1024 * 1024
        ),
    )(right_side, velocity_table, layer_index, absorb_level)


def solution(mesh):
    placed = (P(None, "gx", "gy", None), P(), P("gx", "gy", None), P("gx", "gy", None))
    return jax.shard_map(
        functools.partial(local, mesh.shape["gx"], mesh.shape["gy"]),
        mesh=mesh, in_specs=placed, out_specs=P(None, "gx", "gy", None), check_vma=False,
    )
```

```python
import functools
import math

import jax
import jax.numpy as jnp
from jax import lax
from jax.experimental import pallas as pl
from jax.experimental.pallas import tpu as pltpu
from jax.sharding import PartitionSpec as P

NC = 8
OMEGA = 0.6
BETA = 0.5
ABSORB = 0.25
KH_FACTOR = 2.0 * math.pi * 6.0 * 20.0
MESH = pl.DeviceIdType.MESH
HIGHEST = lax.Precision.HIGHEST

CORNERS = [(1, 1), (1, -1), (-1, 1), (-1, -1)]


def product(a, b):
    return a[0] * b[0] - a[1] * b[1], a[0] * b[1] + a[1] * b[0]


def dot(a, b):
    return jnp.dot(a, b, precision=HIGHEST, preferred_element_type=jnp.float32)


def iota(shape, dim):
    return lax.broadcasted_iota(jnp.int32, shape, dim)


def scratch_of(ngx, ngy, layers, depth):
    f32 = jnp.float32

    def vmem(*shape):
        return pltpu.VMEM(shape, f32)

    def dense():
        return dict(own=vmem(8, depth), got=vmem(4, 8, depth), cs=vmem(4, 2, 1, depth), cr=vmem(4, 2, 1, depth))

    cycles = [
        dict(
            source=dense(), fine=dense(), solution=dense(),
            far=vmem(2, 2, 8, depth), farown=vmem(2, 2, 8, depth),
            up=vmem(2, 8, depth), down=vmem(2, 8, depth), low=vmem(2, 8, depth), high=vmem(2, 8, depth),
            cs=vmem(4, 2, 1, depth), cr=vmem(4, 2, 1, depth), tiles=vmem(ngx * ngy, 8, 128),
        )
        for _ in range(2)
    ]
    return dict(
        rhs=vmem(2, 4, 8, depth), layer=pltpu.VMEM((4, 8, depth), jnp.int32),
        absorb=pltpu.VMEM((4, 8, depth), jnp.int32), table=pltpu.SMEM((layers,), f32),
        ewf=vmem(8, 2, 8, depth), ew=vmem(8, 2, 8, depth),
        up=vmem(4, 8, depth), down=vmem(4, 8, depth), low=vmem(4, 8, depth), high=vmem(4, 8, depth),
        cs=vmem(4, 4, 1, depth), cr=vmem(4, 4, 1, depth),
        coef1=dict(own=vmem(8, depth), got=vmem(4, 8, depth)),
        first=vmem(10, 2, 8, depth),
        fup=vmem(4, 8, depth), fdown=vmem(4, 8, depth), flow=vmem(4, 8, depth), fhigh=vmem(4, 8, depth),
        fcs=vmem(4, 6, 1, depth), fcr=vmem(4, 6, 1, depth),
        cycles=cycles,
        diag0=vmem(4, 2, 8, depth), source0=vmem(4, 2, 8, depth),
        wf0=vmem(8, 2, 16, depth), w0=vmem(8, 2, 16, depth), upd0=vmem(8, 2, 16, depth), upd0b=vmem(8, 2, 16, depth),
        first16=vmem(10, 2, 16, depth),
        diag1=vmem(2, 2, 8, depth), source1=vmem(2, 2, 8, depth),
        wf1=vmem(6, 2, 16, depth), w1=vmem(6, 2, 16, depth), upd1=vmem(6, 2, 16, depth), upd1b=vmem(6, 2, 16, depth),
        padded=vmem(ngx + 2, 2, 2 * ngy, 128),
        send_sem=pltpu.SemaphoreType.DMA((88,)), recv_sem=pltpu.SemaphoreType.DMA((88,)),
        tile_send=pltpu.SemaphoreType.DMA((2,)), tile_recv=pltpu.SemaphoreType.DMA((2,)),
        load_sem=pltpu.SemaphoreType.DMA((4,)),
    )


def kernel(ngx, ngy, depth, tree, rhs_in, table_in, layer_in, absorb_in, out, *scratch):
    m = jax.tree.unflatten(tree, scratch)
    count = ngx * ngy
    gx, gy = lax.axis_index("gx"), lax.axis_index("gy")
    me = gx * ngy + gy
    f32 = jnp.float32

    loads = [
        pltpu.make_async_copy(a, m[b], m["load_sem"].at[i])
        for i, (a, b) in enumerate(((layer_in, "layer"), (absorb_in, "absorb"), (table_in, "table"), (rhs_in, "rhs")))
    ]
    for load_copy in loads:
        load_copy.start()

    barrier = pltpu.get_barrier_semaphore()

    def greet(k, carry):
        other = lax.rem(me + k, count)
        pl.semaphore_signal(barrier, inc=1, device_id=(other // ngy, lax.rem(other, ngy)), device_id_type=MESH)
        return carry

    lax.fori_loop(1, count, greet, 0)

    def exists(dx, dy):
        checks = []
        if dx:
            checks.append(gx < ngx - 1 if dx > 0 else gx > 0)
        if dy:
            checks.append(gy < ngy - 1 if dy > 0 else gy > 0)
        return functools.reduce(jnp.logical_and, checks)

    plan = []

    def add(name, step, src, dst):
        plan.append((name, step, src, dst, len(plan)))

    def cut(ref, first, size=1):
        return ref.at[pl.ds(first, size)]

    def add_packets(name, up, down, low, high):
        add(name, (0, 1), up, low)
        add(name, (0, -1), down, high)

    def add_corners(name, cs, cr):
        for i, step in enumerate(CORNERS):
            add(name, step, cs.at[i], cr.at[i])

    def add_dense(name, b):
        for i, step in enumerate([(1, 0), (-1, 0), (0, 1), (0, -1)]):
            add(name, step, b["own"], b["got"].at[i])
        if "cs" in b:
            add_corners(name, b["cs"], b["cr"])

    add("begin", (1, 0), cut(m["ewf"], 4, 2), cut(m["ewf"], 0, 2))
    add("begin", (-1, 0), cut(m["ewf"], 2, 2), cut(m["ewf"], 6, 2))
    add("begin", (1, 0), cut(m["ew"], 5), cut(m["ew"], 1))
    add("begin", (-1, 0), cut(m["ew"], 2), cut(m["ew"], 6))
    add_packets("begin", m["up"], m["down"], m["low"], m["high"])
    add_corners("begin", m["cs"], m["cr"])
    add_dense("coef1", m["coef1"])
    add("later", (1, 0), cut(m["ew"], 4), cut(m["ew"], 0))
    add("later", (-1, 0), cut(m["ew"], 3), cut(m["ew"], 7))
    for cycle in range(2):
        b = m["cycles"][cycle]
        add_dense(f"source{cycle}", b["source"])
        add(f"update{cycle}", (1, 0), cut(b["farown"], 0), cut(b["far"], 0))
        add(f"update{cycle}", (-1, 0), cut(b["farown"], 1), cut(b["far"], 1))
        add_packets(f"update{cycle}", b["up"], b["down"], b["low"], b["high"])
        add_corners(f"update{cycle}", b["cs"], b["cr"])
        add_dense(f"fine{cycle}", b["fine"])
        add_dense(f"solution{cycle}", b["solution"])
    add("first", (1, 0), cut(m["first"], 4, 3), cut(m["first"], 0, 3))
    add("first", (-1, 0), cut(m["first"], 3, 3), cut(m["first"], 7, 3))
    add_packets("first", m["fup"], m["fdown"], m["flow"], m["fhigh"])
    add_corners("first", m["fcs"], m["fcr"])
    steps = sorted({entry[1] for entry in plan})

    for step in steps:
        @pl.when(jnp.logical_not(exists(-step[0], -step[1])))
        def _(step=step):
            for _, other, _, dst, _ in plan:
                if other == step:
                    dst[...] = jnp.zeros(dst.shape, f32)

    def remote(entry):
        _, (dx, dy), src, dst, i = entry
        return pltpu.make_async_remote_copy(
            src_ref=src, dst_ref=dst, send_sem=m["send_sem"].at[i], recv_sem=m["recv_sem"].at[i],
            device_id=(gx + dx, gy + dy), device_id_type=MESH,
        )

    def each(names, sign, act):
        for step in steps:
            mine = [entry for entry in plan if entry[0] in names and entry[1] == step]
            if mine:
                @pl.when(exists(sign * step[0], sign * step[1]))
                def _(mine=mine):
                    for entry in mine:
                        act(remote(entry))

    def start(*names):
        each(names, 1, lambda copy: copy.start())

    def receive(*names):
        each(names, -1, lambda copy: copy.wait_recv())

    row8, lane8, lane16 = iota((8, depth), 0), iota((8, depth), 1), iota((16, depth), 1)
    even_row, even_lane = row8 % 2 == 0, lane8 % 2 == 0

    def roll(value, shift, dim):
        size = value.shape[dim]
        return pltpu.roll(value, shift % size, dim) if shift % size else value

    def pack2(values, top):
        result = None
        for c, v in enumerate(values):
            v = roll(v, 2 * c + 2 if top else 2 * c, 0)
            result = v if c == 0 else jnp.where(row8 >= 2 * c, v, result)
        return result

    def unpack2(low, high, c):
        return jnp.where(row8 < 4, roll(high, -2 * c, 0), roll(low, 6 - 2 * c, 0))

    def pack4(pair, top):
        re, im = pair
        return jnp.where(row8 < 4, roll(re, 4, 0), im) if top else jnp.where(row8 < 4, re, roll(im, 4, 0))

    def unpack4(low, high):
        return jnp.where(row8 < 4, high, roll(low, 4, 0)), jnp.where(row8 < 4, roll(high, 4, 0), low)

    def put_corners(cs, j, near_low, near_high, from_edge):
        for i, (dx, dy) in enumerate(CORNERS):
            pair = near_high if dx > 0 else near_low
            at = 7 - from_edge if dy > 0 else from_edge
            for c, v in enumerate(pair):
                cs[i, j + c] = v[at : at + 1]

    def got_corner(cr, side, j):
        i = CORNERS.index((-side, 1))
        return cr[i, j], cr[i + 1, j]

    def corner_tile(cr, side, j, thick=1):
        below, above = got_corner(cr, side, j)
        return jnp.where(row8 >= 8 - thick, below, jnp.where(row8 < thick, above, 0.0))

    def pack_dense(first, second):
        return jnp.where(
            even_lane, jnp.where(even_row, first[0], first[1]), jnp.where(even_row, second[0], second[1])
        )

    def unpack_dense(tile):
        re = jnp.where(even_row, tile, roll(tile, 1, 0))
        im = jnp.where(even_row, roll(tile, -1, 0), tile)
        first = tuple(jnp.where(even_lane, v, roll(v, 1, 1)) for v in (re, im))
        second = tuple(jnp.where(even_lane, roll(v, -1, 1), v) for v in (re, im))
        return first, second

    def send_dense(b, planes):
        b["own"][...] = pack_dense(*planes)
        if "cs" in b:
            put_corners(b["cs"], 0, planes[0], planes[1], 0)

    def get_dense(b, own):
        before, after, below, above = [unpack_dense(b["got"][i]) for i in range(4)]
        none = jnp.zeros((8, depth), f32)
        result = []
        for p, plane in enumerate([*before, *own, *after]):
            pair = []
            for c in range(2):
                if p in (2, 3):
                    halo = jnp.where(row8 < 4, above[p - 2][c], below[p - 2][c])
                elif p in (1, 4) and "cr" in b:
                    halo = corner_tile(b["cr"], -1 if p == 1 else 1, c, 2)
                else:
                    halo = none
                pair.append(jnp.concatenate([plane[c], halo], axis=0))
            result.append(tuple(pair))
        return result

    def around(before, mid, after, s):
        total = before + after + roll(mid, s, 0) + roll(mid, -s, 0)
        total = total + jnp.where(lane16 >= s, roll(mid, s, 1), 0.0)
        return total + jnp.where(lane16 < depth - s, roll(mid, -s, 1), 0.0)

    def load(ref, plane, rows=None):
        return tuple(ref[plane, c] if rows is None else ref[plane, c, :rows] for c in range(2))

    def store(ref, plane, pair):
        ref[plane, 0], ref[plane, 1] = pair

    def neighbours(ref, plane, s):
        return tuple(around(ref[plane - 1, c], ref[plane, c], ref[plane + 1, c], s) for c in range(2))

    def weight(diag):
        scale = OMEGA / (diag[0] * diag[0] + diag[1] * diag[1])
        return diag[0] * scale, -diag[1] * scale

    def first_two(wf_ref, w_ref, target, planes, s, c):
        for p in planes:
            part = product(load(w_ref, p), neighbours(wf_ref, p, s))
            store(target, p, tuple(1.4 * a + c * b for a, b in zip(load(wf_ref, p), part)))

    def sweep(ref, wf_ref, w_ref, planes, s, c):
        for p in planes:
            part = product(load(w_ref, p), neighbours(ref, p, s))
            yield p, tuple(0.4 * a + b + c * d for a, b, d in zip(load(ref, p), load(wf_ref, p), part))

    def residual(source, diag, ref, p, s, c):
        ns, part = neighbours(ref, p, s), product(diag, load(ref, p, 8))
        return tuple(f + c * n[:8] - q for f, n, q in zip(source, ns, part))

    def pair_mean(value):
        value = value + jnp.where(even_row, roll(value, -1, 0), roll(value, 1, 0))
        other = jnp.where(even_lane, roll(value, -1, 1), roll(value, 1, 1))
        return (value + other) * 0.125

    def own8(pair):
        return tuple(v[:8] for v in pair)

    for load_copy in loads:
        load_copy.wait()
    shifts, weights, scaled = [], [], []
    for p in range(4):
        index = m["layer"][p]
        velocity = jnp.zeros((8, depth), f32)
        for number in range(m["table"].shape[0]):
            velocity = jnp.where(index == number, m["table"][number], velocity)
        ratio = KH_FACTOR / velocity
        kh2 = ratio * ratio
        shift = (kh2, -kh2 * (BETA + ABSORB * m["absorb"][p].astype(f32)))
        diag = (6.0 - shift[0], -shift[1])
        source = (m["rhs"][0, p], m["rhs"][1, p])
        w = weight(diag)
        wf = product(w, source)
        store(m["diag0"], p, diag)
        store(m["source0"], p, source)
        store(m["ewf"], p + 2, wf)
        store(m["ew"], p + 2, w)
        m["up"][p] = pack2([*wf, *w], True)
        m["down"][p] = pack2([*wf, *w], False)
        shifts.append(shift)
        weights.append(w)
        scaled.append(wf)
    put_corners(m["cs"], 0, scaled[0], scaled[3], 0)
    put_corners(m["cs"], 2, weights[0], weights[3], 0)
    pl.semaphore_wait(barrier, count - 1)
    start("begin")
    shifts1 = [tuple(pair_mean(shifts[p][c] + shifts[p + 1][c]) for c in range(2)) for p in (0, 2)]
    diags1 = [(1.5 - s[0], -s[1]) for s in shifts1]
    weights1 = [weight(d) for d in diags1]
    send_dense(m["coef1"], weights1)
    start("coef1", "later")
    for p in range(2):
        store(m["diag1"], p, diags1[p])

    spread = 0.25 * (iota((depth, 128), 0) // 4 == iota((depth, 128), 1)).astype(f32)
    widen = (iota((128, depth), 1) // 4 == iota((128, depth), 0)).astype(f32)
    rows2 = 2 * ngy
    slot, entry = iota((96, 6 * rows2), 0), iota((96, 6 * rows2), 1)
    inner = slot % 16
    offset = jnp.where(inner < 12, inner // 4, -1)
    expand = ((entry // rows2 == slot // 16) & (entry % rows2 == 2 * gy + offset)).astype(f32)

    shift2_sum = tuple(shifts1[0][c] + shifts1[1][c] for c in range(2))
    zero_plane = jnp.zeros((rows2, 128), f32)
    for c in range(2):
        m["padded"][0, c] = zero_plane
        m["padded"][ngx + 1, c] = zero_plane
    row2 = iota((ngx, rows2, 128), 1)
    block8 = iota((8, 128), 0) // 2

    def unpack(buffer, comp):
        planes = []
        for x in range(ngx):
            groups = []
            for q in range(0, ngy, 4):
                value = buffer[x * ngy + q]
                for j in range(1, min(4, ngy - q)):
                    value = jnp.where(block8 == (comp + j) % 4, buffer[x * ngy + q + j], value)
                groups.append(roll(value, -2 * comp, 0))
            planes.append(jnp.concatenate(groups, axis=0)[:rows2] if len(groups) > 1 else groups[0][:rows2])
        return jnp.stack(planes)

    coarse = {}

    def coarsest(cycle, sums):
        buffer = m["cycles"][cycle]["tiles"]
        stacked = jnp.concatenate(list(sums) + (list(shift2_sum) if cycle == 0 else []), axis=0)
        rows = stacked.shape[0]
        at, to = iota((8, rows), 1), iota((8, rows), 0)
        left = 0.125 * ((at // 4) == (to + 8 - 2 * lax.rem(gy, 4)) % 8).astype(f32)
        buffer[me] = dot(dot(left, stacked), spread)

        def send(k, carry):
            other = lax.rem(me + k, count)
            pltpu.make_async_remote_copy(
                src_ref=buffer.at[me], dst_ref=buffer.at[me],
                send_sem=m["tile_send"].at[cycle], recv_sem=m["tile_recv"].at[cycle],
                device_id=(other // ngy, lax.rem(other, ngy)), device_id_type=MESH,
            ).start()
            return carry

        lax.fori_loop(1, count, send, 0)

    def coarsest_finish(cycle):
        buffer = m["cycles"][cycle]["tiles"]
        every = buffer.at[pl.ds(0, count - 1)]
        pltpu.make_async_copy(every, every, m["tile_recv"].at[cycle]).wait()
        source = unpack(buffer, 0), unpack(buffer, 1)
        if cycle == 0:
            shift = unpack(buffer, 2), unpack(buffer, 3)
            full = weight((0.375 - shift[0], -shift[1]))
            coarse["w"] = tuple(jnp.where(shift[0] > 0.0, v, 0.0) for v in full)
        w = coarse["w"]
        wf = product(w, source)
        none = jnp.zeros((1, rows2, 128), f32)

        def total(e):
            result = jnp.concatenate([none, e[:-1]], axis=0) + jnp.concatenate([e[1:], none], axis=0)
            result = result + jnp.where(row2 > 0, roll(e, 1, 1), 0.0)
            result = result + jnp.where(row2 < rows2 - 1, roll(e, -1, 1), 0.0)
            return result + roll(e, 1, 2) + roll(e, -1, 2)

        def step(_, e):
            part = product(w, (total(e[0]), total(e[1])))
            return tuple(0.4 * a + b + 0.0625 * d for a, b, d in zip(e, wf, part))

        e = lax.fori_loop(0, NC - 1, step, wf)
        for c in range(2):
            for x in range(ngx):
                m["padded"][x + 1, c] = e[c][x]
        own = jnp.concatenate([m["padded"][gx + i, c] for i in range(3) for c in range(2)], axis=0)
        wide = dot(dot(expand, own), widen)
        return [tuple(wide[32 * i + 16 * c : 32 * i + 16 * c + 16] for c in range(2)) for i in range(3)]

    def cycle_part(cycle):
        b = m["cycles"][cycle]
        wf0, w0, upd0, upd0b = m["wf0"], m["w0"], m["upd0"], m["upd0b"]
        wf1, w1, upd1, upd1b = m["wf1"], m["w1"], m["upd1"], m["upd1b"]
        first_two(wf0, w0, upd0, range(1, 7), 1, 1.0)
        held = [residual(load(m["source0"], p), load(m["diag0"], p), upd0, p + 2, 1, 1.0) for p in range(4)]
        sources = [tuple(pair_mean(held[p][c] + held[p + 1][c]) for c in range(2)) for p in (0, 2)]
        scaled1 = [product(weights1[p], sources[p]) for p in range(2)]
        send_dense(b["source"], scaled1)
        start(f"source{cycle}")
        updates = [load(upd0, p + 2, 8) for p in range(4)]
        store(b["farown"], 0, updates[2])
        store(b["farown"], 1, updates[1])
        for i in range(2):
            b["up"][i] = pack2([*updates[2 * i], *updates[2 * i + 1]], True)
            b["down"][i] = pack2([*updates[2 * i], *updates[2 * i + 1]], False)
        put_corners(b["cs"], 0, updates[0], updates[3], 0)
        start(f"update{cycle}")
        if cycle == 0:
            receive("coef1")
            for p, pair in enumerate(get_dense(m["coef1"], weights1)):
                store(w1, p, pair)
        receive(f"source{cycle}")
        for p, pair in enumerate(get_dense(b["source"], scaled1)):
            store(wf1, p, pair)
        first_two(wf1, w1, upd1, range(1, 5), 2, 0.25)
        left, right = [residual(sources[p], load(m["diag1"], p), upd1, p + 2, 2, 0.25) for p in range(2)]
        coarsest(cycle, tuple(left[c] + right[c] for c in range(2)))
        updates1 = [load(upd1, p + 2, 8) for p in range(2)]
        send_dense(b["fine"], updates1)
        start(f"fine{cycle}")
        receive(f"update{cycle}", f"fine{cycle}")
        around1 = get_dense(b["fine"], updates1)
        none = jnp.zeros((8, depth), f32)
        for c in range(2):
            upd0[0, c] = jnp.concatenate([b["far"][0, c], none], axis=0)
            upd0[7, c] = jnp.concatenate([b["far"][1, c], none], axis=0)
            upd0[1, c, 8:] = corner_tile(b["cr"], -1, c)
            upd0[6, c, 8:] = corner_tile(b["cr"], 1, c)
            for p in range(4):
                upd0[p + 2, c, 8:] = unpack2(b["low"][p // 2], b["high"][p // 2], 2 * (p % 2) + c)
        correction = coarsest_finish(cycle)
        for p, e in enumerate(around1):
            store(upd1, p, tuple(v + x for v, x in zip(e, correction[p // 2])))
        for p, e in sweep(upd1, wf1, w1, range(1, 5), 2, 0.25):
            store(upd1b, p, e)
        solved = [own8(e) for _, e in sweep(upd1b, wf1, w1, range(2, 4), 2, 0.25)]
        send_dense(b["solution"], solved)
        start(f"solution{cycle}")
        receive(f"solution{cycle}")
        around1 = get_dense(b["solution"], solved)
        for p in range(8):
            store(upd0, p, tuple(v + x for v, x in zip(load(upd0, p), around1[p // 2 + 1])))
        for p, e in sweep(upd0, wf0, w0, range(1, 7), 1, 1.0):
            store(upd0b, p, e)
        for p, e in sweep(upd0b, wf0, w0, range(2, 6), 1, 1.0):
            yield p - 2, own8(e)

    none = jnp.zeros((8, depth), f32)

    def halo0(p, j):
        if p in (1, 6):
            return corner_tile(m["cr"], -1 if p == 1 else 1, j)
        if p in (0, 7):
            return none
        return unpack2(m["low"][p - 2], m["high"][p - 2], j)

    receive("begin")
    for p in range(8):
        for c in range(2):
            m["wf0"][p, c] = jnp.concatenate([m["ewf"][p, c], halo0(p, c)], axis=0)
            if p in (0, 7):
                m["w0"][p, c, 8:] = none
            else:
                m["w0"][p, c] = jnp.concatenate([m["ew"][p, c], halo0(p, 2 + c)], axis=0)
    kept = []
    for p, e in cycle_part(0):
        store(m["first"], p + 3, e)
        m["fup"][p] = pack4(e, True)
        m["fdown"][p] = pack4(e, False)
        kept.append(e)
    put_corners(m["fcs"], 0, kept[0], kept[3], 0)
    put_corners(m["fcs"], 2, kept[0], kept[3], 1)
    put_corners(m["fcs"], 4, kept[1], kept[2], 0)
    start("first")
    receive("first", "later")
    for p in (0, 7):
        for c in range(2):
            m["w0"][p, c, :8] = m["ew"][p, c]
    for p in range(10):
        if 3 <= p < 7:
            halo = unpack4(m["flow"][p - 3], m["fhigh"][p - 3])
        elif p in (2, 7):
            side, halo = (-1 if p == 2 else 1), []
            for c in range(2):
                below, above = got_corner(m["fcr"], side, c)
                below2, above2 = got_corner(m["fcr"], side, 2 + c)
                tile = jnp.where(row8 == 7, below, jnp.where(row8 == 6, below2, 0.0))
                halo.append(jnp.where(row8 == 0, above, jnp.where(row8 == 1, above2, tile)))
        elif p in (1, 8):
            halo = [corner_tile(m["fcr"], -1 if p == 1 else 1, 4 + c) for c in range(2)]
        else:
            halo = [none, none]
        for c in range(2):
            m["first16"][p, c] = jnp.concatenate([m["first"][p, c], halo[c]], axis=0)
    for p in range(8):
        ns = neighbours(m["first16"], p + 1, 1)
        e = load(m["first16"], p + 1)
        if 2 <= p < 6:
            part = product(load(m["diag0"], p - 2), own8(e))
            source = load(m["source0"], p - 2)
            store(m["source0"], p - 2, tuple(f + n[:8] - q for f, n, q in zip(source, ns, part)))
        part = product(load(m["w0"], p), ns)
        store(m["wf0"], p, tuple(a + b - OMEGA * v for a, b, v in zip(load(m["wf0"], p), part, e)))
    for p, e in cycle_part(1):
        for c in range(2):
            out[c, p] = m["first"][p + 3, c] + e[c]

    for step in steps:
        @pl.when(exists(*step))
        def _(step=step):
            for entry in plan:
                if entry[1] == step:
                    remote(entry).wait_send()
    for cycle in range(2):
        every = m["cycles"][cycle]["tiles"].at[pl.ds(0, count - 1)]
        pltpu.make_async_copy(every, every, m["tile_send"].at[cycle]).wait()


def local(ngx, ngy, right_side, velocity_table, layer_index, absorb_level):
    depth = right_side.shape[-1]
    scratch = scratch_of(ngx, ngy, velocity_table.shape[0], depth)
    leaves, tree = jax.tree.flatten(scratch)
    anywhere = pl.BlockSpec(memory_space=pl.ANY)
    return pl.pallas_call(
        functools.partial(kernel, ngx, ngy, depth, tree),
        out_shape=jax.ShapeDtypeStruct(right_side.shape, jnp.float32),
        in_specs=[anywhere] * 4,
        out_specs=pl.BlockSpec(memory_space=pltpu.VMEM),
        scratch_shapes=leaves,
        compiler_params=pltpu.CompilerParams(
            collective_id=0, has_side_effects=True, vmem_limit_bytes=48 * 1024 * 1024
        ),
    )(right_side, velocity_table, layer_index, absorb_level)


def solution(mesh):
    placed = (P(None, "gx", "gy", None), P(), P("gx", "gy", None), P("gx", "gy", None))
    return jax.shard_map(
        functools.partial(local, mesh.shape["gx"], mesh.shape["gy"]),
        mesh=mesh, in_specs=placed, out_specs=P(None, "gx", "gy", None), check_vma=False,
    )
```

```python
import functools
import math

import jax
import jax.numpy as jnp
from jax import lax
from jax.experimental import pallas as pl
from jax.experimental.pallas import tpu as pltpu
from jax.sharding import PartitionSpec as P

NC = 8
OMEGA = 0.6
BETA = 0.5
ABSORB = 0.25
KH_FACTOR = 2.0 * math.pi * 6.0 * 20.0
MESH = pl.DeviceIdType.MESH

CORNERS = [(1, 1), (1, -1), (-1, 1), (-1, -1)]


def product(a, b):
    return a[0] * b[0] - a[1] * b[1], a[0] * b[1] + a[1] * b[0]


def dot3(a, b):
    rows = a.shape[0]
    pieces, rest = [], a
    for _ in range(3):
        piece = rest.astype(jnp.bfloat16).astype(jnp.float32)
        pieces.append(piece)
        rest = rest - piece
    stacked = jnp.concatenate(pieces, axis=0).astype(jnp.bfloat16)
    result = jnp.dot(stacked, b, preferred_element_type=jnp.float32)
    return result[:rows] + result[rows : 2 * rows] + result[2 * rows :]


def iota(shape, dim):
    return lax.broadcasted_iota(jnp.int32, shape, dim)


def scratch_of(ngx, ngy, layers, depth):
    f32 = jnp.float32

    def vmem(*shape):
        return pltpu.VMEM(shape, f32)

    def dense():
        return dict(own=vmem(8, depth), got=vmem(4, 8, depth), cs=vmem(4, 2, 1, depth), cr=vmem(4, 2, 1, depth))

    cycles = [
        dict(
            source=dense(), fine=dense(), solution=dense(),
            far=vmem(2, 2, 8, depth), farown=vmem(2, 2, 8, depth),
            up=vmem(2, 8, depth), down=vmem(2, 8, depth), low=vmem(2, 8, depth), high=vmem(2, 8, depth),
            cs=vmem(4, 2, 1, depth), cr=vmem(4, 2, 1, depth), tiles=vmem(ngx * ngy, 8, 128),
        )
        for _ in range(2)
    ]
    return dict(
        rhs=vmem(2, 4, 8, depth), layer=pltpu.VMEM((4, 8, depth), jnp.int32),
        absorb=pltpu.VMEM((4, 8, depth), jnp.int32), table=pltpu.SMEM((layers,), f32),
        ewf=vmem(8, 2, 8, depth), ew=vmem(8, 2, 8, depth),
        up=vmem(4, 8, depth), down=vmem(4, 8, depth), low=vmem(4, 8, depth), high=vmem(4, 8, depth),
        cs=vmem(4, 4, 1, depth), cr=vmem(4, 4, 1, depth),
        coef1=dict(own=vmem(8, depth), got=vmem(4, 8, depth)),
        first=vmem(10, 2, 8, depth),
        fup=vmem(4, 8, depth), fdown=vmem(4, 8, depth), flow=vmem(4, 8, depth), fhigh=vmem(4, 8, depth),
        fcs=vmem(4, 6, 1, depth), fcr=vmem(4, 6, 1, depth),
        cycles=cycles,
        diag0=vmem(4, 2, 8, depth), source0=vmem(4, 2, 8, depth),
        wf0=vmem(8, 2, 16, depth), w0=vmem(8, 2, 16, depth), upd0=vmem(8, 2, 16, depth), upd0b=vmem(8, 2, 16, depth),
        first16=vmem(10, 2, 16, depth),
        diag1=vmem(2, 2, 8, depth), source1=vmem(2, 2, 8, depth),
        wf1=vmem(6, 2, 16, depth), w1=vmem(6, 2, 16, depth), upd1=vmem(6, 2, 16, depth), upd1b=vmem(6, 2, 16, depth),
        padded=vmem(ngx + 2, 2, 2 * ngy + 16, 128),
        send_sem=pltpu.SemaphoreType.DMA((88,)), recv_sem=pltpu.SemaphoreType.DMA((88,)),
        tile_send=pltpu.SemaphoreType.DMA((2,)), tile_recv=pltpu.SemaphoreType.DMA((2,)),
        load_sem=pltpu.SemaphoreType.DMA((4,)),
    )


def kernel(ngx, ngy, depth, tree, rhs_in, table_in, layer_in, absorb_in, out, *scratch):
    m = jax.tree.unflatten(tree, scratch)
    count = ngx * ngy
    gx, gy = lax.axis_index("gx"), lax.axis_index("gy")
    me = gx * ngy + gy
    f32 = jnp.float32

    loads = [
        pltpu.make_async_copy(a, m[b], m["load_sem"].at[i])
        for i, (a, b) in enumerate(((layer_in, "layer"), (absorb_in, "absorb"), (table_in, "table"), (rhs_in, "rhs")))
    ]
    for load_copy in loads:
        load_copy.start()

    barrier = pltpu.get_barrier_semaphore()

    def others(act):
        if count > 64:
            def one(k, carry):
                other = lax.rem(me + k, count)
                act(other // ngy, lax.rem(other, ngy))
                return carry

            lax.fori_loop(1, count, one, 0)
            return
        for i in reversed(range(ngx)):
            for j in reversed(range(ngy)):
                if i or j:
                    x, y = gx + i, gy + j
                    act(jnp.where(x >= ngx, x - ngx, x), jnp.where(y >= ngy, y - ngy, y))

    others(lambda x, y: pl.semaphore_signal(barrier, inc=1, device_id=(x, y), device_id_type=MESH))

    def exists(dx, dy):
        checks = []
        if dx:
            checks.append(gx < ngx - 1 if dx > 0 else gx > 0)
        if dy:
            checks.append(gy < ngy - 1 if dy > 0 else gy > 0)
        return functools.reduce(jnp.logical_and, checks)

    plan = []

    def add(name, step, src, dst):
        plan.append((name, step, src, dst, len(plan)))

    def cut(ref, first, size=1):
        return ref.at[pl.ds(first, size)]

    def add_packets(name, up, down, low, high):
        add(name, (0, 1), up, low)
        add(name, (0, -1), down, high)

    def add_corners(name, cs, cr):
        for i, step in enumerate(CORNERS):
            add(name, step, cs.at[i], cr.at[i])

    def add_dense(name, b):
        for i, step in enumerate([(1, 0), (-1, 0), (0, 1), (0, -1)]):
            add(name, step, b["own"], b["got"].at[i])
        if "cs" in b:
            add_corners(name, b["cs"], b["cr"])

    add("begin", (1, 0), cut(m["ewf"], 4, 2), cut(m["ewf"], 0, 2))
    add("begin", (-1, 0), cut(m["ewf"], 2, 2), cut(m["ewf"], 6, 2))
    add("begin", (1, 0), cut(m["ew"], 5), cut(m["ew"], 1))
    add("begin", (-1, 0), cut(m["ew"], 2), cut(m["ew"], 6))
    add_packets("begin", m["up"], m["down"], m["low"], m["high"])
    add_corners("begin", m["cs"], m["cr"])
    add_dense("coef1", m["coef1"])
    add("later", (1, 0), cut(m["ew"], 4), cut(m["ew"], 0))
    add("later", (-1, 0), cut(m["ew"], 3), cut(m["ew"], 7))
    for cycle in range(2):
        b = m["cycles"][cycle]
        add_dense(f"source{cycle}", b["source"])
        add(f"update{cycle}", (1, 0), cut(b["farown"], 0), cut(b["far"], 0))
        add(f"update{cycle}", (-1, 0), cut(b["farown"], 1), cut(b["far"], 1))
        add_packets(f"update{cycle}", b["up"], b["down"], b["low"], b["high"])
        add_corners(f"update{cycle}", b["cs"], b["cr"])
        add_dense(f"fine{cycle}", b["fine"])
        add_dense(f"solution{cycle}", b["solution"])
    add("first", (1, 0), cut(m["first"], 4, 3), cut(m["first"], 0, 3))
    add("first", (-1, 0), cut(m["first"], 3, 3), cut(m["first"], 7, 3))
    add_packets("first", m["fup"], m["fdown"], m["flow"], m["fhigh"])
    add_corners("first", m["fcs"], m["fcr"])
    steps = sorted({entry[1] for entry in plan})

    for step in steps:
        @pl.when(jnp.logical_not(exists(-step[0], -step[1])))
        def _(step=step):
            for _, other, _, dst, _ in plan:
                if other == step:
                    dst[...] = jnp.zeros(dst.shape, f32)

    def remote(entry):
        _, (dx, dy), src, dst, i = entry
        return pltpu.make_async_remote_copy(
            src_ref=src, dst_ref=dst, send_sem=m["send_sem"].at[i], recv_sem=m["recv_sem"].at[i],
            device_id=(gx + dx, gy + dy), device_id_type=MESH,
        )

    def each(names, sign, act):
        for step in steps:
            mine = [entry for entry in plan if entry[0] in names and entry[1] == step]
            if mine:
                @pl.when(exists(sign * step[0], sign * step[1]))
                def _(mine=mine):
                    for entry in mine:
                        act(remote(entry))

    def start(*names):
        each(names, 1, lambda copy: copy.start())

    def receive(*names):
        each(names, -1, lambda copy: copy.wait_recv())

    row8, lane8, lane16 = iota((8, depth), 0), iota((8, depth), 1), iota((16, depth), 1)
    even_row, even_lane = row8 % 2 == 0, lane8 % 2 == 0

    def roll(value, shift, dim):
        size = value.shape[dim]
        return pltpu.roll(value, shift % size, dim) if shift % size else value

    def pack2(values, top):
        result = None
        for c, v in enumerate(values):
            v = roll(v, 2 * c + 2 if top else 2 * c, 0)
            result = v if c == 0 else jnp.where(row8 >= 2 * c, v, result)
        return result

    def unpack2(low, high, c):
        return jnp.where(row8 < 4, roll(high, -2 * c, 0), roll(low, 6 - 2 * c, 0))

    def pack4(pair, top):
        re, im = pair
        return jnp.where(row8 < 4, roll(re, 4, 0), im) if top else jnp.where(row8 < 4, re, roll(im, 4, 0))

    def unpack4(low, high):
        return jnp.where(row8 < 4, high, roll(low, 4, 0)), jnp.where(row8 < 4, roll(high, 4, 0), low)

    def put_corners(cs, j, near_low, near_high, from_edge):
        for i, (dx, dy) in enumerate(CORNERS):
            pair = near_high if dx > 0 else near_low
            at = 7 - from_edge if dy > 0 else from_edge
            for c, v in enumerate(pair):
                cs[i, j + c] = v[at : at + 1]

    def got_corner(cr, side, j):
        i = CORNERS.index((-side, 1))
        return cr[i, j], cr[i + 1, j]

    def corner_tile(cr, side, j, thick=1):
        below, above = got_corner(cr, side, j)
        return jnp.where(row8 >= 8 - thick, below, jnp.where(row8 < thick, above, 0.0))

    def pack_dense(first, second):
        return jnp.where(
            even_lane, jnp.where(even_row, first[0], first[1]), jnp.where(even_row, second[0], second[1])
        )

    def unpack_dense(tile):
        re = jnp.where(even_row, tile, roll(tile, 1, 0))
        im = jnp.where(even_row, roll(tile, -1, 0), tile)
        first = tuple(jnp.where(even_lane, v, roll(v, 1, 1)) for v in (re, im))
        second = tuple(jnp.where(even_lane, roll(v, -1, 1), v) for v in (re, im))
        return first, second

    def send_dense(b, planes):
        b["own"][...] = pack_dense(*planes)
        if "cs" in b:
            put_corners(b["cs"], 0, planes[0], planes[1], 0)

    def get_dense(b, own):
        before, after, below, above = [unpack_dense(b["got"][i]) for i in range(4)]
        none = jnp.zeros((8, depth), f32)
        result = []
        for p, plane in enumerate([*before, *own, *after]):
            pair = []
            for c in range(2):
                if p in (2, 3):
                    halo = jnp.where(row8 < 4, above[p - 2][c], below[p - 2][c])
                elif p in (1, 4) and "cr" in b:
                    halo = corner_tile(b["cr"], -1 if p == 1 else 1, c, 2)
                else:
                    halo = none
                pair.append(jnp.concatenate([plane[c], halo], axis=0))
            result.append(tuple(pair))
        return result

    def around(before, mid, after, s):
        total = before + after + roll(mid, s, 0) + roll(mid, -s, 0)
        total = total + jnp.where(lane16 >= s, roll(mid, s, 1), 0.0)
        return total + jnp.where(lane16 < depth - s, roll(mid, -s, 1), 0.0)

    def load(ref, plane, rows=None):
        return tuple(ref[plane, c] if rows is None else ref[plane, c, :rows] for c in range(2))

    def store(ref, plane, pair):
        ref[plane, 0], ref[plane, 1] = pair

    def neighbours(ref, plane, s):
        return tuple(around(ref[plane - 1, c], ref[plane, c], ref[plane + 1, c], s) for c in range(2))

    def weight(diag):
        scale = OMEGA / (diag[0] * diag[0] + diag[1] * diag[1])
        return diag[0] * scale, -diag[1] * scale

    def first_two(wf_ref, w_ref, target, planes, s, c):
        for p in planes:
            part = product(load(w_ref, p), neighbours(wf_ref, p, s))
            store(target, p, tuple(1.4 * a + c * b for a, b in zip(load(wf_ref, p), part)))

    def sweep(ref, wf_ref, w_ref, planes, s, c):
        for p in planes:
            part = product(load(w_ref, p), neighbours(ref, p, s))
            yield p, tuple(0.4 * a + b + c * d for a, b, d in zip(load(ref, p), load(wf_ref, p), part))

    def residual(source, diag, ref, p, s, c):
        ns, part = neighbours(ref, p, s), product(diag, load(ref, p, 8))
        return tuple(f + c * n[:8] - q for f, n, q in zip(source, ns, part))

    def pair_mean(value):
        value = value + jnp.where(even_row, roll(value, -1, 0), roll(value, 1, 0))
        other = jnp.where(even_lane, roll(value, -1, 1), roll(value, 1, 1))
        return (value + other) * 0.125

    def own8(pair):
        return tuple(v[:8] for v in pair)

    for load_copy in loads:
        load_copy.wait()
    shifts, weights, scaled = [], [], []
    for p in range(4):
        index = m["layer"][p]
        velocity = jnp.zeros((8, depth), f32)
        for number in range(m["table"].shape[0]):
            velocity = jnp.where(index == number, m["table"][number], velocity)
        ratio = KH_FACTOR / velocity
        kh2 = ratio * ratio
        shift = (kh2, -kh2 * (BETA + ABSORB * m["absorb"][p].astype(f32)))
        diag = (6.0 - shift[0], -shift[1])
        source = (m["rhs"][0, p], m["rhs"][1, p])
        w = weight(diag)
        wf = product(w, source)
        store(m["diag0"], p, diag)
        store(m["source0"], p, source)
        store(m["ewf"], p + 2, wf)
        store(m["ew"], p + 2, w)
        m["up"][p] = pack2([*wf, *w], True)
        m["down"][p] = pack2([*wf, *w], False)
        shifts.append(shift)
        weights.append(w)
        scaled.append(wf)
    put_corners(m["cs"], 0, scaled[0], scaled[3], 0)
    put_corners(m["cs"], 2, weights[0], weights[3], 0)
    pl.semaphore_wait(barrier, count - 1)
    start("begin")
    shifts1 = [tuple(pair_mean(shifts[p][c] + shifts[p + 1][c]) for c in range(2)) for p in (0, 2)]
    diags1 = [(1.5 - s[0], -s[1]) for s in shifts1]
    weights1 = [weight(d) for d in diags1]
    send_dense(m["coef1"], weights1)
    start("coef1", "later")
    for p in range(2):
        store(m["diag1"], p, diags1[p])

    spread = 0.25 * (iota((depth, 128), 0) // 4 == iota((depth, 128), 1)).astype(f32)
    spread = spread.astype(jnp.bfloat16)
    widen = (iota((128, depth), 1) // 4 == iota((128, depth), 0)).astype(f32).astype(jnp.bfloat16)
    rows2 = 2 * ngy
    shift2_sum = tuple(shifts1[0][c] + shifts1[1][c] for c in range(2))
    m["padded"][...] = jnp.zeros(m["padded"].shape, f32)
    row2 = iota((ngx, rows2, 128), 1)
    block8 = iota((8, 128), 0) // 2

    def unpack(buffer, comp):
        planes = []
        for x in range(ngx):
            groups = []
            for q in range(0, ngy, 4):
                value = buffer[x * ngy + q]
                for j in range(1, min(4, ngy - q)):
                    value = jnp.where(block8 == (comp + j) % 4, buffer[x * ngy + q + j], value)
                groups.append(roll(value, -2 * comp, 0))
            planes.append(jnp.concatenate(groups, axis=0)[:rows2] if len(groups) > 1 else groups[0][:rows2])
        return jnp.stack(planes)

    coarse = {}

    def coarsest(cycle, sums):
        buffer = m["cycles"][cycle]["tiles"]
        tile = jnp.zeros((8, depth), f32)
        for c, v in enumerate(list(sums) + (list(shift2_sum) if cycle == 0 else [])):
            v = v + jnp.where(row8 // 2 % 2 == 0, roll(v, -2, 0), roll(v, 2, 0))
            tile = jnp.where(row8 // 2 == c, roll(v, 2 * c - 3, 0), tile)
        tile = dot3(tile * 0.25, spread)
        buffer[me] = pltpu.roll(tile, 2 * lax.rem(gy, 4), 0)

        others(
            lambda x, y: pltpu.make_async_remote_copy(
                src_ref=buffer.at[me], dst_ref=buffer.at[me],
                send_sem=m["tile_send"].at[cycle], recv_sem=m["tile_recv"].at[cycle],
                device_id=(x, y), device_id_type=MESH,
            ).start()
        )

    def coarsest_finish(cycle):
        buffer = m["cycles"][cycle]["tiles"]
        every = buffer.at[pl.ds(0, count - 1)]
        pltpu.make_async_copy(every, every, m["tile_recv"].at[cycle]).wait()
        source = unpack(buffer, 0), unpack(buffer, 1)
        if cycle == 0:
            shift = unpack(buffer, 2), unpack(buffer, 3)
            full = weight((0.375 - shift[0], -shift[1]))
            coarse["w"] = tuple(jnp.where(shift[0] > 0.0, v, 0.0) for v in full)
        w = coarse["w"]
        wf = product(w, source)
        none = jnp.zeros((1, rows2, 128), f32)

        def total(e):
            result = jnp.concatenate([none, e[:-1]], axis=0) + jnp.concatenate([e[1:], none], axis=0)
            result = result + jnp.where(row2 > 0, roll(e, 1, 1), 0.0)
            result = result + jnp.where(row2 < rows2 - 1, roll(e, -1, 1), 0.0)
            return result + roll(e, 1, 2) + roll(e, -1, 2)

        def step(_, e):
            part = product(w, (total(e[0]), total(e[1])))
            return tuple(0.4 * a + b + 0.0625 * d for a, b, d in zip(e, wf, part))

        e = lax.fori_loop(0, NC - 1, step, wf)
        for c in range(2):
            for x in range(ngx):
                m["padded"][x + 1, c, 8 : 8 + rows2] = e[c][x]
        own = [m["padded"][gx + i, c, pl.ds(7 + 2 * gy, 8)] for i in range(3) for c in range(2)]
        wide = dot3(jnp.concatenate(own, axis=0), widen)
        result = []
        for i in range(3):
            pair = []
            for c in range(2):
                below, low, high, above = [wide[16 * i + 8 * c + k : 16 * i + 8 * c + k + 1] for k in range(4)]
                pair.append(
                    jnp.concatenate([jnp.where(row8 < 4, low, high), jnp.where(row8 < 4, above, below)], axis=0)
                )
            result.append(tuple(pair))
        return result

    def cycle_part(cycle):
        b = m["cycles"][cycle]
        wf0, w0, upd0, upd0b = m["wf0"], m["w0"], m["upd0"], m["upd0b"]
        wf1, w1, upd1, upd1b = m["wf1"], m["w1"], m["upd1"], m["upd1b"]
        first_two(wf0, w0, upd0, range(1, 7), 1, 1.0)
        held = [residual(load(m["source0"], p), load(m["diag0"], p), upd0, p + 2, 1, 1.0) for p in range(4)]
        sources = [tuple(pair_mean(held[p][c] + held[p + 1][c]) for c in range(2)) for p in (0, 2)]
        scaled1 = [product(weights1[p], sources[p]) for p in range(2)]
        send_dense(b["source"], scaled1)
        start(f"source{cycle}")
        updates = [load(upd0, p + 2, 8) for p in range(4)]
        store(b["farown"], 0, updates[2])
        store(b["farown"], 1, updates[1])
        for i in range(2):
            b["up"][i] = pack2([*updates[2 * i], *updates[2 * i + 1]], True)
            b["down"][i] = pack2([*updates[2 * i], *updates[2 * i + 1]], False)
        put_corners(b["cs"], 0, updates[0], updates[3], 0)
        start(f"update{cycle}")
        if cycle == 0:
            receive("coef1")
            for p, pair in enumerate(get_dense(m["coef1"], weights1)):
                store(w1, p, pair)
        receive(f"source{cycle}")
        for p, pair in enumerate(get_dense(b["source"], scaled1)):
            store(wf1, p, pair)
        first_two(wf1, w1, upd1, range(1, 5), 2, 0.25)
        left, right = [residual(sources[p], load(m["diag1"], p), upd1, p + 2, 2, 0.25) for p in range(2)]
        coarsest(cycle, tuple(left[c] + right[c] for c in range(2)))
        updates1 = [load(upd1, p + 2, 8) for p in range(2)]
        send_dense(b["fine"], updates1)
        start(f"fine{cycle}")
        receive(f"update{cycle}", f"fine{cycle}")
        around1 = get_dense(b["fine"], updates1)
        none = jnp.zeros((8, depth), f32)
        for c in range(2):
            upd0[0, c] = jnp.concatenate([b["far"][0, c], none], axis=0)
            upd0[7, c] = jnp.concatenate([b["far"][1, c], none], axis=0)
            upd0[1, c, 8:] = corner_tile(b["cr"], -1, c)
            upd0[6, c, 8:] = corner_tile(b["cr"], 1, c)
            for p in range(4):
                upd0[p + 2, c, 8:] = unpack2(b["low"][p // 2], b["high"][p // 2], 2 * (p % 2) + c)
        correction = coarsest_finish(cycle)
        for p, e in enumerate(around1):
            store(upd1, p, tuple(v + x for v, x in zip(e, correction[p // 2])))
        for p, e in sweep(upd1, wf1, w1, range(1, 5), 2, 0.25):
            store(upd1b, p, e)
        solved = [own8(e) for _, e in sweep(upd1b, wf1, w1, range(2, 4), 2, 0.25)]
        send_dense(b["solution"], solved)
        start(f"solution{cycle}")
        receive(f"solution{cycle}")
        around1 = get_dense(b["solution"], solved)
        for p in range(8):
            store(upd0, p, tuple(v + x for v, x in zip(load(upd0, p), around1[p // 2 + 1])))
        for p, e in sweep(upd0, wf0, w0, range(1, 7), 1, 1.0):
            store(upd0b, p, e)
        for p, e in sweep(upd0b, wf0, w0, range(2, 6), 1, 1.0):
            yield p - 2, own8(e)

    none = jnp.zeros((8, depth), f32)

    def halo0(p, j):
        if p in (1, 6):
            return corner_tile(m["cr"], -1 if p == 1 else 1, j)
        if p in (0, 7):
            return none
        return unpack2(m["low"][p - 2], m["high"][p - 2], j)

    receive("begin")
    for p in range(8):
        for c in range(2):
            m["wf0"][p, c] = jnp.concatenate([m["ewf"][p, c], halo0(p, c)], axis=0)
            if p in (0, 7):
                m["w0"][p, c, 8:] = none
            else:
                m["w0"][p, c] = jnp.concatenate([m["ew"][p, c], halo0(p, 2 + c)], axis=0)
    kept = []
    for p, e in cycle_part(0):
        store(m["first"], p + 3, e)
        m["fup"][p] = pack4(e, True)
        m["fdown"][p] = pack4(e, False)
        kept.append(e)
    put_corners(m["fcs"], 0, kept[0], kept[3], 0)
    put_corners(m["fcs"], 2, kept[0], kept[3], 1)
    put_corners(m["fcs"], 4, kept[1], kept[2], 0)
    start("first")
    receive("first", "later")
    for p in (0, 7):
        for c in range(2):
            m["w0"][p, c, :8] = m["ew"][p, c]
    for p in range(10):
        if 3 <= p < 7:
            halo = unpack4(m["flow"][p - 3], m["fhigh"][p - 3])
        elif p in (2, 7):
            side, halo = (-1 if p == 2 else 1), []
            for c in range(2):
                below, above = got_corner(m["fcr"], side, c)
                below2, above2 = got_corner(m["fcr"], side, 2 + c)
                tile = jnp.where(row8 == 7, below, jnp.where(row8 == 6, below2, 0.0))
                halo.append(jnp.where(row8 == 0, above, jnp.where(row8 == 1, above2, tile)))
        elif p in (1, 8):
            halo = [corner_tile(m["fcr"], -1 if p == 1 else 1, 4 + c) for c in range(2)]
        else:
            halo = [none, none]
        for c in range(2):
            m["first16"][p, c] = jnp.concatenate([m["first"][p, c], halo[c]], axis=0)
    for p in range(8):
        ns = neighbours(m["first16"], p + 1, 1)
        e = load(m["first16"], p + 1)
        if 2 <= p < 6:
            part = product(load(m["diag0"], p - 2), own8(e))
            source = load(m["source0"], p - 2)
            store(m["source0"], p - 2, tuple(f + n[:8] - q for f, n, q in zip(source, ns, part)))
        part = product(load(m["w0"], p), ns)
        store(m["wf0"], p, tuple(a + b - OMEGA * v for a, b, v in zip(load(m["wf0"], p), part, e)))
    for p, e in cycle_part(1):
        for c in range(2):
            out[c, p] = m["first"][p + 3, c] + e[c]

    for step in steps:
        @pl.when(exists(*step))
        def _(step=step):
            for entry in plan:
                if entry[1] == step:
                    remote(entry).wait_send()
    for cycle in range(2):
        every = m["cycles"][cycle]["tiles"].at[pl.ds(0, count - 1)]
        pltpu.make_async_copy(every, every, m["tile_send"].at[cycle]).wait()


def local(ngx, ngy, right_side, velocity_table, layer_index, absorb_level):
    depth = right_side.shape[-1]
    scratch = scratch_of(ngx, ngy, velocity_table.shape[0], depth)
    leaves, tree = jax.tree.flatten(scratch)
    anywhere = pl.BlockSpec(memory_space=pltpu.HBM)
    return pl.pallas_call(
        functools.partial(kernel, ngx, ngy, depth, tree),
        out_shape=jax.ShapeDtypeStruct(right_side.shape, jnp.float32),
        in_specs=[anywhere] * 4,
        out_specs=pl.BlockSpec(memory_space=pltpu.VMEM),
        scratch_shapes=leaves,
        compiler_params=pltpu.CompilerParams(
            collective_id=0, has_side_effects=True, vmem_limit_bytes=64 * 1024 * 1024 - 65536
        ),
    )(right_side, velocity_table, layer_index, absorb_level)


def solution(mesh):
    placed = (P(None, "gx", "gy", None), P(), P("gx", "gy", None), P("gx", "gy", None))
    return jax.shard_map(
        functools.partial(local, mesh.shape["gx"], mesh.shape["gy"]),
        mesh=mesh, in_specs=placed, out_specs=P(None, "gx", "gy", None), check_vma=False,
    )
```

```python
import functools
import math

import jax
import jax.numpy as jnp
from jax import lax
from jax.experimental import pallas as pl
from jax.experimental.pallas import tpu as pltpu
from jax.sharding import PartitionSpec as P

NC = 8
OMEGA = 0.6
BETA = 0.5
ABSORB = 0.25
KH_FACTOR = 2.0 * math.pi * 6.0 * 20.0
MESH = pl.DeviceIdType.MESH

AROUND = [(dx, dy) for dx in range(-2, 3) for dy in (-1, 0, 1) if dx or dy]
FACES = [(1, 0), (-1, 0), (0, 1), (0, -1)]
CORNERS = [(1, 1), (1, -1), (-1, 1), (-1, -1)]


def product(a, b):
    return a[0] * b[0] - a[1] * b[1], a[0] * b[1] + a[1] * b[0]


def dot3(a, b):
    rows = a.shape[0]
    pieces, rest = [], a
    for _ in range(3):
        piece = rest.astype(jnp.bfloat16).astype(jnp.float32)
        pieces.append(piece)
        rest = rest - piece
    stacked = jnp.concatenate(pieces, axis=0).astype(jnp.bfloat16)
    result = jnp.dot(stacked, b, preferred_element_type=jnp.float32)
    return result[:rows] + result[rows : 2 * rows] + result[2 * rows :]


def iota(shape, dim):
    return lax.broadcasted_iota(jnp.int32, shape, dim)


def scratch_of(ngx, ngy, layers, depth):
    f32 = jnp.float32

    def vmem(*shape):
        return pltpu.VMEM(shape, f32)

    def dense():
        return dict(own=vmem(8, depth), got=vmem(4, 8, depth), cs=vmem(4, 2, 1, depth), cr=vmem(4, 2, 1, depth))

    cycles = [
        dict(
            source=dense(), fine=dict(own=vmem(8, depth), got=vmem(len(AROUND), 8, depth)), csource=vmem(4, 8, depth),
            far=vmem(2, 2, 8, depth), farown=vmem(2, 2, 8, depth),
            up=vmem(2, 8, depth), down=vmem(2, 8, depth), low=vmem(2, 8, depth), high=vmem(2, 8, depth),
            cs=vmem(4, 2, 1, depth), cr=vmem(4, 2, 1, depth), tiles=vmem(ngx * ngy, 8, 128),
        )
        for _ in range(2)
    ]
    return dict(
        rhs=vmem(2, 4, 8, depth), layer=pltpu.VMEM((4, 8, depth), jnp.int32),
        absorb=pltpu.VMEM((4, 8, depth), jnp.int32), table=pltpu.SMEM((layers,), f32),
        ewf=vmem(8, 2, 8, depth), ew=vmem(8, 2, 8, depth),
        up=vmem(4, 8, depth), down=vmem(4, 8, depth), low=vmem(4, 8, depth), high=vmem(4, 8, depth),
        cs=vmem(4, 4, 1, depth), cr=vmem(4, 4, 1, depth),
        coef1=dict(own=vmem(8, depth), got=vmem(4, 8, depth)), ccoef1=vmem(4, 8, depth),
        first=vmem(10, 2, 8, depth),
        fup=vmem(4, 8, depth), fdown=vmem(4, 8, depth), flow=vmem(4, 8, depth), fhigh=vmem(4, 8, depth),
        fcs=vmem(4, 6, 1, depth), fcr=vmem(4, 6, 1, depth),
        cycles=cycles,
        diag0=vmem(4, 2, 8, depth), source0=vmem(4, 2, 8, depth),
        wf0=vmem(8, 2, 16, depth), w0=vmem(8, 2, 16, depth), upd0=vmem(8, 2, 16, depth), upd0b=vmem(8, 2, 16, depth),
        first16=vmem(10, 2, 16, depth),
        diag1=vmem(2, 2, 8, depth), source1=vmem(2, 2, 8, depth),
        wf1=vmem(6, 2, 16, depth), w1=vmem(6, 2, 16, depth), upd1=vmem(6, 2, 16, depth),
        wide_wf1=vmem(6, 2, 24, depth), wide_w1=vmem(6, 2, 24, depth),
        wide1=vmem(8, 2, 24, depth), wide1b=vmem(8, 2, 24, depth),
        padded=vmem(ngx + 4, 2, 2 * ngy + 16, 128),
        send_sem=pltpu.SemaphoreType.DMA((112,)), recv_sem=pltpu.SemaphoreType.DMA((112,)),
        tile_send=pltpu.SemaphoreType.DMA((2,)), tile_recv=pltpu.SemaphoreType.DMA((2,)),
        load_sem=pltpu.SemaphoreType.DMA((4,)),
    )


def kernel(ngx, ngy, depth, tree, rhs_in, table_in, layer_in, absorb_in, out, *scratch):
    m = jax.tree.unflatten(tree, scratch)
    count = ngx * ngy
    gx, gy = lax.axis_index("gx"), lax.axis_index("gy")
    me = gx * ngy + gy
    f32 = jnp.float32

    loads = [
        pltpu.make_async_copy(a, m[b], m["load_sem"].at[i])
        for i, (a, b) in enumerate(((layer_in, "layer"), (absorb_in, "absorb"), (table_in, "table"), (rhs_in, "rhs")))
    ]
    for load_copy in loads:
        load_copy.start()

    barrier = pltpu.get_barrier_semaphore()

    def others(act):
        if count > 64:
            def one(k, carry):
                other = lax.rem(me + k, count)
                act(other // ngy, lax.rem(other, ngy))
                return carry

            lax.fori_loop(1, count, one, 0)
            return
        for i in reversed(range(ngx)):
            for j in reversed(range(ngy)):
                if i or j:
                    x, y = gx + i, gy + j
                    act(jnp.where(x >= ngx, x - ngx, x), jnp.where(y >= ngy, y - ngy, y))

    others(lambda x, y: pl.semaphore_signal(barrier, inc=1, device_id=(x, y), device_id_type=MESH))

    def exists(dx, dy):
        checks = []
        if dx:
            checks.append(gx < ngx - dx if dx > 0 else gx >= -dx)
        if dy:
            checks.append(gy < ngy - 1 if dy > 0 else gy > 0)
        return functools.reduce(jnp.logical_and, checks)

    plan = []

    def add(name, step, src, dst):
        plan.append((name, step, src, dst, len(plan)))

    def cut(ref, first, size=1):
        return ref.at[pl.ds(first, size)]

    def add_packets(name, up, down, low, high):
        add(name, (0, 1), up, low)
        add(name, (0, -1), down, high)

    def add_corners(name, cs, cr):
        for i, step in enumerate(CORNERS):
            add(name, step, cs.at[i], cr.at[i])

    def add_dense(name, b):
        for i, step in enumerate(FACES):
            add(name, step, b["own"], b["got"].at[i])
        if "cs" in b:
            add_corners(name, b["cs"], b["cr"])

    add("begin", (1, 0), cut(m["ewf"], 4, 2), cut(m["ewf"], 0, 2))
    add("begin", (-1, 0), cut(m["ewf"], 2, 2), cut(m["ewf"], 6, 2))
    add("begin", (1, 0), cut(m["ew"], 5), cut(m["ew"], 1))
    add("begin", (-1, 0), cut(m["ew"], 2), cut(m["ew"], 6))
    add_packets("begin", m["up"], m["down"], m["low"], m["high"])
    add_corners("begin", m["cs"], m["cr"])
    add_dense("coef1", m["coef1"])
    for i, step in enumerate(CORNERS):
        add("later1", step, m["coef1"]["own"], m["ccoef1"].at[i])
    add("later", (1, 0), cut(m["ew"], 4), cut(m["ew"], 0))
    add("later", (-1, 0), cut(m["ew"], 3), cut(m["ew"], 7))
    for cycle in range(2):
        b = m["cycles"][cycle]
        add_dense(f"source{cycle}", b["source"])
        add(f"update{cycle}", (1, 0), cut(b["farown"], 0), cut(b["far"], 0))
        add(f"update{cycle}", (-1, 0), cut(b["farown"], 1), cut(b["far"], 1))
        add_packets(f"update{cycle}", b["up"], b["down"], b["low"], b["high"])
        add_corners(f"update{cycle}", b["cs"], b["cr"])
        for i, step in enumerate(AROUND):
            add(f"fine{cycle}", step, b["fine"]["own"], b["fine"]["got"].at[i])
        for i, step in enumerate(CORNERS):
            add(f"fine{cycle}", step, b["source"]["own"], b["csource"].at[i])
    add("first", (1, 0), cut(m["first"], 4, 3), cut(m["first"], 0, 3))
    add("first", (-1, 0), cut(m["first"], 3, 3), cut(m["first"], 7, 3))
    add_packets("first", m["fup"], m["fdown"], m["flow"], m["fhigh"])
    add_corners("first", m["fcs"], m["fcr"])
    steps = sorted({entry[1] for entry in plan})

    for step in steps:
        @pl.when(jnp.logical_not(exists(-step[0], -step[1])))
        def _(step=step):
            for _, other, _, dst, _ in plan:
                if other == step:
                    dst[...] = jnp.zeros(dst.shape, f32)

    def remote(entry):
        _, (dx, dy), src, dst, i = entry
        return pltpu.make_async_remote_copy(
            src_ref=src, dst_ref=dst, send_sem=m["send_sem"].at[i], recv_sem=m["recv_sem"].at[i],
            device_id=(gx + dx, gy + dy), device_id_type=MESH,
        )

    def each(names, sign, act):
        for step in steps:
            mine = [entry for entry in plan if entry[0] in names and entry[1] == step]
            if mine:
                @pl.when(exists(sign * step[0], sign * step[1]))
                def _(mine=mine):
                    for entry in mine:
                        act(remote(entry))

    def start(*names):
        each(names, 1, lambda copy: copy.start())

    def receive(*names):
        each(names, -1, lambda copy: copy.wait_recv())

    row8, lane8 = iota((8, depth), 0), iota((8, depth), 1)
    even_row, even_lane = row8 % 2 == 0, lane8 % 2 == 0

    def roll(value, shift, dim):
        size = value.shape[dim]
        return pltpu.roll(value, shift % size, dim) if shift % size else value

    def pack2(values, top):
        result = None
        for c, v in enumerate(values):
            v = roll(v, 2 * c + 2 if top else 2 * c, 0)
            result = v if c == 0 else jnp.where(row8 >= 2 * c, v, result)
        return result

    def unpack2(low, high, c):
        return jnp.where(row8 < 4, roll(high, -2 * c, 0), roll(low, 6 - 2 * c, 0))

    def pack4(pair, top):
        re, im = pair
        return jnp.where(row8 < 4, roll(re, 4, 0), im) if top else jnp.where(row8 < 4, re, roll(im, 4, 0))

    def unpack4(low, high):
        return jnp.where(row8 < 4, high, roll(low, 4, 0)), jnp.where(row8 < 4, roll(high, 4, 0), low)

    def put_corners(cs, j, near_low, near_high, from_edge):
        for i, (dx, dy) in enumerate(CORNERS):
            pair = near_high if dx > 0 else near_low
            at = 7 - from_edge if dy > 0 else from_edge
            for c, v in enumerate(pair):
                cs[i, j + c] = v[at : at + 1]

    def got_corner(cr, side, j):
        i = CORNERS.index((-side, 1))
        return cr[i, j], cr[i + 1, j]

    def corner_tile(cr, side, j, thick=1):
        below, above = got_corner(cr, side, j)
        return jnp.where(row8 >= 8 - thick, below, jnp.where(row8 < thick, above, 0.0))

    def pack_dense(first, second):
        return jnp.where(
            even_lane, jnp.where(even_row, first[0], first[1]), jnp.where(even_row, second[0], second[1])
        )

    def unpack_dense(tile):
        re = jnp.where(even_row, tile, roll(tile, 1, 0))
        im = jnp.where(even_row, roll(tile, -1, 0), tile)
        first = tuple(jnp.where(even_lane, v, roll(v, 1, 1)) for v in (re, im))
        second = tuple(jnp.where(even_lane, roll(v, -1, 1), v) for v in (re, im))
        return first, second

    def send_dense(b, planes):
        b["own"][...] = pack_dense(*planes)
        if "cs" in b:
            put_corners(b["cs"], 0, planes[0], planes[1], 0)

    def get_dense(b, own):
        before, after, below, above = [unpack_dense(b["got"][i]) for i in range(4)]
        none = jnp.zeros((8, depth), f32)
        result = []
        for p, plane in enumerate([*before, *own, *after]):
            pair = []
            for c in range(2):
                if p in (2, 3):
                    halo = jnp.where(row8 < 4, above[p - 2][c], below[p - 2][c])
                elif p in (1, 4) and "cr" in b:
                    halo = corner_tile(b["cr"], -1 if p == 1 else 1, c, 2)
                else:
                    halo = none
                pair.append(jnp.concatenate([plane[c], halo], axis=0))
            result.append(tuple(pair))
        return result

    def around(before, mid, after, s):
        total = before + after + roll(mid, s, 0) + roll(mid, -s, 0)
        lane = iota(mid.shape, 1)
        total = total + jnp.where(lane >= s, roll(mid, s, 1), 0.0)
        return total + jnp.where(lane < depth - s, roll(mid, -s, 1), 0.0)

    def load(ref, plane, rows=None):
        return tuple(ref[plane, c] if rows is None else ref[plane, c, :rows] for c in range(2))

    def store(ref, plane, pair):
        ref[plane, 0], ref[plane, 1] = pair

    def neighbours(ref, plane, s):
        return tuple(around(ref[plane - 1, c], ref[plane, c], ref[plane + 1, c], s) for c in range(2))

    def weight(diag):
        scale = OMEGA / (diag[0] * diag[0] + diag[1] * diag[1])
        return diag[0] * scale, -diag[1] * scale

    def first_two(wf_ref, w_ref, target, planes, s, c):
        for p in planes:
            part = product(load(w_ref, p), neighbours(wf_ref, p, s))
            store(target, p, tuple(1.4 * a + c * b for a, b in zip(load(wf_ref, p), part)))

    def sweep(ref, wf_ref, w_ref, planes, s, c, behind=0):
        for p in planes:
            part = product(load(w_ref, p - behind), neighbours(ref, p, s))
            wf = load(wf_ref, p - behind)
            yield p, tuple(0.4 * a + b + c * d for a, b, d in zip(load(ref, p), wf, part))

    def wide_planes(tile_of, reach):
        result = []
        for rx in range(-reach, reach + 1):
            blocks = [tile_of(rx, ry) for ry in (0, 1, -1)]
            for half in range(2):
                result.append(tuple(jnp.concatenate([v[half][c] for v in blocks], axis=0) for c in range(2)))
        return result

    def residual(source, diag, ref, p, s, c):
        ns, part = neighbours(ref, p, s), product(diag, load(ref, p, 8))
        return tuple(f + c * n[:8] - q for f, n, q in zip(source, ns, part))

    def pair_mean(value):
        value = value + jnp.where(even_row, roll(value, -1, 0), roll(value, 1, 0))
        other = jnp.where(even_lane, roll(value, -1, 1), roll(value, 1, 1))
        return (value + other) * 0.125

    def own8(pair):
        return tuple(v[:8] for v in pair)

    for load_copy in loads:
        load_copy.wait()
    shifts, weights, scaled = [], [], []
    for p in range(4):
        index = m["layer"][p]
        velocity = jnp.zeros((8, depth), f32)
        for number in range(m["table"].shape[0]):
            velocity = jnp.where(index == number, m["table"][number], velocity)
        ratio = KH_FACTOR / velocity
        kh2 = ratio * ratio
        shift = (kh2, -kh2 * (BETA + ABSORB * m["absorb"][p].astype(f32)))
        diag = (6.0 - shift[0], -shift[1])
        source = (m["rhs"][0, p], m["rhs"][1, p])
        w = weight(diag)
        wf = product(w, source)
        store(m["diag0"], p, diag)
        store(m["source0"], p, source)
        store(m["ewf"], p + 2, wf)
        store(m["ew"], p + 2, w)
        m["up"][p] = pack2([*wf, *w], True)
        m["down"][p] = pack2([*wf, *w], False)
        shifts.append(shift)
        weights.append(w)
        scaled.append(wf)
    put_corners(m["cs"], 0, scaled[0], scaled[3], 0)
    put_corners(m["cs"], 2, weights[0], weights[3], 0)
    pl.semaphore_wait(barrier, count - 1)
    start("begin")
    shifts1 = [tuple(pair_mean(shifts[p][c] + shifts[p + 1][c]) for c in range(2)) for p in (0, 2)]
    diags1 = [(1.5 - s[0], -s[1]) for s in shifts1]
    weights1 = [weight(d) for d in diags1]
    send_dense(m["coef1"], weights1)
    start("coef1", "later", "later1")
    for p in range(2):
        store(m["diag1"], p, diags1[p])

    spread = 0.25 * (iota((depth, 128), 0) // 4 == iota((depth, 128), 1)).astype(f32)
    spread = spread.astype(jnp.bfloat16)
    widen = (iota((128, depth), 1) // 4 == iota((128, depth), 0)).astype(f32).astype(jnp.bfloat16)
    rows2 = 2 * ngy
    shift2_sum = tuple(shifts1[0][c] + shifts1[1][c] for c in range(2))
    m["padded"][...] = jnp.zeros(m["padded"].shape, f32)
    row2 = iota((ngx, rows2, 128), 1)
    block8 = iota((8, 128), 0) // 2

    def unpack(buffer, comp):
        planes = []
        for x in range(ngx):
            groups = []
            for q in range(0, ngy, 4):
                value = buffer[x * ngy + q]
                for j in range(1, min(4, ngy - q)):
                    value = jnp.where(block8 == (comp + j) % 4, buffer[x * ngy + q + j], value)
                groups.append(roll(value, -2 * comp, 0))
            planes.append(jnp.concatenate(groups, axis=0)[:rows2] if len(groups) > 1 else groups[0][:rows2])
        return jnp.stack(planes)

    coarse = {}

    def coarsest(cycle, sums):
        buffer = m["cycles"][cycle]["tiles"]
        tile = jnp.zeros((8, depth), f32)
        for c, v in enumerate(list(sums) + (list(shift2_sum) if cycle == 0 else [])):
            v = v + jnp.where(row8 // 2 % 2 == 0, roll(v, -2, 0), roll(v, 2, 0))
            tile = jnp.where(row8 // 2 == c, roll(v, 2 * c - 3, 0), tile)
        tile = dot3(tile * 0.25, spread)
        buffer[me] = pltpu.roll(tile, 2 * lax.rem(gy, 4), 0)

        others(
            lambda x, y: pltpu.make_async_remote_copy(
                src_ref=buffer.at[me], dst_ref=buffer.at[me],
                send_sem=m["tile_send"].at[cycle], recv_sem=m["tile_recv"].at[cycle],
                device_id=(x, y), device_id_type=MESH,
            ).start()
        )

    def coarsest_finish(cycle):
        buffer = m["cycles"][cycle]["tiles"]
        every = buffer.at[pl.ds(0, count - 1)]
        pltpu.make_async_copy(every, every, m["tile_recv"].at[cycle]).wait()
        source = unpack(buffer, 0), unpack(buffer, 1)
        if cycle == 0:
            shift = unpack(buffer, 2), unpack(buffer, 3)
            full = weight((0.375 - shift[0], -shift[1]))
            coarse["w"] = tuple(jnp.where(shift[0] > 0.0, v, 0.0) for v in full)
        w = coarse["w"]
        wf = product(w, source)
        none = jnp.zeros((1, rows2, 128), f32)

        def total(e):
            result = jnp.concatenate([none, e[:-1]], axis=0) + jnp.concatenate([e[1:], none], axis=0)
            result = result + jnp.where(row2 > 0, roll(e, 1, 1), 0.0)
            result = result + jnp.where(row2 < rows2 - 1, roll(e, -1, 1), 0.0)
            return result + roll(e, 1, 2) + roll(e, -1, 2)

        def step(_, e):
            part = product(w, (total(e[0]), total(e[1])))
            return tuple(0.4 * a + b + 0.0625 * d for a, b, d in zip(e, wf, part))

        e = lax.fori_loop(0, NC - 1, step, wf)
        for c in range(2):
            for x in range(ngx):
                m["padded"][x + 2, c, 8 : 8 + rows2] = e[c][x]
        own = [m["padded"][gx + i, c, pl.ds(6 + 2 * gy, 8)] for i in range(5) for c in range(2)]
        wide = dot3(jnp.concatenate(own, axis=0), widen)
        result = []
        for i in range(5):
            pair = []
            for c in range(2):
                rows = [wide[16 * i + 8 * c + k : 16 * i + 8 * c + k + 1] for k in (2, 3, 4, 5, 0, 1)]
                tiles = [jnp.where(row8 < 4, rows[k], rows[k + 1]) for k in (0, 2, 4)]
                pair.append(jnp.concatenate(tiles, axis=0))
            result.append(tuple(pair))
        return result

    def cycle_part(cycle):
        b = m["cycles"][cycle]
        wf0, w0, upd0, upd0b = m["wf0"], m["w0"], m["upd0"], m["upd0b"]
        wf1, w1, upd1 = m["wf1"], m["w1"], m["upd1"]
        first_two(wf0, w0, upd0, range(1, 7), 1, 1.0)
        held = [residual(load(m["source0"], p), load(m["diag0"], p), upd0, p + 2, 1, 1.0) for p in range(4)]
        sources = [tuple(pair_mean(held[p][c] + held[p + 1][c]) for c in range(2)) for p in (0, 2)]
        scaled1 = [product(weights1[p], sources[p]) for p in range(2)]
        send_dense(b["source"], scaled1)
        start(f"source{cycle}")
        updates = [load(upd0, p + 2, 8) for p in range(4)]
        store(b["farown"], 0, updates[2])
        store(b["farown"], 1, updates[1])
        for i in range(2):
            b["up"][i] = pack2([*updates[2 * i], *updates[2 * i + 1]], True)
            b["down"][i] = pack2([*updates[2 * i], *updates[2 * i + 1]], False)
        put_corners(b["cs"], 0, updates[0], updates[3], 0)
        start(f"update{cycle}")
        if cycle == 0:
            receive("coef1")
            for p, pair in enumerate(get_dense(m["coef1"], weights1)):
                store(w1, p, pair)
        receive(f"source{cycle}")
        for p, pair in enumerate(get_dense(b["source"], scaled1)):
            store(wf1, p, pair)
        first_two(wf1, w1, upd1, range(1, 5), 2, 0.25)
        left, right = [residual(sources[p], load(m["diag1"], p), upd1, p + 2, 2, 0.25) for p in range(2)]
        coarsest(cycle, tuple(left[c] + right[c] for c in range(2)))
        updates1 = [load(upd1, p + 2, 8) for p in range(2)]
        b["fine"]["own"][...] = pack_dense(*updates1)
        start(f"fine{cycle}")

        def beside(own, faces, corners):
            def tile_of(rx, ry):
                step = (-rx, -ry)
                if step == (0, 0):
                    return own
                return unpack_dense(faces[FACES.index(step)] if step in FACES else corners[CORNERS.index(step)])

            return tile_of

        if cycle == 0:
            receive("later1")
            tile_of = beside(weights1, m["coef1"]["got"], m["ccoef1"])
            for p, pair in enumerate(wide_planes(tile_of, 1)):
                store(m["wide_w1"], p, pair)
        receive(f"update{cycle}", f"fine{cycle}")
        for p, pair in enumerate(wide_planes(beside(scaled1, b["source"]["got"], b["csource"]), 1)):
            store(m["wide_wf1"], p, pair)
        around1 = wide_planes(
            lambda rx, ry: unpack_dense(b["fine"]["got"][AROUND.index((-rx, -ry))]) if rx or ry else updates1, 2
        )
        wide1, wide1b = m["wide1"], m["wide1b"]
        for p in range(8):
            store(wide1, p, around1[p + 1])
        none = jnp.zeros((8, depth), f32)
        for c in range(2):
            upd0[0, c] = jnp.concatenate([b["far"][0, c], none], axis=0)
            upd0[7, c] = jnp.concatenate([b["far"][1, c], none], axis=0)
            upd0[1, c, 8:] = corner_tile(b["cr"], -1, c)
            upd0[6, c, 8:] = corner_tile(b["cr"], 1, c)
            for p in range(4):
                upd0[p + 2, c, 8:] = unpack2(b["low"][p // 2], b["high"][p // 2], 2 * (p % 2) + c)
        correction = coarsest_finish(cycle)
        for p in range(8):
            store(wide1, p, tuple(v + x for v, x in zip(load(wide1, p), correction[(p + 1) // 2])))
        for p, e in sweep(wide1, m["wide_wf1"], m["wide_w1"], range(1, 7), 2, 0.25, 1):
            store(wide1b, p, e)
        for p, e in sweep(wide1b, m["wide_wf1"], m["wide_w1"], range(2, 6), 2, 0.25, 1):
            solved = [jnp.concatenate([v[:8], jnp.where(row8 < 4, v[8:16], v[16:24])], axis=0) for v in e]
            for fine in (2 * p - 4, 2 * p - 3):
                store(upd0, fine, tuple(v + x for v, x in zip(load(upd0, fine), solved)))
        for p, e in sweep(upd0, wf0, w0, range(1, 7), 1, 1.0):
            store(upd0b, p, e)
        for p, e in sweep(upd0b, wf0, w0, range(2, 6), 1, 1.0):
            yield p - 2, own8(e)

    none = jnp.zeros((8, depth), f32)

    def halo0(p, j):
        if p in (1, 6):
            return corner_tile(m["cr"], -1 if p == 1 else 1, j)
        if p in (0, 7):
            return none
        return unpack2(m["low"][p - 2], m["high"][p - 2], j)

    receive("begin")
    for p in range(8):
        for c in range(2):
            m["wf0"][p, c] = jnp.concatenate([m["ewf"][p, c], halo0(p, c)], axis=0)
            if p in (0, 7):
                m["w0"][p, c, 8:] = none
            else:
                m["w0"][p, c] = jnp.concatenate([m["ew"][p, c], halo0(p, 2 + c)], axis=0)
    kept = []
    for p, e in cycle_part(0):
        store(m["first"], p + 3, e)
        m["fup"][p] = pack4(e, True)
        m["fdown"][p] = pack4(e, False)
        kept.append(e)
    put_corners(m["fcs"], 0, kept[0], kept[3], 0)
    put_corners(m["fcs"], 2, kept[0], kept[3], 1)
    put_corners(m["fcs"], 4, kept[1], kept[2], 0)
    start("first")
    receive("first", "later")
    for p in (0, 7):
        for c in range(2):
            m["w0"][p, c, :8] = m["ew"][p, c]
    for p in range(10):
        if 3 <= p < 7:
            halo = unpack4(m["flow"][p - 3], m["fhigh"][p - 3])
        elif p in (2, 7):
            side, halo = (-1 if p == 2 else 1), []
            for c in range(2):
                below, above = got_corner(m["fcr"], side, c)
                below2, above2 = got_corner(m["fcr"], side, 2 + c)
                tile = jnp.where(row8 == 7, below, jnp.where(row8 == 6, below2, 0.0))
                halo.append(jnp.where(row8 == 0, above, jnp.where(row8 == 1, above2, tile)))
        elif p in (1, 8):
            halo = [corner_tile(m["fcr"], -1 if p == 1 else 1, 4 + c) for c in range(2)]
        else:
            halo = [none, none]
        for c in range(2):
            m["first16"][p, c] = jnp.concatenate([m["first"][p, c], halo[c]], axis=0)
    for p in range(8):
        ns = neighbours(m["first16"], p + 1, 1)
        e = load(m["first16"], p + 1)
        if 2 <= p < 6:
            part = product(load(m["diag0"], p - 2), own8(e))
            source = load(m["source0"], p - 2)
            store(m["source0"], p - 2, tuple(f + n[:8] - q for f, n, q in zip(source, ns, part)))
        part = product(load(m["w0"], p), ns)
        store(m["wf0"], p, tuple(a + b - OMEGA * v for a, b, v in zip(load(m["wf0"], p), part, e)))
    for p, e in cycle_part(1):
        for c in range(2):
            out[c, p] = m["first"][p + 3, c] + e[c]

    for step in steps:
        @pl.when(exists(*step))
        def _(step=step):
            for entry in plan:
                if entry[1] == step:
                    remote(entry).wait_send()
    for cycle in range(2):
        every = m["cycles"][cycle]["tiles"].at[pl.ds(0, count - 1)]
        pltpu.make_async_copy(every, every, m["tile_send"].at[cycle]).wait()


def local(ngx, ngy, right_side, velocity_table, layer_index, absorb_level):
    depth = right_side.shape[-1]
    scratch = scratch_of(ngx, ngy, velocity_table.shape[0], depth)
    leaves, tree = jax.tree.flatten(scratch)
    anywhere = pl.BlockSpec(memory_space=pltpu.HBM)
    return pl.pallas_call(
        functools.partial(kernel, ngx, ngy, depth, tree),
        out_shape=jax.ShapeDtypeStruct(right_side.shape, jnp.float32),
        in_specs=[anywhere] * 4,
        out_specs=pl.BlockSpec(memory_space=pltpu.VMEM),
        scratch_shapes=leaves,
        compiler_params=pltpu.CompilerParams(
            collective_id=0, has_side_effects=True, vmem_limit_bytes=64 * 1024 * 1024 - 65536
        ),
    )(right_side, velocity_table, layer_index, absorb_level)


def solution(mesh):
    placed = (P(None, "gx", "gy", None), P(), P("gx", "gy", None), P("gx", "gy", None))
    return jax.shard_map(
        functools.partial(local, mesh.shape["gx"], mesh.shape["gy"]),
        mesh=mesh, in_specs=placed, out_specs=P(None, "gx", "gy", None), check_vma=False,
    )
```

```python
import functools
import math

import jax
import jax.numpy as jnp
from jax import lax
from jax.experimental import pallas as pl
from jax.experimental.pallas import tpu as pltpu
from jax.sharding import PartitionSpec as P

NC = 8
OMEGA = 0.6
BETA = 0.5
ABSORB = 0.25
KH_FACTOR = 2.0 * math.pi * 6.0 * 20.0
MESH = pl.DeviceIdType.MESH

AROUND = [(dx, dy) for dx in range(-2, 3) for dy in (-1, 0, 1) if dx or dy]
FACES = [(1, 0), (-1, 0), (0, 1), (0, -1)]
CORNERS = [(1, 1), (1, -1), (-1, 1), (-1, -1)]


def product(a, b):
    return a[0] * b[0] - a[1] * b[1], a[0] * b[1] + a[1] * b[0]


def dot3(a, b):
    rows = a.shape[0]
    pieces, rest = [], a
    for _ in range(3):
        piece = rest.astype(jnp.bfloat16).astype(jnp.float32)
        pieces.append(piece)
        rest = rest - piece
    stacked = jnp.concatenate(pieces, axis=0).astype(jnp.bfloat16)
    result = jnp.dot(stacked, b, preferred_element_type=jnp.float32)
    return result[:rows] + result[rows : 2 * rows] + result[2 * rows :]


def iota(shape, dim):
    return lax.broadcasted_iota(jnp.int32, shape, dim)


def scratch_of(ngx, ngy, layers, depth):
    f32 = jnp.float32

    def vmem(*shape):
        return pltpu.VMEM(shape, f32)

    def dense():
        return dict(own=vmem(8, depth), got=vmem(4, 8, depth), cs=vmem(4, 2, 1, depth), cr=vmem(4, 2, 1, depth))

    cycles = [
        dict(
            source=dense(), fine=dict(own=vmem(8, depth), got=vmem(len(AROUND), 8, depth)), csource=vmem(4, 8, depth),
            far=vmem(2, 2, 8, depth), farown=vmem(2, 2, 8, depth),
            up=vmem(2, 8, depth), down=vmem(2, 8, depth), low=vmem(2, 8, depth), high=vmem(2, 8, depth),
            cs=vmem(4, 2, 1, depth), cr=vmem(4, 2, 1, depth), tiles=vmem(ngx * ngy, 8, 128),
        )
        for _ in range(2)
    ]
    return dict(
        rhs=vmem(2, 4, 8, depth), layer=pltpu.VMEM((4, 8, depth), jnp.int32),
        absorb=pltpu.VMEM((4, 8, depth), jnp.int32), table=pltpu.SMEM((layers,), f32),
        ewf=vmem(8, 2, 8, depth), ew=vmem(8, 2, 8, depth),
        up=vmem(4, 8, depth), down=vmem(4, 8, depth), low=vmem(4, 8, depth), high=vmem(4, 8, depth),
        cs=vmem(4, 4, 1, depth), cr=vmem(4, 4, 1, depth),
        coef1=dict(own=vmem(8, depth), got=vmem(4, 8, depth)), ccoef1=vmem(4, 8, depth),
        first=vmem(10, 2, 8, depth),
        fup=vmem(4, 8, depth), fdown=vmem(4, 8, depth), flow=vmem(4, 8, depth), fhigh=vmem(4, 8, depth),
        fcs=vmem(4, 6, 1, depth), fcr=vmem(4, 6, 1, depth),
        cycles=cycles,
        diag0=vmem(4, 2, 8, depth), source0=vmem(4, 2, 8, depth),
        wf0=vmem(8, 2, 16, depth), w0=vmem(8, 2, 16, depth), upd0=vmem(8, 2, 16, depth), upd0b=vmem(8, 2, 16, depth),
        first16=vmem(10, 2, 16, depth),
        diag1=vmem(2, 2, 8, depth), source1=vmem(2, 2, 8, depth),
        wf1=vmem(6, 2, 16, depth), w1=vmem(6, 2, 16, depth), upd1=vmem(6, 2, 16, depth),
        wide_wf1=vmem(6, 2, 24, depth), wide_w1=vmem(6, 2, 24, depth),
        wide1=vmem(8, 2, 24, depth), wide1b=vmem(8, 2, 24, depth),
        padded=vmem(ngx + 4, 2, 2 * ngy + 16, 128),
        send_sem=pltpu.SemaphoreType.DMA((112,)), recv_sem=pltpu.SemaphoreType.DMA((112,)),
        tile_send=pltpu.SemaphoreType.DMA((2,)), tile_recv=pltpu.SemaphoreType.DMA((2,)),
        load_sem=pltpu.SemaphoreType.DMA((4,)),
    )


def kernel(ngx, ngy, depth, tree, rhs_in, table_in, layer_in, absorb_in, out, *scratch):
    m = jax.tree.unflatten(tree, scratch)
    count = ngx * ngy
    gx, gy = lax.axis_index("gx"), lax.axis_index("gy")
    me = gx * ngy + gy
    f32 = jnp.float32

    loads = [
        pltpu.make_async_copy(a, m[b], m["load_sem"].at[i])
        for i, (a, b) in enumerate(((layer_in, "layer"), (absorb_in, "absorb"), (table_in, "table"), (rhs_in, "rhs")))
    ]
    for load_copy in loads:
        load_copy.start()

    barrier = pltpu.get_barrier_semaphore()

    def others(act):
        if count > 64:
            def one(k, carry):
                other = lax.rem(me + k, count)
                act(other // ngy, lax.rem(other, ngy))
                return carry

            lax.fori_loop(1, count, one, 0)
            return
        for i in reversed(range(ngx)):
            for j in reversed(range(ngy)):
                if i or j:
                    x, y = gx + i, gy + j
                    act(jnp.where(x >= ngx, x - ngx, x), jnp.where(y >= ngy, y - ngy, y))

    others(lambda x, y: pl.semaphore_signal(barrier, inc=1, device_id=(x, y), device_id_type=MESH))

    def exists(dx, dy):
        checks = []
        if dx:
            checks.append(gx < ngx - dx if dx > 0 else gx >= -dx)
        if dy:
            checks.append(gy < ngy - 1 if dy > 0 else gy > 0)
        return functools.reduce(jnp.logical_and, checks)

    plan = []

    def add(name, step, src, dst):
        plan.append((name, step, src, dst, len(plan)))

    def cut(ref, first, size=1):
        return ref.at[pl.ds(first, size)]

    def add_packets(name, up, down, low, high):
        add(name, (0, 1), up, low)
        add(name, (0, -1), down, high)

    def add_corners(name, cs, cr):
        for i, step in enumerate(CORNERS):
            add(name, step, cs.at[i], cr.at[i])

    def add_dense(name, b):
        for i, step in enumerate(FACES):
            add(name, step, b["own"], b["got"].at[i])
        if "cs" in b:
            add_corners(name, b["cs"], b["cr"])

    add("begin", (1, 0), cut(m["ewf"], 4, 2), cut(m["ewf"], 0, 2))
    add("begin", (-1, 0), cut(m["ewf"], 2, 2), cut(m["ewf"], 6, 2))
    add("begin", (1, 0), cut(m["ew"], 5), cut(m["ew"], 1))
    add("begin", (-1, 0), cut(m["ew"], 2), cut(m["ew"], 6))
    add_packets("begin", m["up"], m["down"], m["low"], m["high"])
    add_corners("begin", m["cs"], m["cr"])
    add_dense("coef1", m["coef1"])
    for i, step in enumerate(CORNERS):
        add("later1", step, m["coef1"]["own"], m["ccoef1"].at[i])
    add("later", (1, 0), cut(m["ew"], 4), cut(m["ew"], 0))
    add("later", (-1, 0), cut(m["ew"], 3), cut(m["ew"], 7))
    for cycle in range(2):
        b = m["cycles"][cycle]
        add_dense(f"source{cycle}", b["source"])
        add(f"update{cycle}", (1, 0), cut(b["farown"], 0), cut(b["far"], 0))
        add(f"update{cycle}", (-1, 0), cut(b["farown"], 1), cut(b["far"], 1))
        add_packets(f"update{cycle}", b["up"], b["down"], b["low"], b["high"])
        add_corners(f"update{cycle}", b["cs"], b["cr"])
        for i, step in enumerate(AROUND):
            add(f"fine{cycle}", step, b["fine"]["own"], b["fine"]["got"].at[i])
        for i, step in enumerate(CORNERS):
            add(f"update{cycle}", step, b["source"]["own"], b["csource"].at[i])
    add("first", (1, 0), cut(m["first"], 4, 3), cut(m["first"], 0, 3))
    add("first", (-1, 0), cut(m["first"], 3, 3), cut(m["first"], 7, 3))
    add_packets("first", m["fup"], m["fdown"], m["flow"], m["fhigh"])
    add_corners("first", m["fcs"], m["fcr"])
    steps = sorted({entry[1] for entry in plan})

    for step in steps:
        @pl.when(jnp.logical_not(exists(-step[0], -step[1])))
        def _(step=step):
            for _, other, _, dst, _ in plan:
                if other == step:
                    dst[...] = jnp.zeros(dst.shape, f32)

    def remote(entry):
        _, (dx, dy), src, dst, i = entry
        return pltpu.make_async_remote_copy(
            src_ref=src, dst_ref=dst, send_sem=m["send_sem"].at[i], recv_sem=m["recv_sem"].at[i],
            device_id=(gx + dx, gy + dy), device_id_type=MESH,
        )

    def each(names, sign, act):
        for step in steps:
            mine = [entry for entry in plan if entry[0] in names and entry[1] == step]
            if mine:
                @pl.when(exists(sign * step[0], sign * step[1]))
                def _(mine=mine):
                    for entry in mine:
                        act(remote(entry))

    def start(*names):
        each(names, 1, lambda copy: copy.start())

    def receive(*names):
        each(names, -1, lambda copy: copy.wait_recv())

    def wait_sends(which):
        each({entry[0] for entry in plan if which(entry[0])}, 1, lambda copy: copy.wait_send())

    row8, lane8 = iota((8, depth), 0), iota((8, depth), 1)
    even_row, even_lane = row8 % 2 == 0, lane8 % 2 == 0

    def roll(value, shift, dim):
        size = value.shape[dim]
        return pltpu.roll(value, shift % size, dim) if shift % size else value

    def pack2(values, top):
        result = None
        for c, v in enumerate(values):
            v = roll(v, 2 * c + 2 if top else 2 * c, 0)
            result = v if c == 0 else jnp.where(row8 >= 2 * c, v, result)
        return result

    def unpack2(low, high, c):
        return jnp.where(row8 < 4, roll(high, -2 * c, 0), roll(low, 6 - 2 * c, 0))

    def pack4(pair, top):
        re, im = pair
        return jnp.where(row8 < 4, roll(re, 4, 0), im) if top else jnp.where(row8 < 4, re, roll(im, 4, 0))

    def unpack4(low, high):
        return jnp.where(row8 < 4, high, roll(low, 4, 0)), jnp.where(row8 < 4, roll(high, 4, 0), low)

    def put_corners(cs, j, near_low, near_high, from_edge):
        for i, (dx, dy) in enumerate(CORNERS):
            pair = near_high if dx > 0 else near_low
            at = 7 - from_edge if dy > 0 else from_edge
            for c, v in enumerate(pair):
                cs[i, j + c] = v[at : at + 1]

    def got_corner(cr, side, j):
        i = CORNERS.index((-side, 1))
        return cr[i, j], cr[i + 1, j]

    def corner_tile(cr, side, j, thick=1):
        below, above = got_corner(cr, side, j)
        return jnp.where(row8 >= 8 - thick, below, jnp.where(row8 < thick, above, 0.0))

    def pack_dense(first, second):
        return jnp.where(
            even_lane, jnp.where(even_row, first[0], first[1]), jnp.where(even_row, second[0], second[1])
        )

    def unpack_dense(tile):
        re = jnp.where(even_row, tile, roll(tile, 1, 0))
        im = jnp.where(even_row, roll(tile, -1, 0), tile)
        first = tuple(jnp.where(even_lane, v, roll(v, 1, 1)) for v in (re, im))
        second = tuple(jnp.where(even_lane, roll(v, -1, 1), v) for v in (re, im))
        return first, second

    def send_dense(b, planes):
        b["own"][...] = pack_dense(*planes)
        if "cs" in b:
            put_corners(b["cs"], 0, planes[0], planes[1], 0)

    def get_dense(b, own):
        before, after, below, above = [unpack_dense(b["got"][i]) for i in range(4)]
        none = jnp.zeros((8, depth), f32)
        result = []
        for p, plane in enumerate([*before, *own, *after]):
            pair = []
            for c in range(2):
                if p in (2, 3):
                    halo = jnp.where(row8 < 4, above[p - 2][c], below[p - 2][c])
                elif p in (1, 4) and "cr" in b:
                    halo = corner_tile(b["cr"], -1 if p == 1 else 1, c, 2)
                else:
                    halo = none
                pair.append(jnp.concatenate([plane[c], halo], axis=0))
            result.append(tuple(pair))
        return result

    def around(before, mid, after, s):
        total = before + after + roll(mid, s, 0) + roll(mid, -s, 0)
        lane = iota(mid.shape, 1)
        total = total + jnp.where(lane >= s, roll(mid, s, 1), 0.0)
        return total + jnp.where(lane < depth - s, roll(mid, -s, 1), 0.0)

    def load(ref, plane, rows=None):
        return tuple(ref[plane, c] if rows is None else ref[plane, c, :rows] for c in range(2))

    def store(ref, plane, pair):
        ref[plane, 0], ref[plane, 1] = pair

    def neighbours(ref, plane, s):
        return tuple(around(ref[plane - 1, c], ref[plane, c], ref[plane + 1, c], s) for c in range(2))

    def weight(diag):
        scale = OMEGA / (diag[0] * diag[0] + diag[1] * diag[1])
        return diag[0] * scale, -diag[1] * scale

    def first_two(wf_ref, w_ref, target, planes, s, c):
        for p in planes:
            part = product(load(w_ref, p), neighbours(wf_ref, p, s))
            store(target, p, tuple(1.4 * a + c * b for a, b in zip(load(wf_ref, p), part)))

    def sweep(ref, wf_ref, w_ref, planes, s, c, behind=0):
        for p in planes:
            part = product(load(w_ref, p - behind), neighbours(ref, p, s))
            wf = load(wf_ref, p - behind)
            yield p, tuple(0.4 * a + b + c * d for a, b, d in zip(load(ref, p), wf, part))

    def wide_planes(tile_of, reach):
        result = []
        for rx in range(-reach, reach + 1):
            blocks = [tile_of(rx, ry) for ry in (0, 1, -1)]
            for half in range(2):
                result.append(tuple(jnp.concatenate([v[half][c] for v in blocks], axis=0) for c in range(2)))
        return result

    def residual(source, diag, ref, p, s, c):
        ns, part = neighbours(ref, p, s), product(diag, load(ref, p, 8))
        return tuple(f + c * n[:8] - q for f, n, q in zip(source, ns, part))

    def pair_mean(value):
        value = value + jnp.where(even_row, roll(value, -1, 0), roll(value, 1, 0))
        other = jnp.where(even_lane, roll(value, -1, 1), roll(value, 1, 1))
        return (value + other) * 0.125

    def own8(pair):
        return tuple(v[:8] for v in pair)

    for load_copy in loads:
        load_copy.wait()
    shifts, weights, scaled = [], [], []
    for p in range(4):
        index = m["layer"][p]
        velocity = jnp.zeros((8, depth), f32)
        for number in range(m["table"].shape[0]):
            velocity = jnp.where(index == number, m["table"][number], velocity)
        ratio = KH_FACTOR / velocity
        kh2 = ratio * ratio
        shift = (kh2, -kh2 * (BETA + ABSORB * m["absorb"][p].astype(f32)))
        diag = (6.0 - shift[0], -shift[1])
        source = (m["rhs"][0, p], m["rhs"][1, p])
        w = weight(diag)
        wf = product(w, source)
        store(m["diag0"], p, diag)
        store(m["source0"], p, source)
        store(m["ewf"], p + 2, wf)
        store(m["ew"], p + 2, w)
        m["up"][p] = pack2([*wf, *w], True)
        m["down"][p] = pack2([*wf, *w], False)
        shifts.append(shift)
        weights.append(w)
        scaled.append(wf)
    put_corners(m["cs"], 0, scaled[0], scaled[3], 0)
    put_corners(m["cs"], 2, weights[0], weights[3], 0)
    pl.semaphore_wait(barrier, count - 1)
    start("begin")
    shifts1 = [tuple(pair_mean(shifts[p][c] + shifts[p + 1][c]) for c in range(2)) for p in (0, 2)]
    diags1 = [(1.5 - s[0], -s[1]) for s in shifts1]
    weights1 = [weight(d) for d in diags1]
    send_dense(m["coef1"], weights1)
    start("coef1", "later", "later1")
    for p in range(2):
        store(m["diag1"], p, diags1[p])

    spread = 0.25 * (iota((depth, 128), 0) // 4 == iota((depth, 128), 1)).astype(f32)
    spread = spread.astype(jnp.bfloat16)
    widen = (iota((128, depth), 1) // 4 == iota((128, depth), 0)).astype(f32).astype(jnp.bfloat16)
    rows2 = 2 * ngy
    shift2_sum = tuple(shifts1[0][c] + shifts1[1][c] for c in range(2))
    m["padded"][...] = jnp.zeros(m["padded"].shape, f32)
    row2 = iota((ngx, rows2, 128), 1)
    block8 = iota((8, 128), 0) // 2

    def unpack(buffer, comp):
        planes = []
        for x in range(ngx):
            groups = []
            for q in range(0, ngy, 4):
                value = buffer[x * ngy + q]
                for j in range(1, min(4, ngy - q)):
                    value = jnp.where(block8 == (comp + j) % 4, buffer[x * ngy + q + j], value)
                groups.append(roll(value, -2 * comp, 0))
            planes.append(jnp.concatenate(groups, axis=0)[:rows2] if len(groups) > 1 else groups[0][:rows2])
        return jnp.stack(planes)

    coarse = {}

    def coarsest(cycle, sums):
        buffer = m["cycles"][cycle]["tiles"]
        tile = jnp.zeros((8, depth), f32)
        for c, v in enumerate(list(sums) + (list(shift2_sum) if cycle == 0 else [])):
            v = v + jnp.where(row8 // 2 % 2 == 0, roll(v, -2, 0), roll(v, 2, 0))
            tile = jnp.where(row8 // 2 == c, roll(v, 2 * c - 3, 0), tile)
        tile = dot3(tile * 0.25, spread)
        buffer[me] = pltpu.roll(tile, 2 * lax.rem(gy, 4), 0)

        others(
            lambda x, y: pltpu.make_async_remote_copy(
                src_ref=buffer.at[me], dst_ref=buffer.at[me],
                send_sem=m["tile_send"].at[cycle], recv_sem=m["tile_recv"].at[cycle],
                device_id=(x, y), device_id_type=MESH,
            ).start()
        )

    def coarsest_finish(cycle):
        buffer = m["cycles"][cycle]["tiles"]
        every = buffer.at[pl.ds(0, count - 1)]
        pltpu.make_async_copy(every, every, m["tile_recv"].at[cycle]).wait()
        source = unpack(buffer, 0), unpack(buffer, 1)
        if cycle == 0:
            shift = unpack(buffer, 2), unpack(buffer, 3)
            full = weight((0.375 - shift[0], -shift[1]))
            coarse["w"] = tuple(jnp.where(shift[0] > 0.0, v, 0.0) for v in full)
        w = coarse["w"]
        wf = product(w, source)
        none = jnp.zeros((1, rows2, 128), f32)

        def total(e):
            result = jnp.concatenate([none, e[:-1]], axis=0) + jnp.concatenate([e[1:], none], axis=0)
            result = result + jnp.where(row2 > 0, roll(e, 1, 1), 0.0)
            result = result + jnp.where(row2 < rows2 - 1, roll(e, -1, 1), 0.0)
            return result + roll(e, 1, 2) + roll(e, -1, 2)

        def step(_, e):
            part = product(w, (total(e[0]), total(e[1])))
            return tuple(0.4 * a + b + 0.0625 * d for a, b, d in zip(e, wf, part))

        e = lax.fori_loop(0, NC - 1, step, wf)
        for c in range(2):
            for x in range(ngx):
                m["padded"][x + 2, c, 8 : 8 + rows2] = e[c][x]
        own = [m["padded"][gx + i, c, pl.ds(6 + 2 * gy, 8)] for i in range(5) for c in range(2)]
        wide = dot3(jnp.concatenate(own, axis=0), widen)
        result = []
        for i in range(5):
            pair = []
            for c in range(2):
                rows = [wide[16 * i + 8 * c + k : 16 * i + 8 * c + k + 1] for k in (2, 3, 4, 5, 0, 1)]
                tiles = [jnp.where(row8 < 4, rows[k], rows[k + 1]) for k in (0, 2, 4)]
                pair.append(jnp.concatenate(tiles, axis=0))
            result.append(tuple(pair))
        return result

    def cycle_part(cycle):
        b = m["cycles"][cycle]
        wf0, w0, upd0, upd0b = m["wf0"], m["w0"], m["upd0"], m["upd0b"]
        wf1, w1, upd1 = m["wf1"], m["w1"], m["upd1"]
        first_two(wf0, w0, upd0, range(1, 7), 1, 1.0)
        held = [residual(load(m["source0"], p), load(m["diag0"], p), upd0, p + 2, 1, 1.0) for p in range(4)]
        sources = [tuple(pair_mean(held[p][c] + held[p + 1][c]) for c in range(2)) for p in (0, 2)]
        scaled1 = [product(weights1[p], sources[p]) for p in range(2)]
        send_dense(b["source"], scaled1)
        start(f"source{cycle}")
        updates = [load(upd0, p + 2, 8) for p in range(4)]
        store(b["farown"], 0, updates[2])
        store(b["farown"], 1, updates[1])
        for i in range(2):
            b["up"][i] = pack2([*updates[2 * i], *updates[2 * i + 1]], True)
            b["down"][i] = pack2([*updates[2 * i], *updates[2 * i + 1]], False)
        put_corners(b["cs"], 0, updates[0], updates[3], 0)
        start(f"update{cycle}")
        if cycle == 0:
            receive("coef1")
            for p, pair in enumerate(get_dense(m["coef1"], weights1)):
                store(w1, p, pair)
        receive(f"source{cycle}")
        for p, pair in enumerate(get_dense(b["source"], scaled1)):
            store(wf1, p, pair)
        first_two(wf1, w1, upd1, range(1, 5), 2, 0.25)
        left, right = [residual(sources[p], load(m["diag1"], p), upd1, p + 2, 2, 0.25) for p in range(2)]
        coarsest(cycle, tuple(left[c] + right[c] for c in range(2)))
        updates1 = [load(upd1, p + 2, 8) for p in range(2)]
        b["fine"]["own"][...] = pack_dense(*updates1)
        start(f"fine{cycle}")

        def beside(own, faces, corners):
            def tile_of(rx, ry):
                step = (-rx, -ry)
                if step == (0, 0):
                    return own
                return unpack_dense(faces[FACES.index(step)] if step in FACES else corners[CORNERS.index(step)])

            return tile_of

        if cycle == 0:
            receive("later1")
            tile_of = beside(weights1, m["coef1"]["got"], m["ccoef1"])
            for p, pair in enumerate(wide_planes(tile_of, 1)):
                store(m["wide_w1"], p, pair)
        receive(f"update{cycle}")
        none = jnp.zeros((8, depth), f32)
        for c in range(2):
            upd0[0, c] = jnp.concatenate([b["far"][0, c], none], axis=0)
            upd0[7, c] = jnp.concatenate([b["far"][1, c], none], axis=0)
            upd0[1, c, 8:] = corner_tile(b["cr"], -1, c)
            upd0[6, c, 8:] = corner_tile(b["cr"], 1, c)
            for p in range(4):
                upd0[p + 2, c, 8:] = unpack2(b["low"][p // 2], b["high"][p // 2], 2 * (p % 2) + c)
        for p, pair in enumerate(wide_planes(beside(scaled1, b["source"]["got"], b["csource"]), 1)):
            store(m["wide_wf1"], p, pair)
        wait_sends(lambda name: cycle == 1 and not name.startswith("fine1"))
        correction = coarsest_finish(cycle)
        receive(f"fine{cycle}")
        around1 = wide_planes(
            lambda rx, ry: unpack_dense(b["fine"]["got"][AROUND.index((-rx, -ry))]) if rx or ry else updates1, 2
        )
        wide1, wide1b = m["wide1"], m["wide1b"]
        for p in range(8):
            store(wide1, p, tuple(v + x for v, x in zip(around1[p + 1], correction[(p + 1) // 2])))
        for p, e in sweep(wide1, m["wide_wf1"], m["wide_w1"], range(1, 7), 2, 0.25, 1):
            store(wide1b, p, e)
        for p, e in sweep(wide1b, m["wide_wf1"], m["wide_w1"], range(2, 6), 2, 0.25, 1):
            solved = [jnp.concatenate([v[:8], jnp.where(row8 < 4, v[8:16], v[16:24])], axis=0) for v in e]
            for fine in (2 * p - 4, 2 * p - 3):
                store(upd0, fine, tuple(v + x for v, x in zip(load(upd0, fine), solved)))
        for p, e in sweep(upd0, wf0, w0, range(1, 7), 1, 1.0):
            store(upd0b, p, e)
        for p, e in sweep(upd0b, wf0, w0, range(2, 6), 1, 1.0):
            yield p - 2, own8(e)

    none = jnp.zeros((8, depth), f32)

    def halo0(p, j):
        if p in (1, 6):
            return corner_tile(m["cr"], -1 if p == 1 else 1, j)
        if p in (0, 7):
            return none
        return unpack2(m["low"][p - 2], m["high"][p - 2], j)

    receive("begin")
    for p in range(8):
        for c in range(2):
            m["wf0"][p, c] = jnp.concatenate([m["ewf"][p, c], halo0(p, c)], axis=0)
            if p in (0, 7):
                m["w0"][p, c, 8:] = none
            else:
                m["w0"][p, c] = jnp.concatenate([m["ew"][p, c], halo0(p, 2 + c)], axis=0)
    kept = []
    for p, e in cycle_part(0):
        store(m["first"], p + 3, e)
        m["fup"][p] = pack4(e, True)
        m["fdown"][p] = pack4(e, False)
        kept.append(e)
    put_corners(m["fcs"], 0, kept[0], kept[3], 0)
    put_corners(m["fcs"], 2, kept[0], kept[3], 1)
    put_corners(m["fcs"], 4, kept[1], kept[2], 0)
    start("first")
    receive("first", "later")
    for p in (0, 7):
        for c in range(2):
            m["w0"][p, c, :8] = m["ew"][p, c]
    for p in range(10):
        if 3 <= p < 7:
            halo = unpack4(m["flow"][p - 3], m["fhigh"][p - 3])
        elif p in (2, 7):
            side, halo = (-1 if p == 2 else 1), []
            for c in range(2):
                below, above = got_corner(m["fcr"], side, c)
                below2, above2 = got_corner(m["fcr"], side, 2 + c)
                tile = jnp.where(row8 == 7, below, jnp.where(row8 == 6, below2, 0.0))
                halo.append(jnp.where(row8 == 0, above, jnp.where(row8 == 1, above2, tile)))
        elif p in (1, 8):
            halo = [corner_tile(m["fcr"], -1 if p == 1 else 1, 4 + c) for c in range(2)]
        else:
            halo = [none, none]
        for c in range(2):
            m["first16"][p, c] = jnp.concatenate([m["first"][p, c], halo[c]], axis=0)
    for p in range(8):
        ns = neighbours(m["first16"], p + 1, 1)
        e = load(m["first16"], p + 1)
        if 2 <= p < 6:
            part = product(load(m["diag0"], p - 2), own8(e))
            source = load(m["source0"], p - 2)
            store(m["source0"], p - 2, tuple(f + n[:8] - q for f, n, q in zip(source, ns, part)))
        part = product(load(m["w0"], p), ns)
        store(m["wf0"], p, tuple(a + b - OMEGA * v for a, b, v in zip(load(m["wf0"], p), part, e)))
    for p, e in cycle_part(1):
        for c in range(2):
            out[c, p] = m["first"][p + 3, c] + e[c]

    wait_sends(lambda name: name.startswith("fine1"))
    for cycle in range(2):
        every = m["cycles"][cycle]["tiles"].at[pl.ds(0, count - 1)]
        pltpu.make_async_copy(every, every, m["tile_send"].at[cycle]).wait()


def local(ngx, ngy, right_side, velocity_table, layer_index, absorb_level):
    depth = right_side.shape[-1]
    scratch = scratch_of(ngx, ngy, velocity_table.shape[0], depth)
    leaves, tree = jax.tree.flatten(scratch)
    anywhere = pl.BlockSpec(memory_space=pltpu.HBM)
    return pl.pallas_call(
        functools.partial(kernel, ngx, ngy, depth, tree),
        out_shape=jax.ShapeDtypeStruct(right_side.shape, jnp.float32),
        in_specs=[anywhere] * 4,
        out_specs=pl.BlockSpec(memory_space=pltpu.VMEM),
        scratch_shapes=leaves,
        compiler_params=pltpu.CompilerParams(
            collective_id=0, has_side_effects=True, vmem_limit_bytes=64 * 1024 * 1024 - 65536
        ),
    )(right_side, velocity_table, layer_index, absorb_level)


def solution(mesh):
    placed = (P(None, "gx", "gy", None), P(), P("gx", "gy", None), P("gx", "gy", None))
    return jax.shard_map(
        functools.partial(local, mesh.shape["gx"], mesh.shape["gy"]),
        mesh=mesh, in_specs=placed, out_specs=P(None, "gx", "gy", None), check_vma=False,
    )
```

```python
import functools
import math

import jax
import jax.numpy as jnp
from jax import lax
from jax.experimental import pallas as pl
from jax.experimental.pallas import tpu as pltpu
from jax.sharding import PartitionSpec as P

NC = 8
OMEGA = 0.6
BETA = 0.5
ABSORB = 0.25
KH_FACTOR = 2.0 * math.pi * 6.0 * 20.0
MESH = pl.DeviceIdType.MESH

AROUND = [(dx, dy) for dx in range(-2, 3) for dy in (-1, 0, 1) if dx or dy]
FACES = [(1, 0), (-1, 0), (0, 1), (0, -1)]
CORNERS = [(1, 1), (1, -1), (-1, 1), (-1, -1)]


def product(a, b):
    return a[0] * b[0] - a[1] * b[1], a[0] * b[1] + a[1] * b[0]


def dot3(a, b):
    rows = a.shape[0]
    pieces, rest = [], a
    for _ in range(3):
        piece = rest.astype(jnp.bfloat16).astype(jnp.float32)
        pieces.append(piece)
        rest = rest - piece
    stacked = jnp.concatenate(pieces, axis=0).astype(jnp.bfloat16)
    result = jnp.dot(stacked, b, preferred_element_type=jnp.float32)
    return result[:rows] + result[rows : 2 * rows] + result[2 * rows :]


def iota(shape, dim):
    return lax.broadcasted_iota(jnp.int32, shape, dim)


def scratch_of(ngx, ngy, layers, depth):
    f32 = jnp.float32

    def vmem(*shape):
        return pltpu.VMEM(shape, f32)

    def dense():
        return dict(own=vmem(8, depth), got=vmem(4, 8, depth), cs=vmem(4, 2, 1, depth), cr=vmem(4, 2, 1, depth))

    cycles = [
        dict(
            source=dense(), fine=dict(own=vmem(8, depth), got=vmem(len(AROUND), 8, depth)), csource=vmem(4, 8, depth),
            far=vmem(2, 2, 8, depth), farown=vmem(2, 2, 8, depth),
            up=vmem(2, 8, depth), down=vmem(2, 8, depth), low=vmem(2, 8, depth), high=vmem(2, 8, depth),
            cs=vmem(4, 2, 1, depth), cr=vmem(4, 2, 1, depth), tiles=vmem(ngx * ngy, 8, 128),
        )
        for _ in range(2)
    ]
    return dict(
        rhs=vmem(2, 4, 8, depth), layer=pltpu.VMEM((4, 8, depth), jnp.int32),
        absorb=pltpu.VMEM((4, 8, depth), jnp.int32), table=pltpu.SMEM((layers,), f32),
        ewf=vmem(8, 2, 8, depth), ew=vmem(8, 2, 8, depth),
        up=vmem(4, 8, depth), down=vmem(4, 8, depth), low=vmem(4, 8, depth), high=vmem(4, 8, depth),
        cs=vmem(4, 4, 1, depth), cr=vmem(4, 4, 1, depth),
        coef1=dict(own=vmem(8, depth), got=vmem(4, 8, depth)), ccoef1=vmem(4, 8, depth),
        first=vmem(10, 2, 8, depth),
        fup=vmem(4, 8, depth), fdown=vmem(4, 8, depth), flow=vmem(4, 8, depth), fhigh=vmem(4, 8, depth),
        fcs=vmem(4, 6, 1, depth), fcr=vmem(4, 6, 1, depth),
        cycles=cycles,
        diag0=vmem(4, 2, 8, depth), source0=vmem(4, 2, 8, depth),
        wf0=vmem(8, 2, 16, depth), w0=vmem(8, 2, 16, depth), upd0=vmem(8, 2, 16, depth), upd0b=vmem(8, 2, 16, depth),
        first16=vmem(10, 2, 16, depth),
        diag1=vmem(2, 2, 8, depth), source1=vmem(2, 2, 8, depth),
        wf1=vmem(6, 2, 16, depth), w1=vmem(6, 2, 16, depth), upd1=vmem(6, 2, 16, depth),
        wide_wf1=vmem(6, 2, 24, depth), wide_w1=vmem(6, 2, 24, depth),
        wide1=vmem(8, 2, 24, depth), wide1b=vmem(8, 2, 24, depth),
        padded=vmem(ngx + 4, 2, 2 * ngy + 16, 128),
        send_sem=pltpu.SemaphoreType.DMA((112,)), recv_sem=pltpu.SemaphoreType.DMA((112,)),
        tile_send=pltpu.SemaphoreType.DMA((2,)), tile_recv=pltpu.SemaphoreType.DMA((2,)),
        load_sem=pltpu.SemaphoreType.DMA((4,)),
    )


def kernel(ngx, ngy, depth, tree, rhs_in, table_in, layer_in, absorb_in, out, *scratch):
    m = jax.tree.unflatten(tree, scratch)
    count = ngx * ngy
    gx, gy = lax.axis_index("gx"), lax.axis_index("gy")
    me = gx * ngy + gy
    f32 = jnp.float32

    loads = [
        pltpu.make_async_copy(a, m[b], m["load_sem"].at[i])
        for i, (a, b) in enumerate(((layer_in, "layer"), (absorb_in, "absorb"), (table_in, "table"), (rhs_in, "rhs")))
    ]
    for load_copy in loads:
        load_copy.start()

    barrier = pltpu.get_barrier_semaphore()

    def others(act):
        if count > 64:
            def one(k, carry):
                other = lax.rem(me + k, count)
                act(other // ngy, lax.rem(other, ngy))
                return carry

            lax.fori_loop(1, count, one, 0)
            return
        for i in reversed(range(ngx)):
            for j in reversed(range(ngy)):
                if i or j:
                    x, y = gx + i, gy + j
                    act(jnp.where(x >= ngx, x - ngx, x), jnp.where(y >= ngy, y - ngy, y))

    others(lambda x, y: pl.semaphore_signal(barrier, inc=1, device_id=(x, y), device_id_type=MESH))

    def exists(dx, dy):
        checks = []
        if dx:
            checks.append(gx < ngx - dx if dx > 0 else gx >= -dx)
        if dy:
            checks.append(gy < ngy - 1 if dy > 0 else gy > 0)
        return functools.reduce(jnp.logical_and, checks)

    plan = []

    def add(name, step, src, dst):
        plan.append((name, step, src, dst, len(plan)))

    def cut(ref, first, size=1):
        return ref.at[pl.ds(first, size)]

    def add_packets(name, up, down, low, high):
        add(name, (0, 1), up, low)
        add(name, (0, -1), down, high)

    def add_corners(name, cs, cr):
        for i, step in enumerate(CORNERS):
            add(name, step, cs.at[i], cr.at[i])

    def add_dense(name, b):
        for i, step in enumerate(FACES):
            add(name, step, b["own"], b["got"].at[i])
        if "cs" in b:
            add_corners(name, b["cs"], b["cr"])

    add("begin", (1, 0), cut(m["ewf"], 4, 2), cut(m["ewf"], 0, 2))
    add("begin", (-1, 0), cut(m["ewf"], 2, 2), cut(m["ewf"], 6, 2))
    add("begin", (1, 0), cut(m["ew"], 5), cut(m["ew"], 1))
    add("begin", (-1, 0), cut(m["ew"], 2), cut(m["ew"], 6))
    add_packets("begin", m["up"], m["down"], m["low"], m["high"])
    add_corners("begin", m["cs"], m["cr"])
    add_dense("coef1", m["coef1"])
    for i, step in enumerate(CORNERS):
        add("later1", step, m["coef1"]["own"], m["ccoef1"].at[i])
    add("later", (1, 0), cut(m["ew"], 4), cut(m["ew"], 0))
    add("later", (-1, 0), cut(m["ew"], 3), cut(m["ew"], 7))
    for cycle in range(2):
        b = m["cycles"][cycle]
        add_dense(f"source{cycle}", b["source"])
        add(f"update{cycle}", (1, 0), cut(b["farown"], 0), cut(b["far"], 0))
        add(f"update{cycle}", (-1, 0), cut(b["farown"], 1), cut(b["far"], 1))
        add_packets(f"update{cycle}", b["up"], b["down"], b["low"], b["high"])
        add_corners(f"update{cycle}", b["cs"], b["cr"])
        for i, step in enumerate(AROUND):
            add(f"fine{cycle}", step, b["fine"]["own"], b["fine"]["got"].at[i])
        for i, step in enumerate(CORNERS):
            add(f"update{cycle}", step, b["source"]["own"], b["csource"].at[i])
    add("first", (1, 0), cut(m["first"], 4, 3), cut(m["first"], 0, 3))
    add("first", (-1, 0), cut(m["first"], 3, 3), cut(m["first"], 7, 3))
    add_packets("first", m["fup"], m["fdown"], m["flow"], m["fhigh"])
    add_corners("first", m["fcs"], m["fcr"])
    steps = sorted({entry[1] for entry in plan})

    for step in steps:
        @pl.when(jnp.logical_not(exists(-step[0], -step[1])))
        def _(step=step):
            for _, other, _, dst, _ in plan:
                if other == step:
                    dst[...] = jnp.zeros(dst.shape, f32)

    def remote(entry):
        _, (dx, dy), src, dst, i = entry
        return pltpu.make_async_remote_copy(
            src_ref=src, dst_ref=dst, send_sem=m["send_sem"].at[i], recv_sem=m["recv_sem"].at[i],
            device_id=(gx + dx, gy + dy), device_id_type=MESH,
        )

    def each(names, sign, act):
        for step in steps:
            mine = [entry for entry in plan if entry[0] in names and entry[1] == step]
            if mine:
                @pl.when(exists(sign * step[0], sign * step[1]))
                def _(mine=mine):
                    for entry in mine:
                        act(remote(entry))

    def start(*names):
        each(names, 1, lambda copy: copy.start())

    def receive(*names):
        each(names, -1, lambda copy: copy.wait_recv())

    def wait_sends(which):
        each({entry[0] for entry in plan if which(entry[0])}, 1, lambda copy: copy.wait_send())

    row8, lane8 = iota((8, depth), 0), iota((8, depth), 1)
    even_row, even_lane = row8 % 2 == 0, lane8 % 2 == 0

    def roll(value, shift, dim):
        size = value.shape[dim]
        return pltpu.roll(value, shift % size, dim) if shift % size else value

    def pack2(values, top):
        result = None
        for c, v in enumerate(values):
            v = roll(v, 2 * c + 2 if top else 2 * c, 0)
            result = v if c == 0 else jnp.where(row8 >= 2 * c, v, result)
        return result

    def unpack2(low, high, c):
        return jnp.where(row8 < 4, roll(high, -2 * c, 0), roll(low, 6 - 2 * c, 0))

    def pack4(pair, top):
        re, im = pair
        return jnp.where(row8 < 4, roll(re, 4, 0), im) if top else jnp.where(row8 < 4, re, roll(im, 4, 0))

    def unpack4(low, high):
        return jnp.where(row8 < 4, high, roll(low, 4, 0)), jnp.where(row8 < 4, roll(high, 4, 0), low)

    def put_corners(cs, j, near_low, near_high, from_edge):
        for i, (dx, dy) in enumerate(CORNERS):
            pair = near_high if dx > 0 else near_low
            at = 7 - from_edge if dy > 0 else from_edge
            for c, v in enumerate(pair):
                cs[i, j + c] = v[at : at + 1]

    def got_corner(cr, side, j):
        i = CORNERS.index((-side, 1))
        return cr[i, j], cr[i + 1, j]

    def corner_tile(cr, side, j, thick=1):
        below, above = got_corner(cr, side, j)
        return jnp.where(row8 >= 8 - thick, below, jnp.where(row8 < thick, above, 0.0))

    def pack_dense(first, second):
        return jnp.where(
            even_lane, jnp.where(even_row, first[0], first[1]), jnp.where(even_row, second[0], second[1])
        )

    def unpack_dense(tile):
        re = jnp.where(even_row, tile, roll(tile, 1, 0))
        im = jnp.where(even_row, roll(tile, -1, 0), tile)
        first = tuple(jnp.where(even_lane, v, roll(v, 1, 1)) for v in (re, im))
        second = tuple(jnp.where(even_lane, roll(v, -1, 1), v) for v in (re, im))
        return first, second

    def send_dense(b, planes):
        b["own"][...] = pack_dense(*planes)
        if "cs" in b:
            put_corners(b["cs"], 0, planes[0], planes[1], 0)

    def get_dense(b, own):
        before, after, below, above = [unpack_dense(b["got"][i]) for i in range(4)]
        none = jnp.zeros((8, depth), f32)
        result = []
        for p, plane in enumerate([*before, *own, *after]):
            pair = []
            for c in range(2):
                if p in (2, 3):
                    halo = jnp.where(row8 < 4, above[p - 2][c], below[p - 2][c])
                elif p in (1, 4) and "cr" in b:
                    halo = corner_tile(b["cr"], -1 if p == 1 else 1, c, 2)
                else:
                    halo = none
                pair.append(jnp.concatenate([plane[c], halo], axis=0))
            result.append(tuple(pair))
        return result

    def around(before, mid, after, s):
        total = before + after + roll(mid, s, 0) + roll(mid, -s, 0)
        lane = iota(mid.shape, 1)
        total = total + jnp.where(lane >= s, roll(mid, s, 1), 0.0)
        return total + jnp.where(lane < depth - s, roll(mid, -s, 1), 0.0)

    def load(ref, plane, rows=None):
        return tuple(ref[plane, c] if rows is None else ref[plane, c, :rows] for c in range(2))

    def store(ref, plane, pair):
        ref[plane, 0], ref[plane, 1] = pair

    def neighbours(ref, plane, s):
        return tuple(around(ref[plane - 1, c], ref[plane, c], ref[plane + 1, c], s) for c in range(2))

    def weight(diag):
        scale = OMEGA / (diag[0] * diag[0] + diag[1] * diag[1])
        return diag[0] * scale, -diag[1] * scale

    def in_pairs(low, high, body):
        def two(i, carry):
            body(low + 2 * i)
            body(low + 2 * i + 1)
            return carry

        lax.fori_loop(0, (high - low) // 2, two, 0)

    def first_two(wf_ref, w_ref, target, low, high, s, c):
        def body(p):
            part = product(load(w_ref, p), neighbours(wf_ref, p, s))
            store(target, p, tuple(1.4 * a + c * b for a, b in zip(load(wf_ref, p), part)))

        in_pairs(low, high, body)

    def sweep(ref, wf_ref, w_ref, low, high, s, c, done, behind=0):
        def body(p):
            part = product(load(w_ref, p - behind), neighbours(ref, p, s))
            wf = load(wf_ref, p - behind)
            done(p, tuple(0.4 * a + b + c * d for a, b, d in zip(load(ref, p), wf, part)))

        in_pairs(low, high, body)

    def wide_planes(tile_of, reach):
        result = []
        for rx in range(-reach, reach + 1):
            blocks = [tile_of(rx, ry) for ry in (0, 1, -1)]
            for half in range(2):
                result.append(tuple(jnp.concatenate([v[half][c] for v in blocks], axis=0) for c in range(2)))
        return result

    def residual(source, diag, ref, p, s, c):
        ns, part = neighbours(ref, p, s), product(diag, load(ref, p, 8))
        return tuple(f + c * n[:8] - q for f, n, q in zip(source, ns, part))

    def pair_mean(value):
        value = value + jnp.where(even_row, roll(value, -1, 0), roll(value, 1, 0))
        other = jnp.where(even_lane, roll(value, -1, 1), roll(value, 1, 1))
        return (value + other) * 0.125

    def own8(pair):
        return tuple(v[:8] for v in pair)

    for load_copy in loads:
        load_copy.wait()
    shifts, weights, scaled = [], [], []
    for p in range(4):
        index = m["layer"][p]
        velocity = jnp.zeros((8, depth), f32)
        for number in range(m["table"].shape[0]):
            velocity = jnp.where(index == number, m["table"][number], velocity)
        ratio = KH_FACTOR / velocity
        kh2 = ratio * ratio
        shift = (kh2, -kh2 * (BETA + ABSORB * m["absorb"][p].astype(f32)))
        diag = (6.0 - shift[0], -shift[1])
        source = (m["rhs"][0, p], m["rhs"][1, p])
        w = weight(diag)
        wf = product(w, source)
        store(m["diag0"], p, diag)
        store(m["source0"], p, source)
        store(m["ewf"], p + 2, wf)
        store(m["ew"], p + 2, w)
        m["up"][p] = pack2([*wf, *w], True)
        m["down"][p] = pack2([*wf, *w], False)
        shifts.append(shift)
        weights.append(w)
        scaled.append(wf)
    put_corners(m["cs"], 0, scaled[0], scaled[3], 0)
    put_corners(m["cs"], 2, weights[0], weights[3], 0)
    pl.semaphore_wait(barrier, count - 1)
    start("begin")
    shifts1 = [tuple(pair_mean(shifts[p][c] + shifts[p + 1][c]) for c in range(2)) for p in (0, 2)]
    diags1 = [(1.5 - s[0], -s[1]) for s in shifts1]
    weights1 = [weight(d) for d in diags1]
    send_dense(m["coef1"], weights1)
    start("coef1", "later", "later1")
    for p in range(2):
        store(m["diag1"], p, diags1[p])

    spread = 0.25 * (iota((depth, 128), 0) // 4 == iota((depth, 128), 1)).astype(f32)
    spread = spread.astype(jnp.bfloat16)
    widen = (iota((128, depth), 1) // 4 == iota((128, depth), 0)).astype(f32).astype(jnp.bfloat16)
    rows2 = 2 * ngy
    shift2_sum = tuple(shifts1[0][c] + shifts1[1][c] for c in range(2))
    m["padded"][...] = jnp.zeros(m["padded"].shape, f32)
    row2 = iota((ngx, rows2, 128), 1)
    block8 = iota((8, 128), 0) // 2

    def unpack(buffer, comp):
        planes = []
        for x in range(ngx):
            groups = []
            for q in range(0, ngy, 4):
                value = buffer[x * ngy + q]
                for j in range(1, min(4, ngy - q)):
                    value = jnp.where(block8 == (comp + j) % 4, buffer[x * ngy + q + j], value)
                groups.append(roll(value, -2 * comp, 0))
            planes.append(jnp.concatenate(groups, axis=0)[:rows2] if len(groups) > 1 else groups[0][:rows2])
        return jnp.stack(planes)

    coarse = {}

    def coarsest(cycle, sums):
        buffer = m["cycles"][cycle]["tiles"]
        tile = jnp.zeros((8, depth), f32)
        for c, v in enumerate(list(sums) + (list(shift2_sum) if cycle == 0 else [])):
            v = v + jnp.where(row8 // 2 % 2 == 0, roll(v, -2, 0), roll(v, 2, 0))
            tile = jnp.where(row8 // 2 == c, roll(v, 2 * c - 3, 0), tile)
        tile = dot3(tile * 0.25, spread)
        buffer[me] = pltpu.roll(tile, 2 * lax.rem(gy, 4), 0)

        others(
            lambda x, y: pltpu.make_async_remote_copy(
                src_ref=buffer.at[me], dst_ref=buffer.at[me],
                send_sem=m["tile_send"].at[cycle], recv_sem=m["tile_recv"].at[cycle],
                device_id=(x, y), device_id_type=MESH,
            ).start()
        )

    def coarsest_finish(cycle):
        buffer = m["cycles"][cycle]["tiles"]
        every = buffer.at[pl.ds(0, count - 1)]
        pltpu.make_async_copy(every, every, m["tile_recv"].at[cycle]).wait()
        source = unpack(buffer, 0), unpack(buffer, 1)
        if cycle == 0:
            shift = unpack(buffer, 2), unpack(buffer, 3)
            full = weight((0.375 - shift[0], -shift[1]))
            coarse["w"] = tuple(jnp.where(shift[0] > 0.0, v, 0.0) for v in full)
        w = coarse["w"]
        wf = product(w, source)
        none = jnp.zeros((1, rows2, 128), f32)

        def total(e):
            result = jnp.concatenate([none, e[:-1]], axis=0) + jnp.concatenate([e[1:], none], axis=0)
            result = result + jnp.where(row2 > 0, roll(e, 1, 1), 0.0)
            result = result + jnp.where(row2 < rows2 - 1, roll(e, -1, 1), 0.0)
            return result + roll(e, 1, 2) + roll(e, -1, 2)

        def step(_, e):
            part = product(w, (total(e[0]), total(e[1])))
            return tuple(0.4 * a + b + 0.0625 * d for a, b, d in zip(e, wf, part))

        e = lax.fori_loop(0, NC - 1, step, wf)
        for c in range(2):
            for x in range(ngx):
                m["padded"][x + 2, c, 8 : 8 + rows2] = e[c][x]
        own = [m["padded"][gx + i, c, pl.ds(6 + 2 * gy, 8)] for i in range(5) for c in range(2)]
        wide = dot3(jnp.concatenate(own, axis=0), widen)
        result = []
        for i in range(5):
            pair = []
            for c in range(2):
                rows = [wide[16 * i + 8 * c + k : 16 * i + 8 * c + k + 1] for k in (2, 3, 4, 5, 0, 1)]
                tiles = [jnp.where(row8 < 4, rows[k], rows[k + 1]) for k in (0, 2, 4)]
                pair.append(jnp.concatenate(tiles, axis=0))
            result.append(tuple(pair))
        return result

    def cycle_part(cycle, finish):
        b = m["cycles"][cycle]
        wf0, w0, upd0, upd0b = m["wf0"], m["w0"], m["upd0"], m["upd0b"]
        wf1, w1, upd1 = m["wf1"], m["w1"], m["upd1"]
        first_two(wf0, w0, upd0, 1, 7, 1, 1.0)
        held = [residual(load(m["source0"], p), load(m["diag0"], p), upd0, p + 2, 1, 1.0) for p in range(4)]
        sources = [tuple(pair_mean(held[p][c] + held[p + 1][c]) for c in range(2)) for p in (0, 2)]
        scaled1 = [product(weights1[p], sources[p]) for p in range(2)]
        send_dense(b["source"], scaled1)
        start(f"source{cycle}")
        updates = [load(upd0, p + 2, 8) for p in range(4)]
        store(b["farown"], 0, updates[2])
        store(b["farown"], 1, updates[1])
        for i in range(2):
            b["up"][i] = pack2([*updates[2 * i], *updates[2 * i + 1]], True)
            b["down"][i] = pack2([*updates[2 * i], *updates[2 * i + 1]], False)
        put_corners(b["cs"], 0, updates[0], updates[3], 0)
        start(f"update{cycle}")
        if cycle == 0:
            receive("coef1")
            for p, pair in enumerate(get_dense(m["coef1"], weights1)):
                store(w1, p, pair)
        receive(f"source{cycle}")
        for p, pair in enumerate(get_dense(b["source"], scaled1)):
            store(wf1, p, pair)
        first_two(wf1, w1, upd1, 1, 5, 2, 0.25)
        left, right = [residual(sources[p], load(m["diag1"], p), upd1, p + 2, 2, 0.25) for p in range(2)]
        coarsest(cycle, tuple(left[c] + right[c] for c in range(2)))
        updates1 = [load(upd1, p + 2, 8) for p in range(2)]
        b["fine"]["own"][...] = pack_dense(*updates1)
        start(f"fine{cycle}")

        def beside(own, faces, corners):
            def tile_of(rx, ry):
                step = (-rx, -ry)
                if step == (0, 0):
                    return own
                return unpack_dense(faces[FACES.index(step)] if step in FACES else corners[CORNERS.index(step)])

            return tile_of

        if cycle == 0:
            receive("later1")
            tile_of = beside(weights1, m["coef1"]["got"], m["ccoef1"])
            for p, pair in enumerate(wide_planes(tile_of, 1)):
                store(m["wide_w1"], p, pair)
        receive(f"update{cycle}")
        none = jnp.zeros((8, depth), f32)
        for c in range(2):
            upd0[0, c] = jnp.concatenate([b["far"][0, c], none], axis=0)
            upd0[7, c] = jnp.concatenate([b["far"][1, c], none], axis=0)
            upd0[1, c, 8:] = corner_tile(b["cr"], -1, c)
            upd0[6, c, 8:] = corner_tile(b["cr"], 1, c)
            for p in range(4):
                upd0[p + 2, c, 8:] = unpack2(b["low"][p // 2], b["high"][p // 2], 2 * (p % 2) + c)
        for p, pair in enumerate(wide_planes(beside(scaled1, b["source"]["got"], b["csource"]), 1)):
            store(m["wide_wf1"], p, pair)
        wait_sends(lambda name: cycle == 1 and not name.startswith("fine1"))
        correction = coarsest_finish(cycle)
        receive(f"fine{cycle}")
        around1 = wide_planes(
            lambda rx, ry: unpack_dense(b["fine"]["got"][AROUND.index((-rx, -ry))]) if rx or ry else updates1, 2
        )
        wide1, wide1b = m["wide1"], m["wide1b"]
        for p in range(8):
            store(wide1, p, tuple(v + x for v, x in zip(around1[p + 1], correction[(p + 1) // 2])))
        sweep(
            wide1, m["wide_wf1"], m["wide_w1"], 1, 7, 2, 0.25, lambda p, e: store(wide1b, p, e), behind=1
        )

        def prolong(p, e):
            solved = [jnp.concatenate([v[:8], jnp.where(row8 < 4, v[8:16], v[16:24])], axis=0) for v in e]
            for fine in (2 * p - 4, 2 * p - 3):
                store(upd0, fine, tuple(v + x for v, x in zip(load(upd0, fine), solved)))

        sweep(wide1b, m["wide_wf1"], m["wide_w1"], 2, 6, 2, 0.25, prolong, behind=1)
        sweep(upd0, wf0, w0, 1, 7, 1, 1.0, lambda p, e: store(upd0b, p, e))
        sweep(upd0b, wf0, w0, 2, 6, 1, 1.0, lambda p, e: finish(p - 2, own8(e)))

    none = jnp.zeros((8, depth), f32)

    def halo0(p, j):
        if p in (1, 6):
            return corner_tile(m["cr"], -1 if p == 1 else 1, j)
        if p in (0, 7):
            return none
        return unpack2(m["low"][p - 2], m["high"][p - 2], j)

    receive("begin")
    for p in range(8):
        for c in range(2):
            m["wf0"][p, c] = jnp.concatenate([m["ewf"][p, c], halo0(p, c)], axis=0)
            if p in (0, 7):
                m["w0"][p, c, 8:] = none
            else:
                m["w0"][p, c] = jnp.concatenate([m["ew"][p, c], halo0(p, 2 + c)], axis=0)

    def keep(p, e):
        store(m["first"], p + 3, e)
        m["fup"][p] = pack4(e, True)
        m["fdown"][p] = pack4(e, False)

    cycle_part(0, keep)
    kept = [load(m["first"], p + 3) for p in range(4)]
    put_corners(m["fcs"], 0, kept[0], kept[3], 0)
    put_corners(m["fcs"], 2, kept[0], kept[3], 1)
    put_corners(m["fcs"], 4, kept[1], kept[2], 0)
    start("first")
    receive("first", "later")
    for p in (0, 7):
        for c in range(2):
            m["w0"][p, c, :8] = m["ew"][p, c]
    for p in range(10):
        if 3 <= p < 7:
            halo = unpack4(m["flow"][p - 3], m["fhigh"][p - 3])
        elif p in (2, 7):
            side, halo = (-1 if p == 2 else 1), []
            for c in range(2):
                below, above = got_corner(m["fcr"], side, c)
                below2, above2 = got_corner(m["fcr"], side, 2 + c)
                tile = jnp.where(row8 == 7, below, jnp.where(row8 == 6, below2, 0.0))
                halo.append(jnp.where(row8 == 0, above, jnp.where(row8 == 1, above2, tile)))
        elif p in (1, 8):
            halo = [corner_tile(m["fcr"], -1 if p == 1 else 1, 4 + c) for c in range(2)]
        else:
            halo = [none, none]
        for c in range(2):
            m["first16"][p, c] = jnp.concatenate([m["first"][p, c], halo[c]], axis=0)
    def next_source(p):
        part = product(load(m["w0"], p), neighbours(m["first16"], p + 1, 1))
        e = load(m["first16"], p + 1)
        store(m["wf0"], p, tuple(a + b - OMEGA * v for a, b, v in zip(load(m["wf0"], p), part, e)))

    def next_own(p):
        store(m["source0"], p, residual(load(m["source0"], p), load(m["diag0"], p), m["first16"], p + 3, 1, 1.0))

    in_pairs(0, 8, next_source)
    in_pairs(0, 4, next_own)

    def give(p, e):
        for c in range(2):
            out[c, p] = m["first"][p + 3, c] + e[c]

    cycle_part(1, give)

    wait_sends(lambda name: name.startswith("fine1"))
    for cycle in range(2):
        every = m["cycles"][cycle]["tiles"].at[pl.ds(0, count - 1)]
        pltpu.make_async_copy(every, every, m["tile_send"].at[cycle]).wait()


def local(ngx, ngy, right_side, velocity_table, layer_index, absorb_level):
    depth = right_side.shape[-1]
    scratch = scratch_of(ngx, ngy, velocity_table.shape[0], depth)
    leaves, tree = jax.tree.flatten(scratch)
    anywhere = pl.BlockSpec(memory_space=pltpu.HBM)
    return pl.pallas_call(
        functools.partial(kernel, ngx, ngy, depth, tree),
        out_shape=jax.ShapeDtypeStruct(right_side.shape, jnp.float32),
        in_specs=[anywhere] * 4,
        out_specs=pl.BlockSpec(memory_space=pltpu.VMEM),
        scratch_shapes=leaves,
        compiler_params=pltpu.CompilerParams(
            collective_id=0, has_side_effects=True, vmem_limit_bytes=64 * 1024 * 1024 - 65536
        ),
    )(right_side, velocity_table, layer_index, absorb_level)


def solution(mesh):
    placed = (P(None, "gx", "gy", None), P(), P("gx", "gy", None), P("gx", "gy", None))
    return jax.shard_map(
        functools.partial(local, mesh.shape["gx"], mesh.shape["gy"]),
        mesh=mesh, in_specs=placed, out_specs=P(None, "gx", "gy", None), check_vma=False,
    )
```

```python
import functools
import math

import jax
import jax.numpy as jnp
from jax import lax
from jax.experimental import pallas as pl
from jax.experimental.pallas import tpu as pltpu
from jax.sharding import PartitionSpec as P

NC = 8
OMEGA = 0.6
BETA = 0.5
ABSORB = 0.25
KH_FACTOR = 2.0 * math.pi * 6.0 * 20.0
MESH = pl.DeviceIdType.MESH

AROUND = [(dx, dy) for dx in range(-2, 3) for dy in (-1, 0, 1) if dx or dy]
FACES = [(1, 0), (-1, 0), (0, 1), (0, -1)]
CORNERS = [(1, 1), (1, -1), (-1, 1), (-1, -1)]


def product(a, b):
    return a[0] * b[0] - a[1] * b[1], a[0] * b[1] + a[1] * b[0]


def dot3(a, b):
    rows = a.shape[0]
    pieces, rest = [], a
    for _ in range(3):
        piece = rest.astype(jnp.bfloat16).astype(jnp.float32)
        pieces.append(piece)
        rest = rest - piece
    stacked = jnp.concatenate(pieces, axis=0).astype(jnp.bfloat16)
    result = jnp.dot(stacked, b, preferred_element_type=jnp.float32)
    return result[:rows] + result[rows : 2 * rows] + result[2 * rows :]


def iota(shape, dim):
    return lax.broadcasted_iota(jnp.int32, shape, dim)


def scratch_of(ngx, ngy, layers, depth):
    f32 = jnp.float32

    def vmem(*shape):
        return pltpu.VMEM(shape, f32)

    def dense():
        return dict(own=vmem(8, depth), got=vmem(4, 8, depth), cs=vmem(4, 2, 1, depth), cr=vmem(4, 2, 1, depth))

    cycles = [
        dict(
            source=dense(), fine=dict(own=vmem(8, depth), got=vmem(len(AROUND), 8, depth)), csource=vmem(4, 8, depth),
            far=vmem(2, 2, 8, depth), farown=vmem(2, 2, 8, depth),
            up=vmem(2, 8, depth), down=vmem(2, 8, depth), low=vmem(2, 8, depth), high=vmem(2, 8, depth),
            cs=vmem(4, 2, 1, depth), cr=vmem(4, 2, 1, depth), tiles=vmem(ngx * ngy, 8, 128),
        )
        for _ in range(2)
    ]
    return dict(
        rhs=vmem(2, 4, 8, depth), layer=pltpu.VMEM((4, 8, depth), jnp.int32),
        absorb=pltpu.VMEM((4, 8, depth), jnp.int32), table=pltpu.SMEM((layers,), f32),
        ewf=vmem(8, 2, 8, depth), ew=vmem(8, 2, 8, depth),
        up=vmem(4, 8, depth), down=vmem(4, 8, depth), low=vmem(4, 8, depth), high=vmem(4, 8, depth),
        cs=vmem(4, 4, 1, depth), cr=vmem(4, 4, 1, depth),
        coef1=dict(own=vmem(8, depth), got=vmem(4, 8, depth)), ccoef1=vmem(4, 8, depth),
        first=vmem(10, 2, 8, depth),
        fup=vmem(4, 8, depth), fdown=vmem(4, 8, depth), flow=vmem(4, 8, depth), fhigh=vmem(4, 8, depth),
        fcs=vmem(4, 6, 1, depth), fcr=vmem(4, 6, 1, depth),
        cycles=cycles,
        diag0=vmem(4, 2, 8, depth), source0=vmem(4, 2, 8, depth),
        wf0=vmem(8, 2, 16, depth), w0=vmem(8, 2, 16, depth), upd0=vmem(8, 2, 16, depth), upd0b=vmem(8, 2, 16, depth),
        first16=vmem(10, 2, 16, depth),
        diag1=vmem(2, 2, 8, depth), source1=vmem(2, 2, 8, depth),
        wf1=vmem(6, 2, 16, depth), w1=vmem(6, 2, 16, depth), upd1=vmem(6, 2, 16, depth),
        wide_wf1=vmem(6, 2, 24, depth), wide_w1=vmem(6, 2, 24, depth),
        wide1=vmem(8, 2, 24, depth), wide1b=vmem(8, 2, 24, depth),
        padded=vmem(ngx + 4, 2, 2 * ngy + 16, 128),
        send_sem=pltpu.SemaphoreType.DMA((112,)), recv_sem=pltpu.SemaphoreType.DMA((112,)),
        tile_send=pltpu.SemaphoreType.DMA((2,)), tile_recv=pltpu.SemaphoreType.DMA((2,)),
        load_sem=pltpu.SemaphoreType.DMA((4,)),
    )


def kernel(ngx, ngy, depth, tree, rhs_in, table_in, layer_in, absorb_in, out, *scratch):
    m = jax.tree.unflatten(tree, scratch)
    count = ngx * ngy
    gx, gy = lax.axis_index("gx"), lax.axis_index("gy")
    me = gx * ngy + gy
    f32 = jnp.float32

    loads = [
        pltpu.make_async_copy(a, m[b], m["load_sem"].at[i])
        for i, (a, b) in enumerate(((layer_in, "layer"), (absorb_in, "absorb"), (table_in, "table"), (rhs_in, "rhs")))
    ]
    for load_copy in loads:
        load_copy.start()

    barrier = pltpu.get_barrier_semaphore()

    def others(act):
        if count > 64:
            def one(k, carry):
                other = lax.rem(me + k, count)
                act(other // ngy, lax.rem(other, ngy))
                return carry

            lax.fori_loop(1, count, one, 0)
            return
        for i in reversed(range(ngx)):
            for j in reversed(range(ngy)):
                if i or j:
                    x, y = gx + i, gy + j
                    act(jnp.where(x >= ngx, x - ngx, x), jnp.where(y >= ngy, y - ngy, y))

    others(lambda x, y: pl.semaphore_signal(barrier, inc=1, device_id=(x, y), device_id_type=MESH))

    def exists(dx, dy):
        checks = []
        if dx:
            checks.append(gx < ngx - dx if dx > 0 else gx >= -dx)
        if dy:
            checks.append(gy < ngy - 1 if dy > 0 else gy > 0)
        return functools.reduce(jnp.logical_and, checks)

    plan = []

    def add(name, step, src, dst):
        plan.append((name, step, src, dst, len(plan)))

    def cut(ref, first, size=1):
        return ref.at[pl.ds(first, size)]

    def add_packets(name, up, down, low, high):
        add(name, (0, 1), up, low)
        add(name, (0, -1), down, high)

    def add_corners(name, cs, cr):
        for i, step in enumerate(CORNERS):
            add(name, step, cs.at[i], cr.at[i])

    def add_dense(name, b):
        for i, step in enumerate(FACES):
            add(name, step, b["own"], b["got"].at[i])
        if "cs" in b:
            add_corners(name, b["cs"], b["cr"])

    add("begin", (1, 0), cut(m["ewf"], 4, 2), cut(m["ewf"], 0, 2))
    add("begin", (-1, 0), cut(m["ewf"], 2, 2), cut(m["ewf"], 6, 2))
    add("begin", (1, 0), cut(m["ew"], 5), cut(m["ew"], 1))
    add("begin", (-1, 0), cut(m["ew"], 2), cut(m["ew"], 6))
    add_packets("begin", m["up"], m["down"], m["low"], m["high"])
    add_corners("begin", m["cs"], m["cr"])
    add_dense("coef1", m["coef1"])
    for i, step in enumerate(CORNERS):
        add("later1", step, m["coef1"]["own"], m["ccoef1"].at[i])
    add("later", (1, 0), cut(m["ew"], 4), cut(m["ew"], 0))
    add("later", (-1, 0), cut(m["ew"], 3), cut(m["ew"], 7))
    for cycle in range(2):
        b = m["cycles"][cycle]
        add_dense(f"source{cycle}", b["source"])
        add(f"update{cycle}", (1, 0), cut(b["farown"], 0), cut(b["far"], 0))
        add(f"update{cycle}", (-1, 0), cut(b["farown"], 1), cut(b["far"], 1))
        add_packets(f"update{cycle}", b["up"], b["down"], b["low"], b["high"])
        add_corners(f"update{cycle}", b["cs"], b["cr"])
        for i, step in enumerate(AROUND):
            add(f"fine{cycle}", step, b["fine"]["own"], b["fine"]["got"].at[i])
        for i, step in enumerate(CORNERS):
            add(f"update{cycle}", step, b["source"]["own"], b["csource"].at[i])
    add("first", (1, 0), cut(m["first"], 4, 3), cut(m["first"], 0, 3))
    add("first", (-1, 0), cut(m["first"], 3, 3), cut(m["first"], 7, 3))
    add_packets("first", m["fup"], m["fdown"], m["flow"], m["fhigh"])
    add_corners("first", m["fcs"], m["fcr"])
    steps = sorted({entry[1] for entry in plan})

    for step in steps:
        @pl.when(jnp.logical_not(exists(-step[0], -step[1])))
        def _(step=step):
            for _, other, _, dst, _ in plan:
                if other == step:
                    dst[...] = jnp.zeros(dst.shape, f32)

    def remote(entry):
        _, (dx, dy), src, dst, i = entry
        return pltpu.make_async_remote_copy(
            src_ref=src, dst_ref=dst, send_sem=m["send_sem"].at[i], recv_sem=m["recv_sem"].at[i],
            device_id=(gx + dx, gy + dy), device_id_type=MESH,
        )

    def each(names, sign, act):
        for step in steps:
            mine = [entry for entry in plan if entry[0] in names and entry[1] == step]
            if mine:
                @pl.when(exists(sign * step[0], sign * step[1]))
                def _(mine=mine):
                    for entry in mine:
                        act(remote(entry))

    def start(*names):
        each(names, 1, lambda copy: copy.start())

    def receive(*names):
        each(names, -1, lambda copy: copy.wait_recv())

    def wait_sends(which):
        each({entry[0] for entry in plan if which(entry[0])}, 1, lambda copy: copy.wait_send())

    row8, lane8 = iota((8, depth), 0), iota((8, depth), 1)
    even_row, even_lane = row8 % 2 == 0, lane8 % 2 == 0

    def roll(value, shift, dim):
        size = value.shape[dim]
        return pltpu.roll(value, shift % size, dim) if shift % size else value

    def pack2(values, top):
        result = None
        for c, v in enumerate(values):
            v = roll(v, 2 * c + 2 if top else 2 * c, 0)
            result = v if c == 0 else jnp.where(row8 >= 2 * c, v, result)
        return result

    def unpack2(low, high, c):
        return jnp.where(row8 < 4, roll(high, -2 * c, 0), roll(low, 6 - 2 * c, 0))

    def pack4(pair, top):
        re, im = pair
        return jnp.where(row8 < 4, roll(re, 4, 0), im) if top else jnp.where(row8 < 4, re, roll(im, 4, 0))

    def unpack4(low, high):
        return jnp.where(row8 < 4, high, roll(low, 4, 0)), jnp.where(row8 < 4, roll(high, 4, 0), low)

    def put_corners(cs, j, near_low, near_high, from_edge):
        for i, (dx, dy) in enumerate(CORNERS):
            pair = near_high if dx > 0 else near_low
            at = 7 - from_edge if dy > 0 else from_edge
            for c, v in enumerate(pair):
                cs[i, j + c] = v[at : at + 1]

    def got_corner(cr, side, j):
        i = CORNERS.index((-side, 1))
        return cr[i, j], cr[i + 1, j]

    def corner_tile(cr, side, j, thick=1):
        below, above = got_corner(cr, side, j)
        return jnp.where(row8 >= 8 - thick, below, jnp.where(row8 < thick, above, 0.0))

    def pack_dense(first, second):
        return jnp.where(
            even_lane, jnp.where(even_row, first[0], first[1]), jnp.where(even_row, second[0], second[1])
        )

    def unpack_dense(tile):
        re = jnp.where(even_row, tile, roll(tile, 1, 0))
        im = jnp.where(even_row, roll(tile, -1, 0), tile)
        first = tuple(jnp.where(even_lane, v, roll(v, 1, 1)) for v in (re, im))
        second = tuple(jnp.where(even_lane, roll(v, -1, 1), v) for v in (re, im))
        return first, second

    def send_dense(b, planes):
        b["own"][...] = pack_dense(*planes)
        if "cs" in b:
            put_corners(b["cs"], 0, planes[0], planes[1], 0)

    def get_dense(b, own):
        before, after, below, above = [unpack_dense(b["got"][i]) for i in range(4)]
        none = jnp.zeros((8, depth), f32)
        result = []
        for p, plane in enumerate([*before, *own, *after]):
            pair = []
            for c in range(2):
                if p in (2, 3):
                    halo = jnp.where(row8 < 4, above[p - 2][c], below[p - 2][c])
                elif p in (1, 4) and "cr" in b:
                    halo = corner_tile(b["cr"], -1 if p == 1 else 1, c, 2)
                else:
                    halo = none
                pair.append(jnp.concatenate([plane[c], halo], axis=0))
            result.append(tuple(pair))
        return result

    def around(before, mid, after, s, rows):
        beside = roll(mid, s, 0) + roll(mid, -s, 0)
        total, mid = before + after + beside[:rows], mid[:rows]
        lane = iota(mid.shape, 1)
        total = total + jnp.where(lane >= s, roll(mid, s, 1), 0.0)
        return total + jnp.where(lane < depth - s, roll(mid, -s, 1), 0.0)

    def load(ref, plane, rows=None):
        return tuple(ref[plane, c] if rows is None else ref[plane, c, :rows] for c in range(2))

    def store(ref, plane, pair):
        for c, v in enumerate(pair):
            ref[plane, c, : v.shape[0]] = v

    def neighbours(ref, plane, s, rows=None):
        rows = rows or ref.shape[2]
        return tuple(
            around(ref[plane - 1, c, :rows], ref[plane, c], ref[plane + 1, c, :rows], s, rows) for c in range(2)
        )

    def weight(diag):
        scale = OMEGA / (diag[0] * diag[0] + diag[1] * diag[1])
        return diag[0] * scale, -diag[1] * scale

    def first_two(wf_ref, w_ref, target, planes, s, c):
        for p in planes:
            rows = 8 if p in (planes[0], planes[-1]) else 16
            part = product(load(w_ref, p, rows), neighbours(wf_ref, p, s, rows))
            store(target, p, tuple(1.4 * a + c * b for a, b in zip(load(wf_ref, p, rows), part)))

    def sweep(ref, wf_ref, w_ref, planes, s, c, behind=0, rows_of=lambda p: None):
        for p in planes:
            rows = rows_of(p) or ref.shape[2]
            part = product(load(w_ref, p - behind, rows), neighbours(ref, p, s, rows))
            wf = load(wf_ref, p - behind, rows)
            yield p, tuple(0.4 * a + b + c * d for a, b, d in zip(load(ref, p, rows), wf, part))

    def wide_planes(tile_of, reach):
        result = []
        for rx in range(-reach, reach + 1):
            blocks = [tile_of(rx, ry) for ry in (0, 1, -1)]
            for half in range(2):
                result.append(tuple(jnp.concatenate([v[half][c] for v in blocks], axis=0) for c in range(2)))
        return result

    def residual(source, diag, ref, p, s, c):
        ns, part = neighbours(ref, p, s, 8), product(diag, load(ref, p, 8))
        return tuple(f + c * n - q for f, n, q in zip(source, ns, part))

    def pair_mean(value):
        value = value + jnp.where(even_row, roll(value, -1, 0), roll(value, 1, 0))
        other = jnp.where(even_lane, roll(value, -1, 1), roll(value, 1, 1))
        return (value + other) * 0.125

    def own8(pair):
        return tuple(v[:8] for v in pair)

    for load_copy in loads:
        load_copy.wait()
    shifts, weights, scaled = [], [], []
    for p in range(4):
        index = m["layer"][p]
        velocity = jnp.zeros((8, depth), f32)
        for number in range(m["table"].shape[0]):
            velocity = jnp.where(index == number, m["table"][number], velocity)
        ratio = KH_FACTOR / velocity
        kh2 = ratio * ratio
        shift = (kh2, -kh2 * (BETA + ABSORB * m["absorb"][p].astype(f32)))
        diag = (6.0 - shift[0], -shift[1])
        source = (m["rhs"][0, p], m["rhs"][1, p])
        w = weight(diag)
        wf = product(w, source)
        store(m["diag0"], p, diag)
        store(m["source0"], p, source)
        store(m["ewf"], p + 2, wf)
        store(m["ew"], p + 2, w)
        m["up"][p] = pack2([*wf, *w], True)
        m["down"][p] = pack2([*wf, *w], False)
        shifts.append(shift)
        weights.append(w)
        scaled.append(wf)
    put_corners(m["cs"], 0, scaled[0], scaled[3], 0)
    put_corners(m["cs"], 2, weights[0], weights[3], 0)
    pl.semaphore_wait(barrier, count - 1)
    start("begin")
    shifts1 = [tuple(pair_mean(shifts[p][c] + shifts[p + 1][c]) for c in range(2)) for p in (0, 2)]
    diags1 = [(1.5 - s[0], -s[1]) for s in shifts1]
    weights1 = [weight(d) for d in diags1]
    send_dense(m["coef1"], weights1)
    start("coef1", "later", "later1")
    for p in range(2):
        store(m["diag1"], p, diags1[p])

    spread = 0.25 * (iota((depth, 128), 0) // 4 == iota((depth, 128), 1)).astype(f32)
    spread = spread.astype(jnp.bfloat16)
    widen = (iota((128, depth), 1) // 4 == iota((128, depth), 0)).astype(f32).astype(jnp.bfloat16)
    rows2 = 2 * ngy
    shift2_sum = tuple(shifts1[0][c] + shifts1[1][c] for c in range(2))
    m["padded"][...] = jnp.zeros(m["padded"].shape, f32)
    row2 = iota((ngx, rows2, 128), 1)
    block8 = iota((8, 128), 0) // 2

    def unpack(buffer, comp):
        planes = []
        for x in range(ngx):
            groups = []
            for q in range(0, ngy, 4):
                value = buffer[x * ngy + q]
                for j in range(1, min(4, ngy - q)):
                    value = jnp.where(block8 == (comp + j) % 4, buffer[x * ngy + q + j], value)
                groups.append(roll(value, -2 * comp, 0))
            planes.append(jnp.concatenate(groups, axis=0)[:rows2] if len(groups) > 1 else groups[0][:rows2])
        return jnp.stack(planes)

    coarse = {}

    def coarsest(cycle, sums):
        buffer = m["cycles"][cycle]["tiles"]
        tile = jnp.zeros((8, depth), f32)
        for c, v in enumerate(list(sums) + (list(shift2_sum) if cycle == 0 else [])):
            v = v + jnp.where(row8 // 2 % 2 == 0, roll(v, -2, 0), roll(v, 2, 0))
            tile = jnp.where(row8 // 2 == c, roll(v, 2 * c - 3, 0), tile)
        tile = dot3(tile * 0.25, spread)
        buffer[me] = pltpu.roll(tile, 2 * lax.rem(gy, 4), 0)

        others(
            lambda x, y: pltpu.make_async_remote_copy(
                src_ref=buffer.at[me], dst_ref=buffer.at[me],
                send_sem=m["tile_send"].at[cycle], recv_sem=m["tile_recv"].at[cycle],
                device_id=(x, y), device_id_type=MESH,
            ).start()
        )

    def coarsest_finish(cycle):
        buffer = m["cycles"][cycle]["tiles"]
        every = buffer.at[pl.ds(0, count - 1)]
        pltpu.make_async_copy(every, every, m["tile_recv"].at[cycle]).wait()
        source = unpack(buffer, 0), unpack(buffer, 1)
        if cycle == 0:
            shift = unpack(buffer, 2), unpack(buffer, 3)
            full = weight((0.375 - shift[0], -shift[1]))
            coarse["w"] = tuple(jnp.where(shift[0] > 0.0, v, 0.0) for v in full)
        w = coarse["w"]
        wf = product(w, source)
        none = jnp.zeros((1, rows2, 128), f32)

        def total(e):
            result = jnp.concatenate([none, e[:-1]], axis=0) + jnp.concatenate([e[1:], none], axis=0)
            result = result + jnp.where(row2 > 0, roll(e, 1, 1), 0.0)
            result = result + jnp.where(row2 < rows2 - 1, roll(e, -1, 1), 0.0)
            return result + roll(e, 1, 2) + roll(e, -1, 2)

        def step(_, e):
            part = product(w, (total(e[0]), total(e[1])))
            return tuple(0.4 * a + b + 0.0625 * d for a, b, d in zip(e, wf, part))

        e = lax.fori_loop(0, NC - 1, step, wf)
        for c in range(2):
            for x in range(ngx):
                m["padded"][x + 2, c, 8 : 8 + rows2] = e[c][x]
        own = [m["padded"][gx + i, c, pl.ds(6 + 2 * gy, 8)] for i in range(5) for c in range(2)]
        wide = dot3(jnp.concatenate(own, axis=0), widen)
        result = []
        for i in range(5):
            pair = []
            for c in range(2):
                rows = [wide[16 * i + 8 * c + k : 16 * i + 8 * c + k + 1] for k in (2, 3, 4, 5, 0, 1)]
                tiles = [jnp.where(row8 < 4, rows[k], rows[k + 1]) for k in (0, 2, 4)]
                pair.append(jnp.concatenate(tiles, axis=0))
            result.append(tuple(pair))
        return result

    def cycle_part(cycle):
        b = m["cycles"][cycle]
        wf0, w0, upd0, upd0b = m["wf0"], m["w0"], m["upd0"], m["upd0b"]
        wf1, w1, upd1 = m["wf1"], m["w1"], m["upd1"]
        first_two(wf0, w0, upd0, range(1, 7), 1, 1.0)
        held = [residual(load(m["source0"], p), load(m["diag0"], p), upd0, p + 2, 1, 1.0) for p in range(4)]
        sources = [tuple(pair_mean(held[p][c] + held[p + 1][c]) for c in range(2)) for p in (0, 2)]
        scaled1 = [product(weights1[p], sources[p]) for p in range(2)]
        send_dense(b["source"], scaled1)
        start(f"source{cycle}")
        updates = [load(upd0, p + 2, 8) for p in range(4)]
        store(b["farown"], 0, updates[2])
        store(b["farown"], 1, updates[1])
        for i in range(2):
            b["up"][i] = pack2([*updates[2 * i], *updates[2 * i + 1]], True)
            b["down"][i] = pack2([*updates[2 * i], *updates[2 * i + 1]], False)
        put_corners(b["cs"], 0, updates[0], updates[3], 0)
        start(f"update{cycle}")
        if cycle == 0:
            receive("coef1")
            for p, pair in enumerate(get_dense(m["coef1"], weights1)):
                store(w1, p, pair)
        receive(f"source{cycle}")
        for p, pair in enumerate(get_dense(b["source"], scaled1)):
            store(wf1, p, pair)
        first_two(wf1, w1, upd1, range(1, 5), 2, 0.25)
        left, right = [residual(sources[p], load(m["diag1"], p), upd1, p + 2, 2, 0.25) for p in range(2)]
        coarsest(cycle, tuple(left[c] + right[c] for c in range(2)))
        updates1 = [load(upd1, p + 2, 8) for p in range(2)]
        b["fine"]["own"][...] = pack_dense(*updates1)
        start(f"fine{cycle}")

        def beside(own, faces, corners):
            def tile_of(rx, ry):
                step = (-rx, -ry)
                if step == (0, 0):
                    return own
                return unpack_dense(faces[FACES.index(step)] if step in FACES else corners[CORNERS.index(step)])

            return tile_of

        if cycle == 0:
            receive("later1")
            tile_of = beside(weights1, m["coef1"]["got"], m["ccoef1"])
            for p, pair in enumerate(wide_planes(tile_of, 1)):
                store(m["wide_w1"], p, pair)
        receive(f"update{cycle}")
        none = jnp.zeros((8, depth), f32)
        for c in range(2):
            upd0[0, c] = jnp.concatenate([b["far"][0, c], none], axis=0)
            upd0[7, c] = jnp.concatenate([b["far"][1, c], none], axis=0)
            upd0[1, c, 8:] = corner_tile(b["cr"], -1, c)
            upd0[6, c, 8:] = corner_tile(b["cr"], 1, c)
            for p in range(4):
                upd0[p + 2, c, 8:] = unpack2(b["low"][p // 2], b["high"][p // 2], 2 * (p % 2) + c)
        for p, pair in enumerate(wide_planes(beside(scaled1, b["source"]["got"], b["csource"]), 1)):
            store(m["wide_wf1"], p, pair)
        wait_sends(lambda name: cycle == 1 and not name.startswith("fine1"))
        correction = coarsest_finish(cycle)
        receive(f"fine{cycle}")
        around1 = wide_planes(
            lambda rx, ry: unpack_dense(b["fine"]["got"][AROUND.index((-rx, -ry))]) if rx or ry else updates1, 2
        )
        wide1, wide1b = m["wide1"], m["wide1b"]
        for p in range(8):
            store(wide1, p, tuple(v + x for v, x in zip(around1[p + 1], correction[(p + 1) // 2])))
        for p, e in sweep(wide1, m["wide_wf1"], m["wide_w1"], range(1, 7), 2, 0.25, 1):
            store(wide1b, p, e)
        for p, e in sweep(wide1b, m["wide_wf1"], m["wide_w1"], range(2, 6), 2, 0.25, 1):
            solved = [jnp.concatenate([v[:8], jnp.where(row8 < 4, v[8:16], v[16:24])], axis=0) for v in e]
            for fine in (2 * p - 4, 2 * p - 3):
                store(upd0, fine, tuple(v + x for v, x in zip(load(upd0, fine), solved)))
        for p, e in sweep(upd0, wf0, w0, range(1, 7), 1, 1.0, rows_of=lambda p: 8 if p in (1, 6) else 16):
            store(upd0b, p, e)
        for p, e in sweep(upd0b, wf0, w0, range(2, 6), 1, 1.0, rows_of=lambda p: 8):
            yield p - 2, own8(e)

    none = jnp.zeros((8, depth), f32)

    def halo0(p, j):
        if p in (1, 6):
            return corner_tile(m["cr"], -1 if p == 1 else 1, j)
        if p in (0, 7):
            return none
        return unpack2(m["low"][p - 2], m["high"][p - 2], j)

    receive("begin")
    for p in range(8):
        for c in range(2):
            m["wf0"][p, c] = jnp.concatenate([m["ewf"][p, c], halo0(p, c)], axis=0)
            if p in (0, 7):
                m["w0"][p, c, 8:] = none
            else:
                m["w0"][p, c] = jnp.concatenate([m["ew"][p, c], halo0(p, 2 + c)], axis=0)
    kept = []
    for p, e in cycle_part(0):
        store(m["first"], p + 3, e)
        m["fup"][p] = pack4(e, True)
        m["fdown"][p] = pack4(e, False)
        kept.append(e)
    put_corners(m["fcs"], 0, kept[0], kept[3], 0)
    put_corners(m["fcs"], 2, kept[0], kept[3], 1)
    put_corners(m["fcs"], 4, kept[1], kept[2], 0)
    start("first")
    receive("first", "later")
    for p in (0, 7):
        for c in range(2):
            m["w0"][p, c, :8] = m["ew"][p, c]
    for p in range(10):
        if 3 <= p < 7:
            halo = unpack4(m["flow"][p - 3], m["fhigh"][p - 3])
        elif p in (2, 7):
            side, halo = (-1 if p == 2 else 1), []
            for c in range(2):
                below, above = got_corner(m["fcr"], side, c)
                below2, above2 = got_corner(m["fcr"], side, 2 + c)
                tile = jnp.where(row8 == 7, below, jnp.where(row8 == 6, below2, 0.0))
                halo.append(jnp.where(row8 == 0, above, jnp.where(row8 == 1, above2, tile)))
        elif p in (1, 8):
            halo = [corner_tile(m["fcr"], -1 if p == 1 else 1, 4 + c) for c in range(2)]
        else:
            halo = [none, none]
        for c in range(2):
            m["first16"][p, c] = jnp.concatenate([m["first"][p, c], halo[c]], axis=0)
    for p in range(8):
        rows = 8 if p in (0, 7) else 16
        ns = neighbours(m["first16"], p + 1, 1, rows)
        e = load(m["first16"], p + 1, rows)
        if 2 <= p < 6:
            part = product(load(m["diag0"], p - 2), own8(e))
            source = load(m["source0"], p - 2)
            store(m["source0"], p - 2, tuple(f + n[:8] - q for f, n, q in zip(source, ns, part)))
        part = product(load(m["w0"], p, rows), ns)
        store(m["wf0"], p, tuple(a + b - OMEGA * v for a, b, v in zip(load(m["wf0"], p, rows), part, e)))
    for p, e in cycle_part(1):
        for c in range(2):
            out[c, p] = m["first"][p + 3, c] + e[c]

    wait_sends(lambda name: name.startswith("fine1"))
    for cycle in range(2):
        every = m["cycles"][cycle]["tiles"].at[pl.ds(0, count - 1)]
        pltpu.make_async_copy(every, every, m["tile_send"].at[cycle]).wait()


def local(ngx, ngy, right_side, velocity_table, layer_index, absorb_level):
    depth = right_side.shape[-1]
    scratch = scratch_of(ngx, ngy, velocity_table.shape[0], depth)
    leaves, tree = jax.tree.flatten(scratch)
    anywhere = pl.BlockSpec(memory_space=pltpu.HBM)
    return pl.pallas_call(
        functools.partial(kernel, ngx, ngy, depth, tree),
        out_shape=jax.ShapeDtypeStruct(right_side.shape, jnp.float32),
        in_specs=[anywhere] * 4,
        out_specs=pl.BlockSpec(memory_space=pltpu.VMEM),
        scratch_shapes=leaves,
        compiler_params=pltpu.CompilerParams(
            collective_id=0, has_side_effects=True, vmem_limit_bytes=64 * 1024 * 1024 - 65536
        ),
    )(right_side, velocity_table, layer_index, absorb_level)


def solution(mesh):
    placed = (P(None, "gx", "gy", None), P(), P("gx", "gy", None), P("gx", "gy", None))
    return jax.shard_map(
        functools.partial(local, mesh.shape["gx"], mesh.shape["gy"]),
        mesh=mesh, in_specs=placed, out_specs=P(None, "gx", "gy", None), check_vma=False,
    )
```

```python
import functools
import math

import jax
import jax.numpy as jnp
from jax import lax
from jax.experimental import pallas as pl
from jax.experimental.pallas import tpu as pltpu
from jax.sharding import PartitionSpec as P

NC = 8
OMEGA = 0.6
BETA = 0.5
ABSORB = 0.25
KH_FACTOR = 2.0 * math.pi * 6.0 * 20.0
MESH = pl.DeviceIdType.MESH

AROUND = [(dx, dy) for dx in range(-2, 3) for dy in (-1, 0, 1) if dx or dy]
FACES = [(1, 0), (-1, 0), (0, 1), (0, -1)]
CORNERS = [(1, 1), (1, -1), (-1, 1), (-1, -1)]


def product(a, b):
    return a[0] * b[0] - a[1] * b[1], a[0] * b[1] + a[1] * b[0]


def dot3(a, b):
    rows = a.shape[0]
    pieces, rest = [], a
    for _ in range(3):
        piece = rest.astype(jnp.bfloat16).astype(jnp.float32)
        pieces.append(piece)
        rest = rest - piece
    stacked = jnp.concatenate(pieces, axis=0).astype(jnp.bfloat16)
    result = jnp.dot(stacked, b, preferred_element_type=jnp.float32)
    return result[:rows] + result[rows : 2 * rows] + result[2 * rows :]


def iota(shape, dim):
    return lax.broadcasted_iota(jnp.int32, shape, dim)


def scratch_of(ngx, ngy, layers, depth):
    f32 = jnp.float32

    def vmem(*shape):
        return pltpu.VMEM(shape, f32)

    def dense():
        return dict(own=vmem(8, depth), got=vmem(4, 8, depth), cs=vmem(4, 2, 1, depth), cr=vmem(4, 2, 1, depth))

    cycles = [
        dict(
            source=dense(), fine=dict(own=vmem(8, depth), got=vmem(len(AROUND), 8, depth)), csource=vmem(4, 8, depth),
            far=vmem(2, 2, 8, depth), farown=vmem(2, 2, 8, depth),
            up=vmem(2, 8, depth), down=vmem(2, 8, depth), low=vmem(2, 8, depth), high=vmem(2, 8, depth),
            cs=vmem(4, 2, 1, depth), cr=vmem(4, 2, 1, depth), tiles=vmem(ngx * ngy, 8, 128),
        )
        for _ in range(2)
    ]
    return dict(
        rhs=vmem(2, 4, 8, depth), layer=pltpu.VMEM((4, 8, depth), jnp.int32),
        absorb=pltpu.VMEM((4, 8, depth), jnp.int32), table=pltpu.SMEM((layers,), f32),
        ewf=vmem(8, 2, 8, depth), ew=vmem(8, 2, 8, depth),
        up=vmem(4, 8, depth), down=vmem(4, 8, depth), low=vmem(4, 8, depth), high=vmem(4, 8, depth),
        cs=vmem(4, 4, 1, depth), cr=vmem(4, 4, 1, depth),
        coef1=dict(own=vmem(8, depth), got=vmem(4, 8, depth)), ccoef1=vmem(4, 8, depth),
        first=vmem(10, 2, 8, depth),
        fup=vmem(4, 8, depth), fdown=vmem(4, 8, depth), flow=vmem(4, 8, depth), fhigh=vmem(4, 8, depth),
        fcs=vmem(4, 6, 1, depth), fcr=vmem(4, 6, 1, depth),
        cycles=cycles,
        diag0=vmem(4, 2, 8, depth), source0=vmem(4, 2, 8, depth),
        wf0=vmem(8, 2, 16, depth), w0=vmem(8, 2, 16, depth), upd0=vmem(8, 2, 16, depth), upd0b=vmem(8, 2, 16, depth),
        first16=vmem(10, 2, 16, depth),
        diag1=vmem(2, 2, 8, depth), source1=vmem(2, 2, 8, depth),
        wf1=vmem(6, 2, 16, depth), w1=vmem(6, 2, 16, depth), upd1=vmem(6, 2, 16, depth),
        wide_wf1=vmem(6, 2, 24, depth), wide_w1=vmem(6, 2, 24, depth),
        wide1=vmem(8, 2, 24, depth), wide1b=vmem(8, 2, 24, depth),
        padded=vmem(ngx + 4, 2, 2 * ngy + 16, 128),
        send_sem=pltpu.SemaphoreType.DMA((112,)), recv_sem=pltpu.SemaphoreType.DMA((112,)),
        tile_send=pltpu.SemaphoreType.DMA((2,)), tile_recv=pltpu.SemaphoreType.DMA((2,)),
        load_sem=pltpu.SemaphoreType.DMA((4,)),
    )


def kernel(ngx, ngy, depth, tree, rhs_in, table_in, layer_in, absorb_in, out, *scratch):
    m = jax.tree.unflatten(tree, scratch)
    count = ngx * ngy
    gx, gy = lax.axis_index("gx"), lax.axis_index("gy")
    me = gx * ngy + gy
    f32 = jnp.float32

    loads = [
        pltpu.make_async_copy(a, m[b], m["load_sem"].at[i])
        for i, (a, b) in enumerate(((layer_in, "layer"), (absorb_in, "absorb"), (table_in, "table"), (rhs_in, "rhs")))
    ]
    for load_copy in loads:
        load_copy.start()

    barrier = pltpu.get_barrier_semaphore()

    def others(act):
        if count > 64:
            def one(k, carry):
                other = lax.rem(me + k, count)
                act(other // ngy, lax.rem(other, ngy))
                return carry

            lax.fori_loop(1, count, one, 0)
            return
        for i in reversed(range(ngx)):
            for j in reversed(range(ngy)):
                if i or j:
                    x, y = gx + i, gy + j
                    act(jnp.where(x >= ngx, x - ngx, x), jnp.where(y >= ngy, y - ngy, y))

    others(lambda x, y: pl.semaphore_signal(barrier, inc=1, device_id=(x, y), device_id_type=MESH))

    def exists(dx, dy):
        checks = []
        if dx:
            checks.append(gx < ngx - dx if dx > 0 else gx >= -dx)
        if dy:
            checks.append(gy < ngy - 1 if dy > 0 else gy > 0)
        return functools.reduce(jnp.logical_and, checks)

    plan = []

    def add(name, step, src, dst):
        plan.append((name, step, src, dst, len(plan)))

    def cut(ref, first, size=1):
        return ref.at[pl.ds(first, size)]

    def add_packets(name, up, down, low, high):
        add(name, (0, 1), up, low)
        add(name, (0, -1), down, high)

    def add_corners(name, cs, cr):
        for i, step in enumerate(CORNERS):
            add(name, step, cs.at[i], cr.at[i])

    def add_dense(name, b):
        for i, step in enumerate(FACES):
            add(name, step, b["own"], b["got"].at[i])
        if "cs" in b:
            add_corners(name, b["cs"], b["cr"])

    add("begin", (1, 0), cut(m["ewf"], 4, 2), cut(m["ewf"], 0, 2))
    add("begin", (-1, 0), cut(m["ewf"], 2, 2), cut(m["ewf"], 6, 2))
    add("begin", (1, 0), cut(m["ew"], 5), cut(m["ew"], 1))
    add("begin", (-1, 0), cut(m["ew"], 2), cut(m["ew"], 6))
    add_packets("begin", m["up"], m["down"], m["low"], m["high"])
    add_corners("begin", m["cs"], m["cr"])
    add_dense("coef1", m["coef1"])
    for i, step in enumerate(CORNERS):
        add("later1", step, m["coef1"]["own"], m["ccoef1"].at[i])
    add("later", (1, 0), cut(m["ew"], 4), cut(m["ew"], 0))
    add("later", (-1, 0), cut(m["ew"], 3), cut(m["ew"], 7))
    for cycle in range(2):
        b = m["cycles"][cycle]
        add_dense(f"source{cycle}", b["source"])
        add(f"update{cycle}", (1, 0), cut(b["farown"], 0), cut(b["far"], 0))
        add(f"update{cycle}", (-1, 0), cut(b["farown"], 1), cut(b["far"], 1))
        add_packets(f"update{cycle}", b["up"], b["down"], b["low"], b["high"])
        add_corners(f"update{cycle}", b["cs"], b["cr"])
        for i, step in enumerate(AROUND):
            add(f"fine{cycle}", step, b["fine"]["own"], b["fine"]["got"].at[i])
        for i, step in enumerate(CORNERS):
            add(f"update{cycle}", step, b["source"]["own"], b["csource"].at[i])
    add("first", (1, 0), cut(m["first"], 4, 3), cut(m["first"], 0, 3))
    add("first", (-1, 0), cut(m["first"], 3, 3), cut(m["first"], 7, 3))
    add_packets("first", m["fup"], m["fdown"], m["flow"], m["fhigh"])
    add_corners("first", m["fcs"], m["fcr"])
    steps = sorted({entry[1] for entry in plan})

    for step in steps:
        @pl.when(jnp.logical_not(exists(-step[0], -step[1])))
        def _(step=step):
            for _, other, _, dst, _ in plan:
                if other == step:
                    dst[...] = jnp.zeros(dst.shape, f32)

    def remote(entry):
        _, (dx, dy), src, dst, i = entry
        return pltpu.make_async_remote_copy(
            src_ref=src, dst_ref=dst, send_sem=m["send_sem"].at[i], recv_sem=m["recv_sem"].at[i],
            device_id=(gx + dx, gy + dy), device_id_type=MESH,
        )

    def each(names, sign, act):
        for step in steps:
            mine = [entry for entry in plan if entry[0] in names and entry[1] == step]
            if mine:
                @pl.when(exists(sign * step[0], sign * step[1]))
                def _(mine=mine):
                    for entry in mine:
                        act(remote(entry))

    def start(*names):
        each(names, 1, lambda copy: copy.start())

    def receive(*names):
        each(names, -1, lambda copy: copy.wait_recv())

    def wait_sends(which):
        each({entry[0] for entry in plan if which(entry[0])}, 1, lambda copy: copy.wait_send())

    row8, lane8 = iota((8, depth), 0), iota((8, depth), 1)
    even_row, even_lane = row8 % 2 == 0, lane8 % 2 == 0

    def roll(value, shift, dim):
        size = value.shape[dim]
        return pltpu.roll(value, shift % size, dim) if shift % size else value

    def pack2(values, top):
        result = None
        for c, v in enumerate(values):
            v = roll(v, 2 * c + 2 if top else 2 * c, 0)
            result = v if c == 0 else jnp.where(row8 >= 2 * c, v, result)
        return result

    def unpack2(low, high, c):
        return jnp.where(row8 < 4, roll(high, -2 * c, 0), roll(low, 6 - 2 * c, 0))

    def pack4(pair, top):
        re, im = pair
        return jnp.where(row8 < 4, roll(re, 4, 0), im) if top else jnp.where(row8 < 4, re, roll(im, 4, 0))

    def unpack4(low, high):
        return jnp.where(row8 < 4, high, roll(low, 4, 0)), jnp.where(row8 < 4, roll(high, 4, 0), low)

    def put_corners(cs, j, near_low, near_high, from_edge):
        for i, (dx, dy) in enumerate(CORNERS):
            pair = near_high if dx > 0 else near_low
            at = 7 - from_edge if dy > 0 else from_edge
            for c, v in enumerate(pair):
                cs[i, j + c] = v[at : at + 1]

    def got_corner(cr, side, j):
        i = CORNERS.index((-side, 1))
        return cr[i, j], cr[i + 1, j]

    def corner_tile(cr, side, j, thick=1):
        below, above = got_corner(cr, side, j)
        return jnp.where(row8 >= 8 - thick, below, jnp.where(row8 < thick, above, 0.0))

    def pack_dense(first, second):
        return jnp.where(
            even_lane, jnp.where(even_row, first[0], first[1]), jnp.where(even_row, second[0], second[1])
        )

    def unpack_dense(tile):
        re = jnp.where(even_row, tile, roll(tile, 1, 0))
        im = jnp.where(even_row, roll(tile, -1, 0), tile)
        first = tuple(jnp.where(even_lane, v, roll(v, 1, 1)) for v in (re, im))
        second = tuple(jnp.where(even_lane, roll(v, -1, 1), v) for v in (re, im))
        return first, second

    def send_dense(b, planes):
        b["own"][...] = pack_dense(*planes)
        if "cs" in b:
            put_corners(b["cs"], 0, planes[0], planes[1], 0)

    def get_dense(b, own):
        before, after, below, above = [unpack_dense(b["got"][i]) for i in range(4)]
        none = jnp.zeros((8, depth), f32)
        result = []
        for p, plane in enumerate([*before, *own, *after]):
            pair = []
            for c in range(2):
                if p in (2, 3):
                    halo = jnp.where(row8 < 4, above[p - 2][c], below[p - 2][c])
                elif p in (1, 4) and "cr" in b:
                    halo = corner_tile(b["cr"], -1 if p == 1 else 1, c, 2)
                else:
                    halo = none
                pair.append(jnp.concatenate([plane[c], halo], axis=0))
            result.append(tuple(pair))
        return result

    def around(before, mid, after, s, rows):
        beside = roll(mid, s, 0) + roll(mid, -s, 0)
        total, mid = before + after + beside[:rows], mid[:rows]
        lane = iota(mid.shape, 1)
        total = total + jnp.where(lane >= s, roll(mid, s, 1), 0.0)
        return total + jnp.where(lane < depth - s, roll(mid, -s, 1), 0.0)

    def load(ref, plane, rows=None):
        return tuple(ref[plane, c] if rows is None else ref[plane, c, :rows] for c in range(2))

    def store(ref, plane, pair):
        for c, v in enumerate(pair):
            ref[plane, c, : v.shape[0]] = v

    def neighbours(ref, plane, s, rows=None):
        rows = rows or ref.shape[2]
        return tuple(
            around(ref[plane - 1, c, :rows], ref[plane, c], ref[plane + 1, c, :rows], s, rows) for c in range(2)
        )

    def weight(diag):
        scale = OMEGA / (diag[0] * diag[0] + diag[1] * diag[1])
        return diag[0] * scale, -diag[1] * scale

    def first_two(wf_ref, w_ref, target, planes, s, c):
        for p in planes:
            rows = 8 if p in (planes[0], planes[-1]) else 16
            part = product(load(w_ref, p, rows), neighbours(wf_ref, p, s, rows))
            store(target, p, tuple(1.4 * a + c * b for a, b in zip(load(wf_ref, p, rows), part)))

    def sweep(ref, wf_ref, w_ref, planes, s, c, behind=0, rows_of=lambda p: None):
        for p in planes:
            rows = rows_of(p) or ref.shape[2]
            part = product(load(w_ref, p - behind, rows), neighbours(ref, p, s, rows))
            wf = load(wf_ref, p - behind, rows)
            yield p, tuple(0.4 * a + b + c * d for a, b, d in zip(load(ref, p, rows), wf, part))

    def wide_planes(tile_of, reach):
        result = []
        for rx in range(-reach, reach + 1):
            blocks = [tile_of(rx, ry) for ry in (0, 1, -1)]
            for half in range(2):
                result.append(tuple(jnp.concatenate([v[half][c] for v in blocks], axis=0) for c in range(2)))
        return result

    def residual(source, diag, ref, p, s, c):
        ns, part = neighbours(ref, p, s, 8), product(diag, load(ref, p, 8))
        return tuple(f + c * n - q for f, n, q in zip(source, ns, part))

    def pair_mean(value):
        value = value + jnp.where(even_row, roll(value, -1, 0), roll(value, 1, 0))
        other = jnp.where(even_lane, roll(value, -1, 1), roll(value, 1, 1))
        return (value + other) * 0.125

    def own8(pair):
        return tuple(v[:8] for v in pair)

    for load_copy in loads:
        load_copy.wait()
    shifts, weights, scaled = [], [], []
    for p in range(4):
        index = m["layer"][p]
        velocity = jnp.zeros((8, depth), f32)
        for number in range(m["table"].shape[0]):
            velocity = jnp.where(index == number, m["table"][number], velocity)
        ratio = KH_FACTOR / velocity
        kh2 = ratio * ratio
        shift = (kh2, -kh2 * (BETA + ABSORB * m["absorb"][p].astype(f32)))
        diag = (6.0 - shift[0], -shift[1])
        source = (m["rhs"][0, p], m["rhs"][1, p])
        w = weight(diag)
        wf = product(w, source)
        store(m["diag0"], p, diag)
        store(m["source0"], p, source)
        store(m["ewf"], p + 2, wf)
        store(m["ew"], p + 2, w)
        m["up"][p] = pack2([*wf, *w], True)
        m["down"][p] = pack2([*wf, *w], False)
        shifts.append(shift)
        weights.append(w)
        scaled.append(wf)
    put_corners(m["cs"], 0, scaled[0], scaled[3], 0)
    put_corners(m["cs"], 2, weights[0], weights[3], 0)
    pl.semaphore_wait(barrier, count - 1)
    start("begin")
    shifts1 = [tuple(pair_mean(shifts[p][c] + shifts[p + 1][c]) for c in range(2)) for p in (0, 2)]
    diags1 = [(1.5 - s[0], -s[1]) for s in shifts1]
    weights1 = [weight(d) for d in diags1]
    send_dense(m["coef1"], weights1)
    start("coef1", "later", "later1")
    for p in range(2):
        store(m["diag1"], p, diags1[p])

    spread = 0.25 * (iota((depth, 128), 0) // 4 == iota((depth, 128), 1)).astype(f32)
    spread = spread.astype(jnp.bfloat16)
    widen = (iota((128, depth), 1) // 4 == iota((128, depth), 0)).astype(f32).astype(jnp.bfloat16)
    rows2 = 2 * ngy
    shift2_sum = tuple(shifts1[0][c] + shifts1[1][c] for c in range(2))
    m["padded"][...] = jnp.zeros(m["padded"].shape, f32)
    row2 = iota((ngx, rows2, 128), 1)
    block8 = iota((8, 128), 0) // 2

    def unpack(buffer, comp):
        planes = []
        for x in range(ngx):
            groups = []
            for q in range(0, ngy, 4):
                value = buffer[x * ngy + q]
                for j in range(1, min(4, ngy - q)):
                    value = jnp.where(block8 == (comp + j) % 4, buffer[x * ngy + q + j], value)
                groups.append(roll(value, -2 * comp, 0))
            planes.append(jnp.concatenate(groups, axis=0)[:rows2] if len(groups) > 1 else groups[0][:rows2])
        return jnp.stack(planes)

    coarse = {}

    def coarsest(cycle, sums):
        buffer = m["cycles"][cycle]["tiles"]
        tile = jnp.zeros((8, depth), f32)
        for c, v in enumerate(list(sums) + (list(shift2_sum) if cycle == 0 else [])):
            v = v + jnp.where(row8 // 2 % 2 == 0, roll(v, -2, 0), roll(v, 2, 0))
            tile = jnp.where(row8 // 2 == c, roll(v, 2 * c - 3, 0), tile)
        tile = dot3(tile * 0.25, spread)
        buffer[me] = pltpu.roll(tile, 2 * lax.rem(gy, 4), 0)

        others(
            lambda x, y: pltpu.make_async_remote_copy(
                src_ref=buffer.at[me], dst_ref=buffer.at[me],
                send_sem=m["tile_send"].at[cycle], recv_sem=m["tile_recv"].at[cycle],
                device_id=(x, y), device_id_type=MESH,
            ).start()
        )

    def coarsest_finish(cycle):
        buffer = m["cycles"][cycle]["tiles"]
        every = buffer.at[pl.ds(0, count - 1)]
        pltpu.make_async_copy(every, every, m["tile_recv"].at[cycle]).wait()
        source = unpack(buffer, 0), unpack(buffer, 1)
        if cycle == 0:
            shift = unpack(buffer, 2), unpack(buffer, 3)
            full = weight((0.375 - shift[0], -shift[1]))
            coarse["w"] = tuple(jnp.where(shift[0] > 0.0, v, 0.0) for v in full)
        w = coarse["w"]
        wf = product(w, source)
        none = jnp.zeros((1, rows2, 128), f32)

        def total(e):
            result = jnp.concatenate([none, e[:-1]], axis=0) + jnp.concatenate([e[1:], none], axis=0)
            result = result + jnp.where(row2 > 0, roll(e, 1, 1), 0.0)
            result = result + jnp.where(row2 < rows2 - 1, roll(e, -1, 1), 0.0)
            return result + roll(e, 1, 2) + roll(e, -1, 2)

        def step(_, e):
            part = product(w, (total(e[0]), total(e[1])))
            return tuple(0.4 * a + b + 0.0625 * d for a, b, d in zip(e, wf, part))

        e = wf
        for k in range(NC - 1):
            e = step(k, e)
        for c in range(2):
            for x in range(ngx):
                m["padded"][x + 2, c, 8 : 8 + rows2] = e[c][x]
        own = [m["padded"][gx + i, c, pl.ds(6 + 2 * gy, 8)] for i in range(5) for c in range(2)]
        wide = dot3(jnp.concatenate(own, axis=0), widen)
        result = []
        for i in range(5):
            pair = []
            for c in range(2):
                rows = [wide[16 * i + 8 * c + k : 16 * i + 8 * c + k + 1] for k in (2, 3, 4, 5, 0, 1)]
                tiles = [jnp.where(row8 < 4, rows[k], rows[k + 1]) for k in (0, 2, 4)]
                pair.append(jnp.concatenate(tiles, axis=0))
            result.append(tuple(pair))
        return result

    def cycle_part(cycle):
        b = m["cycles"][cycle]
        wf0, w0, upd0, upd0b = m["wf0"], m["w0"], m["upd0"], m["upd0b"]
        wf1, w1, upd1 = m["wf1"], m["w1"], m["upd1"]
        first_two(wf0, w0, upd0, range(1, 7), 1, 1.0)
        held = [residual(load(m["source0"], p), load(m["diag0"], p), upd0, p + 2, 1, 1.0) for p in range(4)]
        sources = [tuple(pair_mean(held[p][c] + held[p + 1][c]) for c in range(2)) for p in (0, 2)]
        scaled1 = [product(weights1[p], sources[p]) for p in range(2)]
        send_dense(b["source"], scaled1)
        start(f"source{cycle}")
        updates = [load(upd0, p + 2, 8) for p in range(4)]
        store(b["farown"], 0, updates[2])
        store(b["farown"], 1, updates[1])
        for i in range(2):
            b["up"][i] = pack2([*updates[2 * i], *updates[2 * i + 1]], True)
            b["down"][i] = pack2([*updates[2 * i], *updates[2 * i + 1]], False)
        put_corners(b["cs"], 0, updates[0], updates[3], 0)
        start(f"update{cycle}")
        if cycle == 0:
            receive("coef1")
            for p, pair in enumerate(get_dense(m["coef1"], weights1)):
                store(w1, p, pair)
        receive(f"source{cycle}")
        for p, pair in enumerate(get_dense(b["source"], scaled1)):
            store(wf1, p, pair)
        first_two(wf1, w1, upd1, range(1, 5), 2, 0.25)
        left, right = [residual(sources[p], load(m["diag1"], p), upd1, p + 2, 2, 0.25) for p in range(2)]
        coarsest(cycle, tuple(left[c] + right[c] for c in range(2)))
        updates1 = [load(upd1, p + 2, 8) for p in range(2)]
        b["fine"]["own"][...] = pack_dense(*updates1)
        start(f"fine{cycle}")

        def beside(own, faces, corners):
            def tile_of(rx, ry):
                step = (-rx, -ry)
                if step == (0, 0):
                    return own
                return unpack_dense(faces[FACES.index(step)] if step in FACES else corners[CORNERS.index(step)])

            return tile_of

        if cycle == 0:
            receive("later1")
            tile_of = beside(weights1, m["coef1"]["got"], m["ccoef1"])
            for p, pair in enumerate(wide_planes(tile_of, 1)):
                store(m["wide_w1"], p, pair)
        receive(f"update{cycle}")
        none = jnp.zeros((8, depth), f32)
        for c in range(2):
            upd0[0, c] = jnp.concatenate([b["far"][0, c], none], axis=0)
            upd0[7, c] = jnp.concatenate([b["far"][1, c], none], axis=0)
            upd0[1, c, 8:] = corner_tile(b["cr"], -1, c)
            upd0[6, c, 8:] = corner_tile(b["cr"], 1, c)
            for p in range(4):
                upd0[p + 2, c, 8:] = unpack2(b["low"][p // 2], b["high"][p // 2], 2 * (p % 2) + c)
        for p, pair in enumerate(wide_planes(beside(scaled1, b["source"]["got"], b["csource"]), 1)):
            store(m["wide_wf1"], p, pair)
        wait_sends(lambda name: cycle == 1 and not name.startswith("fine1"))
        correction = coarsest_finish(cycle)
        receive(f"fine{cycle}")
        around1 = wide_planes(
            lambda rx, ry: unpack_dense(b["fine"]["got"][AROUND.index((-rx, -ry))]) if rx or ry else updates1, 2
        )
        wide1, wide1b = m["wide1"], m["wide1b"]
        for p in range(8):
            store(wide1, p, tuple(v + x for v, x in zip(around1[p + 1], correction[(p + 1) // 2])))
        for p, e in sweep(wide1, m["wide_wf1"], m["wide_w1"], range(1, 7), 2, 0.25, 1):
            store(wide1b, p, e)
        for p, e in sweep(wide1b, m["wide_wf1"], m["wide_w1"], range(2, 6), 2, 0.25, 1):
            solved = [jnp.concatenate([v[:8], jnp.where(row8 < 4, v[8:16], v[16:24])], axis=0) for v in e]
            for fine in (2 * p - 4, 2 * p - 3):
                store(upd0, fine, tuple(v + x for v, x in zip(load(upd0, fine), solved)))
        for p, e in sweep(upd0, wf0, w0, range(1, 7), 1, 1.0, rows_of=lambda p: 8 if p in (1, 6) else 16):
            store(upd0b, p, e)
        for p, e in sweep(upd0b, wf0, w0, range(2, 6), 1, 1.0, rows_of=lambda p: 8):
            yield p - 2, own8(e)

    none = jnp.zeros((8, depth), f32)

    def halo0(p, j):
        if p in (1, 6):
            return corner_tile(m["cr"], -1 if p == 1 else 1, j)
        if p in (0, 7):
            return none
        return unpack2(m["low"][p - 2], m["high"][p - 2], j)

    receive("begin")
    for p in range(8):
        for c in range(2):
            m["wf0"][p, c] = jnp.concatenate([m["ewf"][p, c], halo0(p, c)], axis=0)
            if p in (0, 7):
                m["w0"][p, c, 8:] = none
            else:
                m["w0"][p, c] = jnp.concatenate([m["ew"][p, c], halo0(p, 2 + c)], axis=0)
    kept = []
    for p, e in cycle_part(0):
        store(m["first"], p + 3, e)
        m["fup"][p] = pack4(e, True)
        m["fdown"][p] = pack4(e, False)
        kept.append(e)
    put_corners(m["fcs"], 0, kept[0], kept[3], 0)
    put_corners(m["fcs"], 2, kept[0], kept[3], 1)
    put_corners(m["fcs"], 4, kept[1], kept[2], 0)
    start("first")
    receive("first", "later")
    for p in (0, 7):
        for c in range(2):
            m["w0"][p, c, :8] = m["ew"][p, c]
    for p in range(10):
        if 3 <= p < 7:
            halo = unpack4(m["flow"][p - 3], m["fhigh"][p - 3])
        elif p in (2, 7):
            side, halo = (-1 if p == 2 else 1), []
            for c in range(2):
                below, above = got_corner(m["fcr"], side, c)
                below2, above2 = got_corner(m["fcr"], side, 2 + c)
                tile = jnp.where(row8 == 7, below, jnp.where(row8 == 6, below2, 0.0))
                halo.append(jnp.where(row8 == 0, above, jnp.where(row8 == 1, above2, tile)))
        elif p in (1, 8):
            halo = [corner_tile(m["fcr"], -1 if p == 1 else 1, 4 + c) for c in range(2)]
        else:
            halo = [none, none]
        for c in range(2):
            m["first16"][p, c] = jnp.concatenate([m["first"][p, c], halo[c]], axis=0)
    for p in range(8):
        rows = 8 if p in (0, 7) else 16
        ns = neighbours(m["first16"], p + 1, 1, rows)
        e = load(m["first16"], p + 1, rows)
        if 2 <= p < 6:
            part = product(load(m["diag0"], p - 2), own8(e))
            source = load(m["source0"], p - 2)
            store(m["source0"], p - 2, tuple(f + n[:8] - q for f, n, q in zip(source, ns, part)))
        part = product(load(m["w0"], p, rows), ns)
        store(m["wf0"], p, tuple(a + b - OMEGA * v for a, b, v in zip(load(m["wf0"], p, rows), part, e)))
    for p, e in cycle_part(1):
        for c in range(2):
            out[c, p] = m["first"][p + 3, c] + e[c]

    wait_sends(lambda name: name.startswith("fine1"))
    for cycle in range(2):
        every = m["cycles"][cycle]["tiles"].at[pl.ds(0, count - 1)]
        pltpu.make_async_copy(every, every, m["tile_send"].at[cycle]).wait()


def local(ngx, ngy, right_side, velocity_table, layer_index, absorb_level):
    depth = right_side.shape[-1]
    scratch = scratch_of(ngx, ngy, velocity_table.shape[0], depth)
    leaves, tree = jax.tree.flatten(scratch)
    anywhere = pl.BlockSpec(memory_space=pltpu.HBM)
    return pl.pallas_call(
        functools.partial(kernel, ngx, ngy, depth, tree),
        out_shape=jax.ShapeDtypeStruct(right_side.shape, jnp.float32),
        in_specs=[anywhere] * 4,
        out_specs=pl.BlockSpec(memory_space=pltpu.VMEM),
        scratch_shapes=leaves,
        compiler_params=pltpu.CompilerParams(
            collective_id=0, has_side_effects=True, vmem_limit_bytes=64 * 1024 * 1024 - 65536
        ),
    )(right_side, velocity_table, layer_index, absorb_level)


def solution(mesh):
    placed = (P(None, "gx", "gy", None), P(), P("gx", "gy", None), P("gx", "gy", None))
    return jax.shard_map(
        functools.partial(local, mesh.shape["gx"], mesh.shape["gy"]),
        mesh=mesh, in_specs=placed, out_specs=P(None, "gx", "gy", None), check_vma=False,
    )
```
